32 devices in a mesh: groups: 2 (over y), expert: 4 (over x, core), tensor: 4 (over z).
Axes of the slice: x: 2, y: 2, z: 4, core: 2. Of those that a mesh axis runs over, the one named last changes fastest.
Arguments:
- context: bfloat16 [4096, 4096], P(('groups', 'expert'), 'tensor'), parts along dimension 0, may hold values from -6 to 6
- o_weight: bfloat16 [4096, 2048], P('tensor'), may hold values from -0.09375 to 0.09375
- resid: bfloat16 [4096, 2048], P(('groups', 'expert', 'tensor')), parts along dimension 0, may hold values from -6 to 6
- norm_gain: float32 [2048], replicated, may hold values from 0.5 to 1.5
- router: bfloat16 [2048, 16], replicated, may hold values from -0.125 to 0.125
- gate_weight: bfloat16 [16, 2048, 768], P(('expert', 'tensor')), may hold values from -0.125 to 0.125
- up_weight: bfloat16 [16, 2048, 768], P(('expert', 'tensor')), may hold values from -0.125 to 0.125
- down_weight: bfloat16 [16, 768, 2048], P(('expert', 'tensor')), may hold values from -0.21875 to 0.21875
- expert_ids: int32 [4096, 4], P(('groups', 'expert', 'tensor')), parts along dimension 0, may hold values from 0 to 15, all different within a row; in each aligned block of 128 rows (0 to 127, 128 to 255, ...) at most 40 rows name the same one
- lengths: int32 [8, 8], P(('groups', 'expert')), parts along dimension 0, may hold values from 1 to 192, 512 in all within a row
Outputs:
- loss_value: float32 [2], P('groups'), parts along dimension 0
- grad_resid: bfloat16 [4096, 2048], P(('groups', 'expert', 'tensor')), parts along dimension 0
The draws below stay inside these ranges and needn't reach their ends.
There are 2 independent parts, one for each index of `groups`. The reference program is written for one: setup_inputs(seed, part) draws one part's arguments, and reference() takes and returns one part's arrays. A program takes and returns all parts, laid end to end along the dimension named above; an argument that names none is the same for every part. Nothing has to cross between parts.
Inputs may be any that keep to these rules, and one draw needn't show every extreme that they name: `expert_ids`: each row names 4 different experts. Within the 128 rows of one device no expert is named more than 40 times, a bound that some block reaches. `lengths`: each row sums to 512 and its largest entry is 192.
All inputs are finite; a program needn't handle non-finite values.
Results may differ from the reference program's by a relative error of at most 0.015.
Values may be sent and summed in bfloat16 or wider, within the bound.
No kernel may reach another device: no remote copies, remote signals or barrier semaphores. Data moves between devices by JAX's collectives and lax.ppermute only.
A program may use at most 128 MiB of HBM per device.

```python
import math
import jax
import jax.numpy as jnp
import numpy as np
from jax import lax

D = 2048
HD = 4096
EXPERTS = 16
FFE = 768
TOPK = 4
TOK_SP = 128
TOK_E = 512
TOKENS = 2048
SEQ_E = 8
SEQS = 32
CAP = 40
LEN_MOST = 192
N_EXPERT = 4
N_TENSOR = 4


def levels(stream_key, dims, cuts, low, largest):
    level, own = 1.0, jax.random.fold_in(stream_key, 6)
    for axis_at, parts in cuts:
        heights = jnp.exp(jax.random.uniform(jax.random.fold_in(own, axis_at), (parts,), jnp.float32, low / len(cuts), largest / len(cuts)))
        level = level * jnp.repeat(heights, dims[axis_at] // parts).reshape([-1 if axis == axis_at else 1 for axis in range(len(dims))])
    return level


def split_up(amount, total, limit, slope):
    weights = [(1 << 20) // math.isqrt(rank ** slope) + 1 for rank in range(2, amount + 1)]
    spare, counts = total - limit - (amount - 1), [1] * (amount - 1)
    while spare > 0:
        movable = [i for i in range(amount - 1) if counts[i] < limit]
        pool, left = sum([weights[i] for i in movable]), spare
        for i in movable:
            more = min(limit - counts[i], max(1, left * weights[i] // pool), spare)
            counts[i] = counts[i] + more
            spare = spare - more
    return np.array([limit] + counts)


def uneven_parts(rng, count, total, limit, slope):
    if count == 2:
        one = jax.random.randint(rng, (), max(1, total - limit), min(limit, total - 1) + 1)
        return jnp.stack([one, total - one])
    sizes = jnp.asarray(split_up(count, total, limit, slope), jnp.int32)
    twos = (count - 1) // 2
    source_of, receiver = sizes[1:1 + 2 * twos:2], sizes[2:2 + 2 * twos:2]
    slack = jnp.minimum(source_of - 1, limit - receiver)
    passed = jax.random.randint(jax.random.fold_in(rng, 1), (twos,), 0, 1 << 20) % (slack + 1)
    sizes = sizes.at[1:1 + 2 * twos:2].set(source_of - passed).at[2:2 + 2 * twos:2].set(receiver + passed)
    return sizes[jax.random.permutation(jax.random.fold_in(rng, 2), count)]


def assign_block(stream_key, own, number, rows, number_of, top, reach, skew):
    sequence = jax.random.permutation(stream_key, number_of)
    packed, usual = shares(number_of, rows * top, reach, skew, True), shares(number_of, rows * top, reach, skew, False)
    places = jnp.arange(number_of)

    def named(sizes, rotation):
        used = int((sizes > 0).sum())
        fixed = max(1, used // 4)
        shifted = fixed + (places - fixed + rotation * (used - fixed)) % max(1, number_of - fixed)
        return jnp.zeros((number_of,), jnp.int32).at[sequence[jnp.where(places < fixed, places, shifted)]].set(jnp.asarray(sizes, jnp.int32))

    sizes = jnp.where(number % 4 == 0, named(packed, number // 4), named(usual, number - number // 4 - 1))
    mixed = jax.random.permutation(jax.random.fold_in(own, 3), number_of)
    donor, sink = mixed[0:number_of // 2 * 2:2], mixed[1:number_of // 2 * 2:2]
    margin = jnp.minimum(sizes[donor] - 1, reach - sizes[sink]) // 2
    margin = jnp.where((donor == sequence[0]) | (sink == sequence[0]) | (sizes[sink] == 0), 0, jnp.maximum(margin, 0))
    shifted = jax.random.randint(jax.random.fold_in(own, 4), (number_of // 2,), 0, 1 << 20) % (margin + 1)
    sizes = sizes.at[donor].add(-shifted).at[sink].add(shifted)
    items = jnp.searchsorted(jnp.cumsum(sizes), jnp.arange(rows * top), side="right").astype(jnp.int32)
    listing = items.reshape(top, rows).T
    listing = listing[jax.random.permutation(jax.random.fold_in(own, 1), rows)]
    rotation = jax.random.randint(jax.random.fold_in(own, 2), (rows, 1), 0, top)
    return jnp.take_along_axis(listing, (jnp.arange(top)[None, :] + rotation) % top, axis=1)


def shares(amount, total, reach, skew, full):
    loads = [(1 << 20) // math.isqrt(standing ** skew) + 1 for standing in range(1, amount + 1)]
    largest = reach if full else min(reach, max(-(-total // amount), total * loads[0] // sum(loads)))
    least = 1 if total - largest >= amount - 1 else 0
    holding, spare = [largest] + [least] * (amount - 1), total - largest - least * (amount - 1)
    while spare > 0:
        free = [i for i in range(1, amount) if holding[i] < largest] or [i for i in range(1, amount) if holding[i] < reach]
        mass, budget = sum([loads[i] for i in free]), spare
        for i in free:
            addition = min(reach - holding[i], max(1, budget * loads[i] // mass), spare)
            holding[i] = holding[i] + addition
            spare = spare - addition
    return np.array(holding)


def gaussian(rng, dims, deviation, most, cuts=(), kind=jnp.bfloat16):
    loudness = levels(rng, dims, cuts, -0.22, 0.18) if cuts else 1.0
    result = jax.random.normal(rng, dims, jnp.float32) * deviation * loudness
    return jnp.minimum(jnp.maximum(result, -most), most).astype(kind)


def setup_inputs(seed: int = 0, part: int = 0) -> dict:
    key_list = jax.random.split(jax.random.key(seed), 11)
    own_keys = jax.random.split(jax.random.fold_in(key_list[10], part), 11)
    context = gaussian(own_keys[0], (TOKENS, HD), 1.0, 6.0, ((0, 4), (1, 4)))
    o_weight = gaussian(key_list[1], (HD, D), HD ** -0.5, 0.09375, ((0, 4),))
    resid = gaussian(own_keys[2], (TOKENS, D), 1.0, 6.0, ((0, 16),))
    norm_gain = jnp.clip(1.0 + 0.1 * jax.random.normal(key_list[3], (D,), jnp.float32), 0.5, 1.5)
    router = gaussian(key_list[4], (D, EXPERTS), D ** -0.5, 0.125)
    gate_weight = gaussian(key_list[5], (EXPERTS, D, FFE), D ** -0.5, 0.125, ((0, 16),))
    up_weight = gaussian(key_list[6], (EXPERTS, D, FFE), D ** -0.5, 0.125, ((0, 16),))
    down_weight = gaussian(key_list[7], (EXPERTS, FFE, D), FFE ** -0.5, 0.21875, ((0, 16),))
    expert_ids_keys = jax.random.split(jax.random.fold_in(own_keys[8], 1), TOKENS // TOK_SP)
    expert_ids_turns = jax.random.permutation(jax.random.fold_in(own_keys[8], 3), TOKENS // TOK_SP)
    expert_ids = jax.vmap(lambda own, number: assign_block(jax.random.fold_in(own_keys[8], 2), own, number, TOK_SP, EXPERTS, TOPK, CAP, 2))(expert_ids_keys, expert_ids_turns).reshape((TOKENS, TOPK))
    lengths = jax.vmap(lambda own: uneven_parts(own, SEQ_E, TOK_E, LEN_MOST, 1))(jax.random.split(own_keys[9], N_EXPERT)).reshape((N_EXPERT, SEQ_E)).astype(jnp.int32)
    return {"context": context, "o_weight": o_weight, "resid": resid, "norm_gain": norm_gain, "router": router, "gate_weight": gate_weight, "up_weight": up_weight, "down_weight": down_weight, "expert_ids": expert_ids, "lengths": lengths}


EPSILON = 1e-06
SOFTMAX_WARMTH = 0.05
LOSS_SCALE = 32768.0
EXACT_PRECISION = lax.Precision.HIGHEST

def slot_positions(flat_ids, expert_total):
    onehot = (flat_ids[..., None] == jnp.arange(expert_total, dtype=jnp.int32)).astype(jnp.int32)
    before = jnp.cumsum(onehot, axis=-2) - onehot
    return lax.optimization_barrier(jnp.sum(before * onehot, axis=-1)).astype(jnp.int32)

def contract_last(left, right):
    return lax.dot_general(left, right, (((1,), (1,)), ((), ())), preferred_element_type=jnp.float32)

def contrast(embedded):
    pair_count = embedded.shape[0] // 2
    norms = jnp.sqrt(lax.optimization_barrier(jnp.sum(embedded * embedded, axis=1, keepdims=True)) + EPSILON)
    unit_rows = embedded / norms
    query_rows = unit_rows[0::2]
    passage_rows = unit_rows[1::2]
    similarity_scores = jnp.dot(query_rows, passage_rows.T, precision=EXACT_PRECISION) / SOFTMAX_WARMTH
    exp_scores = jnp.exp(similarity_scores)
    row_total = lax.optimization_barrier(jnp.sum(exp_scores, axis=1, keepdims=True))
    loss_value = jnp.mean(jnp.log(row_total[:, 0]) - jnp.diagonal(similarity_scores))
    score_gradient = (exp_scores / row_total - jnp.eye(pair_count, dtype=similarity_scores.dtype)) * (LOSS_SCALE / pair_count)
    query_gradient = jnp.dot(score_gradient, passage_rows, precision=EXACT_PRECISION) / SOFTMAX_WARMTH
    passage_gradient = jnp.dot(score_gradient.T, query_rows, precision=EXACT_PRECISION) / SOFTMAX_WARMTH
    dunit_rows = jnp.stack([query_gradient, passage_gradient], axis=1).reshape(embedded.shape)
    radial = lax.optimization_barrier(jnp.sum(unit_rows * dunit_rows, axis=1, keepdims=True))
    return (loss_value, (dunit_rows - unit_rows * radial) / norms)

def reference(context, o_weight, resid, norm_gain, router, gate_weight, up_weight, down_weight, expert_ids, lengths):
    device_count = N_EXPERT * N_TENSOR
    group_width = HD // N_TENSOR
    context_groups = context.reshape(TOKENS, N_TENSOR, group_width).transpose(1, 0, 2)
    weight_groups = o_weight.reshape(N_TENSOR, group_width, D)

    def head_term(carry, operands):
        ctx_block, w_block = operands
        term = jnp.dot(ctx_block, w_block, preferred_element_type=jnp.float32).astype(jnp.bfloat16)
        term = lax.optimization_barrier(term)
        return (carry + term.astype(jnp.float32), None)
    attention_out, _ = lax.scan(head_term, jnp.zeros((TOKENS, D), jnp.float32), (context_groups, weight_groups))
    resid_mid = resid.astype(jnp.float32) + attention_out
    rms_scale = lax.rsqrt(lax.optimization_barrier(jnp.mean(resid_mid * resid_mid, axis=1, keepdims=True)) + EPSILON)
    normed = (resid_mid * rms_scale * norm_gain).astype(jnp.bfloat16)
    logits = jnp.dot(normed, router, preferred_element_type=jnp.float32)
    chosen = jnp.take_along_axis(logits, expert_ids, axis=1)
    exp_chosen = jnp.exp(chosen)
    gate_probs = exp_chosen / lax.optimization_barrier(jnp.sum(exp_chosen, axis=1, keepdims=True))
    blocks = expert_ids.reshape(device_count, TOK_SP * TOPK)
    position = slot_positions(blocks, EXPERTS).reshape(TOKENS, TOPK)
    source = jnp.broadcast_to((jnp.arange(TOKENS, dtype=jnp.int32) // TOK_SP)[:, None], (TOKENS, TOPK))
    row_index = (source * CAP + position).astype(jnp.int32)
    dispatch_buffer = jnp.zeros((EXPERTS, device_count * CAP, D), jnp.bfloat16)
    dispatch_buffer = dispatch_buffer.at[expert_ids, row_index].set(jnp.broadcast_to(normed[:, None, :], (TOKENS, TOPK, D)))

    def expert_forward(operands):
        row_block, w_gate, w_up, w_down = operands
        pre_gate = jnp.dot(row_block, w_gate, preferred_element_type=jnp.float32)
        pre_up = jnp.dot(row_block, w_up, preferred_element_type=jnp.float32)
        hidden = (jax.nn.silu(pre_gate) * pre_up).astype(jnp.bfloat16)
        out_rows = jnp.dot(hidden, w_down, preferred_element_type=jnp.float32).astype(jnp.bfloat16)
        return (out_rows, jnp.stack([pre_gate, pre_up]))
    out_rows, pre_acts = lax.map(expert_forward, (dispatch_buffer, gate_weight, up_weight, down_weight))
    expert_out = out_rows[expert_ids, row_index].astype(jnp.float32)
    resid_out = resid_mid + lax.optimization_barrier(jnp.sum(gate_probs[:, :, None] * expert_out, axis=1))
    seq_ends = jnp.cumsum(lengths, axis=1)
    local_pos = jnp.arange(TOK_E, dtype=jnp.int32)
    segment = lax.optimization_barrier(jnp.sum((local_pos[None, :, None] >= seq_ends[:, None, :]).astype(jnp.int32), axis=2))
    seq_id = (segment + SEQ_E * jnp.arange(N_EXPERT, dtype=jnp.int32)[:, None]).reshape(TOKENS).astype(jnp.int32)
    seq_len = lengths.reshape(SEQS).astype(jnp.float32)
    tok_len = seq_len[seq_id]
    embedded = jax.ops.segment_sum(resid_out / tok_len[:, None], seq_id, num_segments=SEQS)
    loss_value, dembedded = contrast(embedded)
    dresid_out = (dembedded / seq_len[:, None])[seq_id]
    dout_rows = (gate_probs[:, :, None] * dresid_out[:, None, :]).astype(jnp.bfloat16)
    grad_buffer = jnp.zeros((EXPERTS, device_count * CAP, D), jnp.bfloat16).at[expert_ids, row_index].set(dout_rows)

    def expert_backward(operands):
        row_block, w_gate, w_up, w_down, pre_block = operands
        pre_gate = pre_block[0]
        pre_up = pre_block[1]
        dhidden = contract_last(row_block, w_down)
        gate_sigmoid = jax.nn.sigmoid(pre_gate)
        dpre_gate = (dhidden * pre_up * gate_sigmoid * (1.0 + pre_gate * (1.0 - gate_sigmoid))).astype(jnp.bfloat16)
        dpre_up = (dhidden * jax.nn.silu(pre_gate)).astype(jnp.bfloat16)
        summed = contract_last(dpre_gate, w_gate) + contract_last(dpre_up, w_up)
        return summed.astype(jnp.bfloat16)
    dx_rows = lax.map(expert_backward, (grad_buffer, gate_weight, up_weight, down_weight, pre_acts))
    dx_moe = lax.optimization_barrier(jnp.sum(dx_rows[expert_ids, row_index].astype(jnp.float32), axis=1))
    dgate_prob = lax.optimization_barrier(jnp.sum(dresid_out[:, None, :] * expert_out, axis=2))
    dchosen = gate_probs * (dgate_prob - lax.optimization_barrier(jnp.sum(gate_probs * dgate_prob, axis=1, keepdims=True)))
    expert_onehot = (expert_ids[:, :, None] == jnp.arange(EXPERTS, dtype=jnp.int32)).astype(dchosen.dtype)
    dlogits = lax.optimization_barrier(jnp.sum(dchosen[:, :, None] * expert_onehot, axis=1)).astype(jnp.bfloat16)
    dnormed = dx_moe + contract_last(dlogits, router)
    gain_grad = dnormed * norm_gain
    grad_resid = dresid_out + rms_scale * gain_grad - resid_mid * rms_scale ** 3 * lax.optimization_barrier(jnp.mean(gain_grad * resid_mid, axis=1, keepdims=True))
    return (loss_value.reshape(1), grad_resid.astype(jnp.bfloat16))
```

```python
import functools

import jax
import jax.numpy as jnp
from jax import lax
from jax.experimental import pallas as pl
from jax.experimental.pallas import tpu as pltpu
from jax.sharding import PartitionSpec as P

EPSILON = 1e-06
SOFTMAX_WARMTH = 0.05
LOSS_SCALE = 32768.0
EXACT_PRECISION = lax.Precision.HIGHEST


def slot_positions(flat_ids, expert_total):
    onehot = (flat_ids[..., None] == jnp.arange(expert_total, dtype=jnp.int32)).astype(jnp.int32)
    before = jnp.cumsum(onehot, axis=-2) - onehot
    return jnp.sum(before * onehot, axis=-1)


def contract_last(left, right):
    return lax.dot_general(
        left, right, (((1,), (1,)), ((), ())), preferred_element_type=jnp.float32
    )


def contrast(embedded):
    pair_count = embedded.shape[0] // 2
    norms = jnp.sqrt(jnp.sum(embedded * embedded, axis=1, keepdims=True) + EPSILON)
    unit_rows = embedded / norms
    query_rows = unit_rows[0::2]
    passage_rows = unit_rows[1::2]
    similarity_scores = (
        jnp.dot(query_rows, passage_rows.T, precision=EXACT_PRECISION) / SOFTMAX_WARMTH
    )
    exp_scores = jnp.exp(similarity_scores)
    row_total = jnp.sum(exp_scores, axis=1, keepdims=True)
    loss_value = jnp.mean(jnp.log(row_total[:, 0]) - jnp.diagonal(similarity_scores))
    score_gradient = (
        exp_scores / row_total - jnp.eye(pair_count, dtype=similarity_scores.dtype)
    ) * (LOSS_SCALE / pair_count)
    query_gradient = (
        jnp.dot(score_gradient, passage_rows, precision=EXACT_PRECISION) / SOFTMAX_WARMTH
    )
    passage_gradient = (
        jnp.dot(score_gradient.T, query_rows, precision=EXACT_PRECISION) / SOFTMAX_WARMTH
    )
    dunit_rows = jnp.stack([query_gradient, passage_gradient], axis=1).reshape(embedded.shape)
    radial = jnp.sum(unit_rows * dunit_rows, axis=1, keepdims=True)
    return (loss_value, (dunit_rows - unit_rows * radial) / norms)


def body(
    context,
    o_weight,
    resid,
    norm_gain,
    router,
    gate_weight,
    up_weight,
    down_weight,
    expert_ids,
    lengths,
):
    expert_count = lax.axis_size("expert")
    tensor_count = lax.axis_size("tensor")
    device_count = expert_count * tensor_count
    expert_index = lax.axis_index("expert")
    tensor_index = lax.axis_index("tensor")
    local_rows, model_width = resid.shape
    expert_total = router.shape[1]
    top_count = expert_ids.shape[1]
    seq_count = lengths.shape[1]
    seq_total = seq_count * expert_count
    capacity = max(2, local_rows * top_count * 5 // (4 * expert_total))
    attention_out = lax.psum_scatter(
        jnp.dot(context, o_weight, preferred_element_type=jnp.float32).astype(jnp.bfloat16),
        "tensor",
        scatter_dimension=0,
        tiled=True,
    ).astype(jnp.float32)
    resid_mid = resid.astype(jnp.float32) + attention_out
    rms_scale = lax.rsqrt(jnp.mean(resid_mid * resid_mid, axis=1, keepdims=True) + EPSILON)
    normed = (resid_mid * rms_scale * norm_gain).astype(jnp.bfloat16)
    logits = jnp.dot(normed, router, preferred_element_type=jnp.float32)
    expert_onehot = (expert_ids[:, :, None] == jnp.arange(expert_total, dtype=jnp.int32)).astype(
        jnp.float32
    )
    chosen = jnp.sum(logits[:, None, :] * expert_onehot, axis=2)
    exp_chosen = jnp.exp(chosen)
    gate_probs = exp_chosen / jnp.sum(exp_chosen, axis=1, keepdims=True)
    flat_ids = expert_ids.reshape(local_rows * top_count)
    target = flat_ids * capacity + slot_positions(flat_ids, expert_total)

    def move_rows(blocks):
        return lax.all_to_all(blocks, ("expert", "tensor"), split_axis=0, concat_axis=0, tiled=True)

    seq_lengths = lengths[0]
    seq_ends = jnp.cumsum(seq_lengths)
    seq_starts = seq_ends - seq_lengths
    positions = tensor_index * local_rows + jnp.arange(local_rows, dtype=jnp.int32)
    member = (
        (positions[None, :] >= seq_starts[:, None]) & (positions[None, :] < seq_ends[:, None])
    ).astype(jnp.float32)
    tok_len = jnp.sum(member * seq_lengths[:, None].astype(jnp.float32), axis=0)
    repeated = jnp.broadcast_to(normed[:, None, :], (local_rows, top_count, model_width)).reshape(
        local_rows * top_count, model_width
    )
    buffer = (
        jnp.zeros((expert_total * capacity, model_width), jnp.bfloat16).at[target].set(repeated)
    )
    received = move_rows(buffer.reshape(device_count, capacity, model_width)).reshape(
        device_count * capacity, model_width
    )
    pre_gate = jnp.dot(received, gate_weight[0], preferred_element_type=jnp.float32)
    pre_up = jnp.dot(received, up_weight[0], preferred_element_type=jnp.float32)
    hidden = (jax.nn.silu(pre_gate) * pre_up).astype(jnp.bfloat16)
    expert_rows = jnp.dot(hidden, down_weight[0], preferred_element_type=jnp.float32).astype(
        jnp.bfloat16
    )
    seq_local = jnp.dot(jnp.arange(seq_count, dtype=jnp.float32), member, precision=EXACT_PRECISION)
    seq_global = seq_local + (expert_index * seq_count).astype(jnp.float32)
    info_rows = jnp.stack(
        [
            gate_probs,
            jnp.broadcast_to(seq_global[:, None], (local_rows, top_count)),
            jnp.broadcast_to(tok_len[:, None], (local_rows, top_count)),
        ],
        axis=2,
    ).reshape(local_rows * top_count, 3)
    info_init = jnp.zeros((expert_total * capacity, 3), jnp.float32).at[:, 2].set(1.0)
    info_buffer = info_init.at[target].set(info_rows).reshape(device_count, capacity, 3)
    slot_data = lax.all_to_all(
        info_buffer, ("expert", "tensor"), split_axis=0, concat_axis=0, tiled=True
    ).reshape(device_count * capacity, 3)
    slot_gate = slot_data[:, 0:1]
    slot_seq = slot_data[:, 1].astype(jnp.int32)
    slot_len = slot_data[:, 2:3]
    slot_onehot = (slot_seq[:, None] == jnp.arange(seq_total, dtype=jnp.int32)).astype(jnp.float32)
    out_float = expert_rows.astype(jnp.float32)
    expert_part = lax.dot_general(
        slot_onehot,
        slot_gate * out_float / slot_len,
        (((0,), (0,)), ((), ())),
        precision=EXACT_PRECISION,
        preferred_element_type=jnp.float32,
    )
    partial_value = jnp.dot(member, resid_mid / tok_len[:, None], precision=EXACT_PRECISION)
    placed = lax.dynamic_update_slice_in_dim(
        expert_part,
        lax.dynamic_slice_in_dim(expert_part, expert_index * seq_count, seq_count, 0)
        + partial_value,
        expert_index * seq_count,
        0,
    )
    embedded = lax.psum(placed, ("expert", "tensor"))
    loss_value, dembedded = contrast(embedded)
    own_rows = lax.dynamic_slice_in_dim(
        dembedded, expert_index * seq_count, seq_count, 0
    ) / seq_lengths[:, None].astype(jnp.float32)
    dresid_out = lax.dot_general(
        member,
        own_rows,
        (((0,), (0,)), ((), ())),
        precision=EXACT_PRECISION,
        preferred_element_type=jnp.float32,
    )
    slot_dresid = jnp.dot(slot_onehot, dembedded, precision=EXACT_PRECISION) / slot_len
    received_grad = (slot_gate * slot_dresid).astype(jnp.bfloat16)
    slot_dgate = jnp.sum(slot_dresid * out_float, axis=1)
    returned = lax.all_to_all(
        slot_dgate.reshape(device_count, capacity),
        ("expert", "tensor"),
        split_axis=0,
        concat_axis=0,
        tiled=True,
    )
    dgate_prob = returned.reshape(expert_total * capacity)[target].reshape(local_rows, top_count)
    dhidden = contract_last(received_grad, down_weight[0])
    gate_sigmoid = jax.nn.sigmoid(pre_gate)
    dpre_gate = (dhidden * pre_up * gate_sigmoid * (1.0 + pre_gate * (1.0 - gate_sigmoid))).astype(
        jnp.bfloat16
    )
    dpre_up = (dhidden * jax.nn.silu(pre_gate)).astype(jnp.bfloat16)
    dx_rows = (
        contract_last(dpre_gate, gate_weight[0]) + contract_last(dpre_up, up_weight[0])
    ).astype(jnp.bfloat16)
    dx_moe = jnp.sum(
        move_rows(dx_rows.reshape(device_count, capacity, model_width))
        .reshape(expert_total * capacity, model_width)[target]
        .astype(jnp.float32)
        .reshape(local_rows, top_count, model_width),
        axis=1,
    )
    dchosen = gate_probs * (dgate_prob - jnp.sum(gate_probs * dgate_prob, axis=1, keepdims=True))
    dlogits = jnp.sum(dchosen[:, :, None] * expert_onehot, axis=1).astype(jnp.bfloat16)
    dnormed = dx_moe + contract_last(dlogits, router)
    gain_grad = dnormed * norm_gain
    grad_resid = (
        dresid_out
        + rms_scale * gain_grad
        - resid_mid * rms_scale**3 * jnp.mean(gain_grad * resid_mid, axis=1, keepdims=True)
    )
    return (loss_value.reshape(1), grad_resid.astype(jnp.bfloat16))


ROW_EXTRA = 128
LEAVES_IN = ((0, 1), (3, 2))
INNER_SWAP = ((1, 2), (2, 1))
LEAVES_OUT = ((1, 0), (2, 3))
BLOCK_ORDER = ((3, 2, 1, 0), (3, 0, 2, 1), (0, 3, 1, 2), (0, 1, 2, 3))
BF16 = jnp.bfloat16
F32 = jnp.float32


def dot_nn(left, right):
    return lax.dot_general(left, right, (((1,), (0,)), ((), ())), preferred_element_type=F32)


def halves(value):
    high = value.astype(BF16)
    return high, (value - high.astype(F32)).astype(BF16)


def stacked_halves(value):
    high, low = halves(value)
    return jnp.concatenate([high.astype(F32), low.astype(F32)], axis=0).astype(BF16)


def fold(product):
    rows = product.shape[0] // 2
    return product[:rows] + product[rows:]


def iota(shape, axis):
    return lax.broadcasted_iota(jnp.int32, shape, axis)


def dispatch_kernel(capacity, numbers, t_ref, gain_ref, router_ref, mask_ref, token_ref, *outs):
    row_refs, place_ref = outs[:4], outs[4]
    width = t_ref.shape[1]
    rows = t_ref.shape[0]
    experts = router_ref.shape[0]
    x = t_ref[...].astype(F32)
    scale = lax.rsqrt(jnp.mean(x * x, axis=1, keepdims=True) + EPSILON)
    normed = (x * scale * gain_ref[...]).astype(BF16)
    logits = contract_last(router_ref[...], normed)
    mask = mask_ref[...]
    chosen = mask.astype(F32) > 0.5
    exp_chosen = jnp.where(chosen, jnp.exp(jnp.where(chosen, logits, 0.0)), 0.0)
    gates = exp_chosen / jnp.sum(exp_chosen, axis=0, keepdims=True)
    earlier = (iota((rows, rows), 0) < iota((rows, rows), 1)).astype(F32).astype(BF16)
    position = jnp.where(chosen, dot_nn(mask, earlier), -1.0)
    gate_high, gate_low = halves(gates)
    inverse = token_ref[1:2, :]
    inv_high = inverse.astype(BF16).astype(F32)
    inv_mid = (inverse - inv_high).astype(BF16).astype(F32)
    inv_low = inverse - inv_high - inv_mid
    slot_row = iota((8, rows), 0)
    token_part = jnp.where(
        slot_row == 0,
        token_ref[0:1, :],
        jnp.where(slot_row == 1, inv_high, jnp.where(slot_row == 2, inv_mid, jnp.where(slot_row == 3, inv_low, 0.0))),
    )
    extra = jnp.concatenate(
        [
            gate_high.astype(F32),
            gate_low.astype(F32),
            token_part,
            jnp.zeros((ROW_EXTRA - 2 * experts - 8, rows), F32),
        ],
        axis=0,
    ).astype(BF16)
    expert_row = iota((experts, rows), 0)
    slot = iota((capacity, rows), 0).astype(F32)
    picks = []
    for way in range(4):
        own = jnp.sum(jnp.where(expert_row == numbers[way], position, 0.0), axis=0, keepdims=True)
        picks.append((slot == own).astype(F32))
    picked = jnp.concatenate(picks, axis=0)
    place_ref[...] = jnp.transpose(picked).astype(BF16)
    picked = picked.astype(BF16)
    sent = dot_nn(picked, normed)
    sent_extra = contract_last(picked, extra)
    for way in range(4):
        at = slice(way * capacity, (way + 1) * capacity)
        row_refs[way][:, :width] = sent[at].astype(BF16)
        row_refs[way][:, width:] = sent_extra[at].astype(BF16)


def expert_kernel(numbers, r0, r1, r2, r3, gate_ref, up_ref, hidden_ref, a_ref, b_ref, pooled_ref, info_ref, x_ref, weight_ref):
    width = gate_ref.shape[0]
    experts = 16

    @pl.when(pl.program_id(0) == 0)
    def _():
        x_ref[...] = jnp.concatenate([r[:, :width].astype(F32) for r in (r0, r1, r2, r3)], axis=0).astype(BF16)
        extra = jnp.concatenate([r[:, width:].astype(F32) for r in (r0, r1, r2, r3)], axis=0).astype(BF16)
        own = numbers[0]

        def mixer(source, goal):
            gates = (goal < experts) & ((source == goal) | (source == goal + experts))
            sequence = (goal == experts) & (source == 2 * experts)
            inverse = (goal == experts + 1) & (source > 2 * experts) & (source < 2 * experts + 4)
            gate = (goal == experts + 2) & ((source == own) | (source == own + experts))
            return (gates | sequence | inverse | gate).astype(F32).astype(BF16)

        square = (ROW_EXTRA, ROW_EXTRA)
        info = dot_nn(extra, mixer(iota(square, 0), iota(square, 1)))
        info_ref[...] = info
        turned = contract_last(mixer(iota(square, 1), iota(square, 0)), extra)
        sequence = turned[experts : experts + 1]
        weight = turned[experts + 1 : experts + 2] * turned[experts + 2 : experts + 3]
        pool = jnp.where(iota((pooled_ref.shape[0], extra.shape[0]), 0).astype(F32) == sequence, weight, 0.0)
        weight_ref[...] = stacked_halves(pool)

    x = x_ref[...]
    pre_gate = dot_nn(x, gate_ref[...])
    pre_up = dot_nn(x, up_ref[...])
    sigmoid = 1.0 / (1.0 + jnp.exp(-pre_gate))
    silu = pre_gate * sigmoid
    hidden = (silu * pre_up).astype(BF16)
    hidden_ref[...] = hidden
    a_ref[...] = pre_up * sigmoid * (1.0 + pre_gate * (1.0 - sigmoid))
    b_ref[...] = silu
    pooled_ref[...] = fold(dot_nn(weight_ref[...], hidden))


def embed_kernel(numbers, p0, p1, p2, p3, down_ref, t_ref, token_ref, o0, o1, o2, o3, part_ref):
    pooled = p0[...] + p1[...] + p2[...] + p3[...]
    part = fold(dot_nn(stacked_halves(pooled), down_ref[...]))
    sequences = part.shape[0]
    own = jnp.where(
        iota((sequences, t_ref.shape[0]), 0).astype(F32) == token_ref[0:1, :], token_ref[1:2, :], 0.0
    )
    part_ref[...] = part + fold(dot_nn(stacked_halves(own), t_ref[...]))
    rows = o0.shape[0]
    for way, out in enumerate((o0, o1, o2, o3)):
        out[...] = part_ref[pl.ds(pl.multiple_of(numbers[way] * rows, rows), rows), :]


def contrast_kernel(numbers, q0, q1, q2, q3, down_ref, loss_ref, grad_ref, hidden_grad_ref, all_ref):
    rows = q0.shape[0]
    for way, part in enumerate((q0, q1, q2, q3)):
        all_ref[pl.ds(pl.multiple_of(numbers[way] * rows, rows), rows), :] = part[...]
    embedded = all_ref[...]
    count = embedded.shape[0]
    pairs = count // 2
    norms = jnp.sqrt(jnp.sum(embedded * embedded, axis=1, keepdims=True) + EPSILON)
    unit = embedded / norms
    scores = (
        lax.dot_general(
            unit, unit, (((1,), (1,)), ((), ())), precision=EXACT_PRECISION, preferred_element_type=F32
        )
        / SOFTMAX_WARMTH
    )
    row, column = iota((count, count), 0), iota((count, count), 1)
    is_pair = (row % 2 == 0) & (column % 2 == 1)
    matched = is_pair & (column == row + 1)
    exp_scores = jnp.where(is_pair, jnp.exp(jnp.where(is_pair, scores, 0.0)), 0.0)
    row_total = jnp.sum(exp_scores, axis=1, keepdims=True)
    is_query = iota((count, 1), 0) % 2 == 0
    row_total = jnp.where(is_query, row_total, 1.0)
    own_score = jnp.sum(jnp.where(matched, scores, 0.0), axis=1, keepdims=True)
    terms = jnp.where(is_query, jnp.log(row_total) - own_score, 0.0)
    loss_ref[...] = jnp.broadcast_to(jnp.sum(terms, axis=0, keepdims=True) / pairs, loss_ref.shape)
    dscore = (exp_scores / row_total - jnp.where(matched, 1.0, 0.0)) * (LOSS_SCALE / pairs)
    both = dscore + jnp.transpose(dscore)
    dunit = (
        lax.dot_general(
            both, unit, (((1,), (0,)), ((), ())), precision=EXACT_PRECISION, preferred_element_type=F32
        )
        / SOFTMAX_WARMTH
    )
    radial = jnp.sum(unit * dunit, axis=1, keepdims=True)
    grad = (dunit - unit * radial) / norms
    grad_ref[...] = grad
    hidden_grad_ref[...] = fold(contract_last(stacked_halves(grad), down_ref[...]))


def backward_kernel(capacity, numbers, a_ref, b_ref, hidden_ref, info_ref, dh_ref, gate_ref, up_ref, router_ref, o0, o1, o2, o3, dgate_ref, dup_ref, dlog_ref):
    experts = 16

    @pl.when(pl.program_id(0) == 0)
    def _():
        info = info_ref[0]
        slots = info.shape[0]
        sequence = info[:, experts : experts + 1]
        weight = info[:, experts + 1 : experts + 2] * info[:, experts + 2 : experts + 3]
        member = (iota((slots, dh_ref.shape[0]), 1).astype(F32) == sequence).astype(F32).astype(BF16)
        high, low = halves(dh_ref[...])
        dhidden = weight * (dot_nn(member, high) + dot_nn(member, low))
        dgate_ref[...] = (dhidden * a_ref[0]).astype(BF16)
        dup_ref[...] = (dhidden * b_ref[0]).astype(BF16)
        moved = jnp.sum(dhidden * hidden_ref[0].astype(F32), axis=1, keepdims=True)
        lane = iota((slots, ROW_EXTRA), 1)
        gates = jnp.where(lane < experts, info, 0.0)
        dlog_ref[...] = (moved * (jnp.where(lane == numbers[1], 1.0, 0.0) - gates)).astype(BF16)

    total = (
        contract_last(dgate_ref[...], gate_ref[...])
        + contract_last(dup_ref[...], up_ref[...])
        + dot_nn(dlog_ref[...], router_ref[...])
    )
    for way, out in enumerate((o0, o1, o2, o3)):
        out[...] = total[way * capacity : (way + 1) * capacity].astype(BF16)


def combine_kernel(numbers, place_ref, r0, r1, r2, r3, out_ref):
    rows = jnp.concatenate([r[...].astype(F32) for r in (r0, r1, r2, r3)], axis=0).astype(BF16)
    out_ref[...] = dot_nn(place_ref[0], rows)


def finish_kernel(t_ref, gain_ref, grad_ref, token_ref, own_ref, r4, r5, r6, out_ref):
    x = t_ref[...].astype(F32)
    scale = lax.rsqrt(jnp.mean(x * x, axis=1, keepdims=True) + EPSILON)
    sequences = grad_ref.shape[0]
    spread = jnp.where(
        iota((sequences, x.shape[0]), 0).astype(F32) == token_ref[0:1, :], 1.0, 0.0
    )
    spread = jnp.transpose(spread).astype(BF16)
    inverse = jnp.transpose(token_ref[...])[:, 1:2]
    high, low = halves(grad_ref[...])
    dresid = inverse * (dot_nn(spread, high) + dot_nn(spread, low))
    dnormed = own_ref[...] + r4[...].astype(F32) + r5[...].astype(F32) + r6[...].astype(F32)
    gained = dnormed * gain_ref[...]
    out = dresid + scale * gained - x * (scale * scale * scale) * jnp.mean(gained * x, axis=1, keepdims=True)
    out_ref[...] = out.astype(BF16)


def whole_call(kernel, outs, *args, scratch=(), numbers=0, limit=40, flops=0):
    spec = pl.BlockSpec(memory_space=pltpu.VMEM)
    smem = pl.BlockSpec(memory_space=pltpu.SMEM)
    moved = sum(a.size * a.dtype.itemsize for a in args)
    return pl.pallas_call(
        kernel,
        out_shape=outs,
        in_specs=[smem] * numbers + [spec] * (len(args) - numbers),
        out_specs=jax.tree.map(lambda _: spec, outs),
        scratch_shapes=scratch,
        compiler_params=pltpu.CompilerParams(vmem_limit_bytes=limit * 2**20),
        cost_estimate=pl.CostEstimate(flops=flops, bytes_accessed=moved, transcendentals=0),
    )(*args)


def fast_body(context, o_weight, resid, norm_gain, router, gate_weight, up_weight, down_weight, expert_ids, lengths):
    e = lax.axis_index("expert")
    z = lax.axis_index("tensor")
    rows, width = resid.shape
    experts = router.shape[1]
    top = expert_ids.shape[1]
    seq_count = lengths.shape[1]
    sequences = 4 * seq_count
    hidden_width = gate_weight.shape[2]
    capacity = max(2, rows * top * 5 // (4 * experts))
    slots = 4 * capacity
    is_leaf = (z == 0) | (z == 3)
    ways = e ^ jnp.arange(4, dtype=jnp.int32)
    way_experts = ways * 4 + z
    own_expert = (e * 4 + z).astype(jnp.int32)
    gate_w, up_w, down_w = gate_weight[0], up_weight[0], down_weight[0]
    gain = norm_gain.reshape(1, width)
    router_turned = router.T
    router_rows = jnp.zeros((ROW_EXTRA, width), BF16).at[:experts].set(router_turned)

    def along_z(value, pairs):
        return lax.ppermute(value, "tensor", pairs)

    def swap_z(value, bits):
        return lax.ppermute(value, "tensor", [(i, i ^ bits) for i in range(4)])

    def swap_e(value, bits):
        return lax.ppermute(value, "expert", [(i, i ^ bits) for i in range(4)])

    mask_own = jnp.sum(
        (expert_ids[None, :, :] == jnp.arange(experts, dtype=jnp.int32)[:, None, None]).astype(F32), axis=2
    )
    mask_wide = jnp.concatenate([jnp.where(z == c, mask_own, 0.0) for c in range(4)], axis=1).astype(BF16)
    mask_sum = mask_wide + along_z(mask_wide, LEAVES_IN)
    mask_sum = mask_sum + along_z(mask_sum, INNER_SWAP)
    mask_back = along_z(mask_sum, LEAVES_OUT)
    mask_all = jnp.where(is_leaf, mask_back, mask_sum)

    seq_lengths = lengths[0]
    seq_ends = jnp.cumsum(seq_lengths)
    places = jnp.arange(4 * rows, dtype=jnp.int32)
    after = places[None, :] >= seq_ends[:, None]
    seq_local = jnp.sum(after.astype(jnp.int32), axis=0)
    token_len = jnp.sum(
        jnp.where(seq_local[None, :] == jnp.arange(seq_count, dtype=jnp.int32)[:, None], seq_lengths[:, None], 0), axis=0
    )
    token_info = jnp.concatenate(
        [
            (seq_local + e * seq_count).astype(F32)[None],
            (1.0 / token_len.astype(F32))[None],
            jnp.zeros((6, 4 * rows), F32),
        ],
        axis=0,
    )
    token_own = lax.dynamic_slice_in_dim(token_info, z * rows, rows, 1)

    totals, received, placed = [], [], []
    for c in range(4):
        part = jnp.dot(context[c * rows : (c + 1) * rows], o_weight, preferred_element_type=F32)
        part = (part + jnp.where(z == c, resid.astype(F32), 0.0)).astype(BF16)
        arrived = along_z(part, LEAVES_IN)
        half = (part.astype(F32) + arrived.astype(F32)).astype(BF16)
        other = along_z(half, INNER_SWAP)
        total = (half.astype(F32) + other.astype(F32)).astype(BF16)
        back = along_z(total, LEAVES_OUT)
        total = jnp.where(is_leaf, back, total)
        totals.append(total)
        *sent, place = whole_call(
            functools.partial(dispatch_kernel, capacity),
            [jax.ShapeDtypeStruct((capacity, width + ROW_EXTRA), BF16)] * 4
            + [jax.ShapeDtypeStruct((rows, slots), BF16)],
            way_experts,
            total,
            gain,
            router_turned,
            mask_all[:, c * rows : (c + 1) * rows],
            token_info[:, c * rows : (c + 1) * rows],
            numbers=1,
            flops=2 * slots * rows * width,
        )
        placed.append(place)
        received.append([sent[0]] + [swap_e(sent[way], way) for way in (1, 2, 3)])

    tile = 256
    hiddens, a_parts, b_parts, pools, infos = [], [], [], [], []
    for c in range(4):
        whole = pl.BlockSpec((capacity, width + ROW_EXTRA), lambda j, n: (0, 0))
        hid, a, b, pool, info = pl.pallas_call(
            expert_kernel,
            out_shape=[
                jax.ShapeDtypeStruct((slots, hidden_width), BF16),
                jax.ShapeDtypeStruct((slots, hidden_width), F32),
                jax.ShapeDtypeStruct((slots, hidden_width), F32),
                jax.ShapeDtypeStruct((sequences, hidden_width), F32),
                jax.ShapeDtypeStruct((slots, ROW_EXTRA), F32),
            ],
            grid_spec=pltpu.PrefetchScalarGridSpec(
                num_scalar_prefetch=1,
                grid=(hidden_width // tile,),
                in_specs=[whole] * 4 + [pl.BlockSpec((width, tile), lambda j, n: (0, j))] * 2,
                out_specs=[
                    pl.BlockSpec((slots, tile), lambda j, n: (0, j)),
                    pl.BlockSpec((slots, tile), lambda j, n: (0, j)),
                    pl.BlockSpec((slots, tile), lambda j, n: (0, j)),
                    pl.BlockSpec((sequences, tile), lambda j, n: (0, j)),
                    pl.BlockSpec((slots, ROW_EXTRA), lambda j, n: (0, 0)),
                ],
                scratch_shapes=[pltpu.VMEM((slots, width), BF16), pltpu.VMEM((2 * sequences, slots), BF16)],
            ),
            compiler_params=pltpu.CompilerParams(vmem_limit_bytes=40 * 2**20),
            cost_estimate=pl.CostEstimate(
                flops=4 * slots * width * hidden_width, bytes_accessed=4 * width * hidden_width, transcendentals=0
            ),
        )(own_expert.reshape(1), *received[c], gate_w, up_w)
        hiddens.append(hid)
        a_parts.append(a)
        b_parts.append(b)
        pools.append(pool)
        infos.append(info)

    total_own = lax.select_n(z, *totals)
    seq_shape = jax.ShapeDtypeStruct((seq_count, width), F32)
    quarters = whole_call(
        embed_kernel,
        [seq_shape] * 4,
        ways,
        *pools,
        down_w,
        total_own,
        token_own,
        scratch=[pltpu.VMEM((sequences, width), F32)],
        numbers=1,
        flops=4 * sequences * hidden_width * width,
    )
    mine = (quarters[0] + swap_e(quarters[1], 1)) + (swap_e(quarters[2], 2) + swap_e(quarters[3], 3))
    mine = (mine + swap_z(mine, 1)) + (swap_z(mine, 2) + swap_z(mine, 3))
    pieces = [mine] + [swap_e(mine, way) for way in (1, 2, 3)]
    loss, dembedded, hidden_grad = whole_call(
        contrast_kernel,
        [
            jax.ShapeDtypeStruct((1, 128), F32),
            jax.ShapeDtypeStruct((sequences, width), F32),
            jax.ShapeDtypeStruct((sequences, hidden_width), F32),
        ],
        ways,
        *pieces,
        down_w,
        scratch=[pltpu.VMEM((sequences, width), F32)],
        numbers=1,
        flops=4 * sequences * hidden_width * width,
    )

    hidden_all, a_all, b_all, info_all = (jnp.stack(part) for part in (hiddens, a_parts, b_parts, infos))
    place_all = jnp.stack(placed)
    order = jnp.asarray(BLOCK_ORDER, jnp.int32)[z]
    tile = 512
    sums = []
    for j in range(4):
        numbers = jnp.stack([order[j], own_expert])
        block = lambda shape: pl.BlockSpec((1,) + shape, lambda i, n: (n[0], 0, 0))
        out_spec = pl.BlockSpec((capacity, tile), lambda i, n: (0, i))
        grads = pl.pallas_call(
            functools.partial(backward_kernel, capacity),
            out_shape=[jax.ShapeDtypeStruct((capacity, width), BF16)] * 4,
            grid_spec=pltpu.PrefetchScalarGridSpec(
                num_scalar_prefetch=1,
                grid=(width // tile,),
                in_specs=[
                    block((slots, hidden_width)),
                    block((slots, hidden_width)),
                    block((slots, hidden_width)),
                    block((slots, ROW_EXTRA)),
                    pl.BlockSpec((sequences, hidden_width), lambda i, n: (0, 0)),
                    pl.BlockSpec((tile, hidden_width), lambda i, n: (i, 0)),
                    pl.BlockSpec((tile, hidden_width), lambda i, n: (i, 0)),
                    pl.BlockSpec((ROW_EXTRA, tile), lambda i, n: (0, i)),
                ],
                out_specs=[out_spec] * 4,
                scratch_shapes=[
                    pltpu.VMEM((slots, hidden_width), BF16),
                    pltpu.VMEM((slots, hidden_width), BF16),
                    pltpu.VMEM((slots, ROW_EXTRA), BF16),
                ],
            ),
            compiler_params=pltpu.CompilerParams(vmem_limit_bytes=40 * 2**20),
            cost_estimate=pl.CostEstimate(
                flops=4 * slots * width * hidden_width, bytes_accessed=4 * width * hidden_width, transcendentals=0
            ),
        )(numbers, a_all, b_all, hidden_all, info_all, hidden_grad, gate_w, up_w, router_rows)
        back = [grads[0]] + [swap_e(grads[way], way) for way in (1, 2, 3)]
        rows_spec = pl.BlockSpec((capacity, width), lambda i, n: (0, 0))
        summed = pl.pallas_call(
            combine_kernel,
            out_shape=jax.ShapeDtypeStruct((rows, width), F32),
            grid_spec=pltpu.PrefetchScalarGridSpec(
                num_scalar_prefetch=1,
                grid=(1,),
                in_specs=[pl.BlockSpec((1, rows, slots), lambda i, n: (n[0], 0, 0))] + [rows_spec] * 4,
                out_specs=pl.BlockSpec((rows, width), lambda i, n: (0, 0)),
            ),
            compiler_params=pltpu.CompilerParams(vmem_limit_bytes=40 * 2**20),
            cost_estimate=pl.CostEstimate(
                flops=2 * slots * rows * width, bytes_accessed=8 * rows * width, transcendentals=0
            ),
        )(numbers, place_all, *back)
        sums.append(summed)

    def narrow(value):
        return value.astype(BF16)

    got1 = along_z(narrow(sums[0]), LEAVES_IN)
    got2 = along_z(narrow(sums[1]), LEAVES_IN)
    got3 = along_z(narrow(sums[0] + got1.astype(F32)), INNER_SWAP)
    got4 = along_z(narrow(sums[2]), LEAVES_IN)
    got5 = along_z(narrow(sums[2] + got2.astype(F32)), INNER_SWAP)
    got6 = along_z(narrow(sums[1] + got3.astype(F32)), LEAVES_OUT)
    grad = whole_call(
        finish_kernel,
        jax.ShapeDtypeStruct((rows, width), BF16),
        total_own,
        gain,
        dembedded,
        token_own,
        sums[3],
        got4,
        got5,
        got6,
        flops=4 * rows * sequences * width,
    )
    return loss[0, :1], grad


def solution(mesh):
    shape = dict(mesh.shape)
    part_body = fast_body if (shape["expert"], shape["tensor"]) == (4, 4) else body
    in_specs = (
        P(("groups", "expert"), "tensor"),
        P("tensor", None),
        P(("groups", "expert", "tensor"), None),
        P(),
        P(),
        P(("expert", "tensor"), None, None),
        P(("expert", "tensor"), None, None),
        P(("expert", "tensor"), None, None),
        P(("groups", "expert", "tensor"), None),
        P(("groups", "expert"), None),
    )
    out_specs = (P("groups"), P(("groups", "expert", "tensor"), None))
    return jax.shard_map(part_body, mesh=mesh, in_specs=in_specs, out_specs=out_specs, check_vma=False)
```

```python
import functools

import jax
import jax.numpy as jnp
from jax import lax
from jax.experimental import pallas as pl
from jax.experimental.pallas import tpu as pltpu
from jax.sharding import PartitionSpec as P

EPSILON = 1e-06
SOFTMAX_WARMTH = 0.05
LOSS_SCALE = 32768.0
EXACT_PRECISION = lax.Precision.HIGHEST


def slot_positions(flat_ids, expert_total):
    onehot = (flat_ids[..., None] == jnp.arange(expert_total, dtype=jnp.int32)).astype(jnp.int32)
    before = jnp.cumsum(onehot, axis=-2) - onehot
    return jnp.sum(before * onehot, axis=-1)


def contract_last(left, right):
    return lax.dot_general(
        left, right, (((1,), (1,)), ((), ())), preferred_element_type=jnp.float32
    )


def contrast(embedded):
    pair_count = embedded.shape[0] // 2
    norms = jnp.sqrt(jnp.sum(embedded * embedded, axis=1, keepdims=True) + EPSILON)
    unit_rows = embedded / norms
    query_rows = unit_rows[0::2]
    passage_rows = unit_rows[1::2]
    similarity_scores = (
        jnp.dot(query_rows, passage_rows.T, precision=EXACT_PRECISION) / SOFTMAX_WARMTH
    )
    exp_scores = jnp.exp(similarity_scores)
    row_total = jnp.sum(exp_scores, axis=1, keepdims=True)
    loss_value = jnp.mean(jnp.log(row_total[:, 0]) - jnp.diagonal(similarity_scores))
    score_gradient = (
        exp_scores / row_total - jnp.eye(pair_count, dtype=similarity_scores.dtype)
    ) * (LOSS_SCALE / pair_count)
    query_gradient = (
        jnp.dot(score_gradient, passage_rows, precision=EXACT_PRECISION) / SOFTMAX_WARMTH
    )
    passage_gradient = (
        jnp.dot(score_gradient.T, query_rows, precision=EXACT_PRECISION) / SOFTMAX_WARMTH
    )
    dunit_rows = jnp.stack([query_gradient, passage_gradient], axis=1).reshape(embedded.shape)
    radial = jnp.sum(unit_rows * dunit_rows, axis=1, keepdims=True)
    return (loss_value, (dunit_rows - unit_rows * radial) / norms)


def body(
    context,
    o_weight,
    resid,
    norm_gain,
    router,
    gate_weight,
    up_weight,
    down_weight,
    expert_ids,
    lengths,
):
    expert_count = lax.axis_size("expert")
    tensor_count = lax.axis_size("tensor")
    device_count = expert_count * tensor_count
    expert_index = lax.axis_index("expert")
    tensor_index = lax.axis_index("tensor")
    local_rows, model_width = resid.shape
    expert_total = router.shape[1]
    top_count = expert_ids.shape[1]
    seq_count = lengths.shape[1]
    seq_total = seq_count * expert_count
    capacity = max(2, local_rows * top_count * 5 // (4 * expert_total))
    attention_out = lax.psum_scatter(
        jnp.dot(context, o_weight, preferred_element_type=jnp.float32).astype(jnp.bfloat16),
        "tensor",
        scatter_dimension=0,
        tiled=True,
    ).astype(jnp.float32)
    resid_mid = resid.astype(jnp.float32) + attention_out
    rms_scale = lax.rsqrt(jnp.mean(resid_mid * resid_mid, axis=1, keepdims=True) + EPSILON)
    normed = (resid_mid * rms_scale * norm_gain).astype(jnp.bfloat16)
    logits = jnp.dot(normed, router, preferred_element_type=jnp.float32)
    expert_onehot = (expert_ids[:, :, None] == jnp.arange(expert_total, dtype=jnp.int32)).astype(
        jnp.float32
    )
    chosen = jnp.sum(logits[:, None, :] * expert_onehot, axis=2)
    exp_chosen = jnp.exp(chosen)
    gate_probs = exp_chosen / jnp.sum(exp_chosen, axis=1, keepdims=True)
    flat_ids = expert_ids.reshape(local_rows * top_count)
    target = flat_ids * capacity + slot_positions(flat_ids, expert_total)

    def move_rows(blocks):
        return lax.all_to_all(blocks, ("expert", "tensor"), split_axis=0, concat_axis=0, tiled=True)

    seq_lengths = lengths[0]
    seq_ends = jnp.cumsum(seq_lengths)
    seq_starts = seq_ends - seq_lengths
    positions = tensor_index * local_rows + jnp.arange(local_rows, dtype=jnp.int32)
    member = (
        (positions[None, :] >= seq_starts[:, None]) & (positions[None, :] < seq_ends[:, None])
    ).astype(jnp.float32)
    tok_len = jnp.sum(member * seq_lengths[:, None].astype(jnp.float32), axis=0)
    repeated = jnp.broadcast_to(normed[:, None, :], (local_rows, top_count, model_width)).reshape(
        local_rows * top_count, model_width
    )
    buffer = (
        jnp.zeros((expert_total * capacity, model_width), jnp.bfloat16).at[target].set(repeated)
    )
    received = move_rows(buffer.reshape(device_count, capacity, model_width)).reshape(
        device_count * capacity, model_width
    )
    pre_gate = jnp.dot(received, gate_weight[0], preferred_element_type=jnp.float32)
    pre_up = jnp.dot(received, up_weight[0], preferred_element_type=jnp.float32)
    hidden = (jax.nn.silu(pre_gate) * pre_up).astype(jnp.bfloat16)
    expert_rows = jnp.dot(hidden, down_weight[0], preferred_element_type=jnp.float32).astype(
        jnp.bfloat16
    )
    seq_local = jnp.dot(jnp.arange(seq_count, dtype=jnp.float32), member, precision=EXACT_PRECISION)
    seq_global = seq_local + (expert_index * seq_count).astype(jnp.float32)
    info_rows = jnp.stack(
        [
            gate_probs,
            jnp.broadcast_to(seq_global[:, None], (local_rows, top_count)),
            jnp.broadcast_to(tok_len[:, None], (local_rows, top_count)),
        ],
        axis=2,
    ).reshape(local_rows * top_count, 3)
    info_init = jnp.zeros((expert_total * capacity, 3), jnp.float32).at[:, 2].set(1.0)
    info_buffer = info_init.at[target].set(info_rows).reshape(device_count, capacity, 3)
    slot_data = lax.all_to_all(
        info_buffer, ("expert", "tensor"), split_axis=0, concat_axis=0, tiled=True
    ).reshape(device_count * capacity, 3)
    slot_gate = slot_data[:, 0:1]
    slot_seq = slot_data[:, 1].astype(jnp.int32)
    slot_len = slot_data[:, 2:3]
    slot_onehot = (slot_seq[:, None] == jnp.arange(seq_total, dtype=jnp.int32)).astype(jnp.float32)
    out_float = expert_rows.astype(jnp.float32)
    expert_part = lax.dot_general(
        slot_onehot,
        slot_gate * out_float / slot_len,
        (((0,), (0,)), ((), ())),
        precision=EXACT_PRECISION,
        preferred_element_type=jnp.float32,
    )
    partial_value = jnp.dot(member, resid_mid / tok_len[:, None], precision=EXACT_PRECISION)
    placed = lax.dynamic_update_slice_in_dim(
        expert_part,
        lax.dynamic_slice_in_dim(expert_part, expert_index * seq_count, seq_count, 0)
        + partial_value,
        expert_index * seq_count,
        0,
    )
    embedded = lax.psum(placed, ("expert", "tensor"))
    loss_value, dembedded = contrast(embedded)
    own_rows = lax.dynamic_slice_in_dim(
        dembedded, expert_index * seq_count, seq_count, 0
    ) / seq_lengths[:, None].astype(jnp.float32)
    dresid_out = lax.dot_general(
        member,
        own_rows,
        (((0,), (0,)), ((), ())),
        precision=EXACT_PRECISION,
        preferred_element_type=jnp.float32,
    )
    slot_dresid = jnp.dot(slot_onehot, dembedded, precision=EXACT_PRECISION) / slot_len
    received_grad = (slot_gate * slot_dresid).astype(jnp.bfloat16)
    slot_dgate = jnp.sum(slot_dresid * out_float, axis=1)
    returned = lax.all_to_all(
        slot_dgate.reshape(device_count, capacity),
        ("expert", "tensor"),
        split_axis=0,
        concat_axis=0,
        tiled=True,
    )
    dgate_prob = returned.reshape(expert_total * capacity)[target].reshape(local_rows, top_count)
    dhidden = contract_last(received_grad, down_weight[0])
    gate_sigmoid = jax.nn.sigmoid(pre_gate)
    dpre_gate = (dhidden * pre_up * gate_sigmoid * (1.0 + pre_gate * (1.0 - gate_sigmoid))).astype(
        jnp.bfloat16
    )
    dpre_up = (dhidden * jax.nn.silu(pre_gate)).astype(jnp.bfloat16)
    dx_rows = (
        contract_last(dpre_gate, gate_weight[0]) + contract_last(dpre_up, up_weight[0])
    ).astype(jnp.bfloat16)
    dx_moe = jnp.sum(
        move_rows(dx_rows.reshape(device_count, capacity, model_width))
        .reshape(expert_total * capacity, model_width)[target]
        .astype(jnp.float32)
        .reshape(local_rows, top_count, model_width),
        axis=1,
    )
    dchosen = gate_probs * (dgate_prob - jnp.sum(gate_probs * dgate_prob, axis=1, keepdims=True))
    dlogits = jnp.sum(dchosen[:, :, None] * expert_onehot, axis=1).astype(jnp.bfloat16)
    dnormed = dx_moe + contract_last(dlogits, router)
    gain_grad = dnormed * norm_gain
    grad_resid = (
        dresid_out
        + rms_scale * gain_grad
        - resid_mid * rms_scale**3 * jnp.mean(gain_grad * resid_mid, axis=1, keepdims=True)
    )
    return (loss_value.reshape(1), grad_resid.astype(jnp.bfloat16))


ROW_EXTRA = 128
LEAVES_IN = ((0, 1), (3, 2))
INNER_SWAP = ((1, 2), (2, 1))
LEAVES_OUT = ((1, 0), (2, 3))
PIECES = (1, 1, 1, 2)
FORWARD_ORDER = (
    "p0", "p1", "p2", "s0", "p3", "s1", "t0", "p4", "s2", "t1", "d0", "s3", "t2", "d1", "x0", "s4", "t3", "t4", "d2", "x1", "d3", "x2", "x3",
)
VMEM_LIMIT = 24 * 2**20
BLOCK_ORDER = ((3, 2, 1, 0), (3, 0, 2, 1), (0, 3, 1, 2), (0, 1, 2, 3))
OWN_EXPERT, LEAF, Z, PEER, PEER_EXPERT, ORDER = 0, 1, 2, 3, 7, 11
BF16 = jnp.bfloat16
F32 = jnp.float32


def dot_nn(left, right):
    return lax.dot_general(left, right, (((1,), (0,)), ((), ())), preferred_element_type=F32)


def halves(value):
    high = value.astype(BF16)
    return high, (value - high.astype(F32)).astype(BF16)


def stacked_halves(value):
    high, low = halves(value)
    return jnp.concatenate([high.astype(F32), low.astype(F32)], axis=0).astype(BF16)


def fold(product):
    rows = product.shape[0] // 2
    return product[:rows] + product[rows:]


def iota(shape, axis):
    return lax.broadcasted_iota(jnp.int32, shape, axis)


def project_kernel(block, offset, n, context_ref, weight_ref, resid_ref, *rest):
    out_ref = rest[-1]
    rows = context_ref.shape[0]
    part = dot_nn(context_ref[...], weight_ref[...])
    share = jnp.where(n[Z] == block, resid_ref[offset : offset + rows, :].astype(F32), 0.0)
    out_ref[:rows, :] = (part + share).astype(BF16)
    if block == 0:
        mask = rest[0][...]
        out_ref[rows:, :] = jnp.where(pl.program_id(0) == 0, mask.astype(F32), 0.0).astype(BF16)


def add_kernel(n, left_ref, right_ref, _, out_ref):
    out_ref[...] = (left_ref[...].astype(F32) + right_ref[...].astype(F32)).astype(BF16)


def dispatch_kernel(capacity, block, pieces, n, *refs):
    inner_refs, back_refs, refs = refs[:pieces], refs[pieces : 2 * pieces], refs[2 * pieces :]
    gain_ref, router_ref, token_ref, *refs = refs
    rows = token_ref.shape[1]
    outs = refs[-7:] if block == 0 else refs[-6:]
    row_refs, t_ref, place_ref = outs[:4], outs[4], outs[5]
    experts, width = router_ref.shape
    x = jnp.concatenate(
        [
            jnp.where(n[LEAF] == 1, back[...].astype(F32), inner[...].astype(F32))
            for inner, back in zip(inner_refs, back_refs)
        ],
        axis=0,
    )
    if block == 0:
        wide = x[rows:, : 4 * rows].astype(BF16)
        outs[6][...] = wide
        x = x[:rows]
    else:
        wide = refs[0][...]
    mask = wide[:, block * rows : (block + 1) * rows]
    t_ref[0] = x.astype(BF16)
    scale = lax.rsqrt(jnp.mean(x * x, axis=1, keepdims=True) + EPSILON)
    normed = (x * scale * gain_ref[...]).astype(BF16)
    logits = contract_last(router_ref[...], normed)
    chosen = mask.astype(F32) > 0.5
    exp_chosen = jnp.where(chosen, jnp.exp(jnp.where(chosen, logits, 0.0)), 0.0)
    gates = exp_chosen / jnp.sum(exp_chosen, axis=0, keepdims=True)
    earlier = (iota((rows, rows), 0) < iota((rows, rows), 1)).astype(F32).astype(BF16)
    position = jnp.where(chosen, dot_nn(mask, earlier), -1.0)
    gate_high, gate_low = halves(gates)
    inverse = token_ref[1:2, :]
    inv_high = inverse.astype(BF16).astype(F32)
    inv_mid = (inverse - inv_high).astype(BF16).astype(F32)
    inv_low = inverse - inv_high - inv_mid
    slot_row = iota((8, rows), 0)
    token_part = jnp.where(
        slot_row == 0,
        token_ref[0:1, :],
        jnp.where(slot_row == 1, inv_high, jnp.where(slot_row == 2, inv_mid, jnp.where(slot_row == 3, inv_low, 0.0))),
    )
    extra = jnp.concatenate(
        [
            gate_high.astype(F32),
            gate_low.astype(F32),
            token_part,
            jnp.zeros((ROW_EXTRA - 2 * experts - 8, rows), F32),
        ],
        axis=0,
    ).astype(BF16)
    expert_row = iota((experts, rows), 0)
    slot = iota((capacity, rows), 0).astype(F32)
    picks = []
    for way in range(4):
        own = jnp.sum(jnp.where(expert_row == n[PEER_EXPERT + way], position, 0.0), axis=0, keepdims=True)
        picks.append((slot == own).astype(F32))
    picked = jnp.concatenate(picks, axis=0)
    place_ref[0] = jnp.transpose(picked).astype(BF16)
    picked = picked.astype(BF16)
    sent = dot_nn(picked, normed)
    sent_extra = contract_last(picked, extra)
    for way in range(4):
        at = slice(way * capacity, (way + 1) * capacity)
        row_refs[way][:, :width] = sent[at].astype(BF16)
        row_refs[way][:, width:] = sent_extra[at].astype(BF16)


def expert_kernel(n, r0, r1, r2, r3, gate_ref, up_ref, *refs):
    pooled_ref, hidden_ref, a_ref, b_ref, info_ref, x_ref, weight_ref = refs[-7:]
    width = gate_ref.shape[0]
    experts = 16

    @pl.when(pl.program_id(0) == 0)
    def start():
        x_ref[...] = jnp.concatenate([r[:, :width].astype(F32) for r in (r0, r1, r2, r3)], axis=0).astype(BF16)
        extra = jnp.concatenate([r[:, width:].astype(F32) for r in (r0, r1, r2, r3)], axis=0).astype(BF16)
        own = n[OWN_EXPERT]

        def mixer(source, goal):
            gates = (goal < experts) & ((source == goal) | (source == goal + experts))
            sequence = (goal == experts) & (source == 2 * experts)
            inverse = (goal == experts + 1) & (source > 2 * experts) & (source < 2 * experts + 4)
            gate = (goal == experts + 2) & ((source == own) | (source == own + experts))
            return (gates | sequence | inverse | gate).astype(F32).astype(BF16)

        square = (ROW_EXTRA, ROW_EXTRA)
        info = dot_nn(extra, mixer(iota(square, 0), iota(square, 1)))
        info_ref[0] = info
        turned = contract_last(mixer(iota(square, 1), iota(square, 0)), extra)
        sequence = turned[experts : experts + 1]
        weight = turned[experts + 1 : experts + 2] * turned[experts + 2 : experts + 3]
        pool = jnp.where(iota((pooled_ref.shape[0], extra.shape[0]), 0).astype(F32) == sequence, weight, 0.0)
        weight_ref[...] = stacked_halves(pool)

    x = x_ref[...]
    pre_gate = dot_nn(x, gate_ref[...])
    pre_up = dot_nn(x, up_ref[...])
    sigmoid = 1.0 / (1.0 + jnp.exp(-pre_gate))
    silu = pre_gate * sigmoid
    hidden = (silu * pre_up).astype(BF16)
    hidden_ref[0] = hidden
    a_ref[0] = pre_up * sigmoid * (1.0 + pre_gate * (1.0 - sigmoid))
    b_ref[0] = silu
    pooled_ref[...] = fold(dot_nn(weight_ref[...], hidden))


def embed_kernel(n, p0, p1, p2, p3, down_ref, t_ref, token_ref, _, o0, o1, o2, o3, part_ref):
    pooled = p0[...] + p1[...] + p2[...] + p3[...]
    part = fold(dot_nn(stacked_halves(pooled), down_ref[...]))
    sequences = part.shape[0]
    own = jnp.where(
        iota((sequences, t_ref.shape[1]), 0).astype(F32) == token_ref[0:1, :], token_ref[1:2, :], 0.0
    )
    part_ref[...] = part + fold(dot_nn(stacked_halves(own), t_ref[0]))
    rows = o0.shape[0]
    for way, out in enumerate((o0, o1, o2, o3)):
        out[...] = part_ref[pl.ds(pl.multiple_of(n[PEER + way] * rows, rows), rows), :]


def contrast_kernel(n, q0, q1, q2, q3, down_ref, _, loss_ref, grad_ref, hidden_grad_ref, all_ref):
    rows = q0.shape[0]
    for way, part in enumerate((q0, q1, q2, q3)):
        all_ref[pl.ds(pl.multiple_of(n[PEER + way] * rows, rows), rows), :] = part[...]
    embedded = all_ref[...]
    count = embedded.shape[0]
    pairs = count // 2
    norms = jnp.sqrt(jnp.sum(embedded * embedded, axis=1, keepdims=True) + EPSILON)
    unit = embedded / norms
    scores = (
        lax.dot_general(
            unit, unit, (((1,), (1,)), ((), ())), precision=EXACT_PRECISION, preferred_element_type=F32
        )
        / SOFTMAX_WARMTH
    )
    row, column = iota((count, count), 0), iota((count, count), 1)
    is_pair = (row % 2 == 0) & (column % 2 == 1)
    matched = is_pair & (column == row + 1)
    exp_scores = jnp.where(is_pair, jnp.exp(jnp.where(is_pair, scores, 0.0)), 0.0)
    row_total = jnp.sum(exp_scores, axis=1, keepdims=True)
    is_query = iota((count, 1), 0) % 2 == 0
    row_total = jnp.where(is_query, row_total, 1.0)
    own_score = jnp.sum(jnp.where(matched, scores, 0.0), axis=1, keepdims=True)
    terms = jnp.where(is_query, jnp.log(row_total) - own_score, 0.0)
    loss_ref[...] = jnp.broadcast_to(jnp.sum(terms, axis=0, keepdims=True) / pairs, loss_ref.shape)
    dscore = (exp_scores / row_total - jnp.where(matched, 1.0, 0.0)) * (LOSS_SCALE / pairs)
    both = dscore + jnp.transpose(dscore)
    dunit = (
        lax.dot_general(
            both, unit, (((1,), (0,)), ((), ())), precision=EXACT_PRECISION, preferred_element_type=F32
        )
        / SOFTMAX_WARMTH
    )
    radial = jnp.sum(unit * dunit, axis=1, keepdims=True)
    grad = (dunit - unit * radial) / norms
    grad_ref[...] = grad
    hidden_grad_ref[...] = fold(contract_last(stacked_halves(grad), down_ref[...]))


def backward_kernel(capacity, n, a_ref, b_ref, hidden_ref, info_ref, dh_ref, gate_ref, up_ref, router_ref, _, o0, o1, o2, o3, dgate_ref, dup_ref, dlog_ref):
    experts = 16

    @pl.when(pl.program_id(0) == 0)
    def start():
        info = info_ref[0]
        slots = info.shape[0]
        sequence = info[:, experts : experts + 1]
        weight = info[:, experts + 1 : experts + 2] * info[:, experts + 2 : experts + 3]
        member = (iota((slots, dh_ref.shape[0]), 1).astype(F32) == sequence).astype(F32).astype(BF16)
        high, low = halves(dh_ref[...])
        dhidden = weight * (dot_nn(member, high) + dot_nn(member, low))
        dgate_ref[...] = (dhidden * a_ref[0]).astype(BF16)
        dup_ref[...] = (dhidden * b_ref[0]).astype(BF16)
        moved = jnp.sum(dhidden * hidden_ref[0].astype(F32), axis=1, keepdims=True)
        lane = iota((slots, ROW_EXTRA), 1)
        gates = jnp.where(lane < experts, info, 0.0)
        dlog_ref[...] = (moved * (jnp.where(lane == n[OWN_EXPERT], 1.0, 0.0) - gates)).astype(BF16)

    total = (
        contract_last(dgate_ref[...], gate_ref[...])
        + contract_last(dup_ref[...], up_ref[...])
        + dot_nn(dlog_ref[...], router_ref[...])
    )
    for way, out in enumerate((o0, o1, o2, o3)):
        out[...] = total[way * capacity : (way + 1) * capacity].astype(BF16)


def combine_kernel(n, place_ref, r0, r1, r2, r3, _, out_ref, narrow_ref):
    rows = jnp.concatenate([r[...].astype(F32) for r in (r0, r1, r2, r3)], axis=0).astype(BF16)
    total = dot_nn(place_ref[0], rows)
    out_ref[...] = total
    narrow_ref[...] = total.astype(BF16)


def finish_kernel(n, t_ref, gain_ref, grad_ref, token_ref, own_ref, r4, r5, r6, _, out_ref):
    x = t_ref[0].astype(F32)
    scale = lax.rsqrt(jnp.mean(x * x, axis=1, keepdims=True) + EPSILON)
    sequences = grad_ref.shape[0]
    spread = jnp.where(
        iota((sequences, x.shape[0]), 0).astype(F32) == token_ref[0:1, :], 1.0, 0.0
    )
    spread = jnp.transpose(spread).astype(BF16)
    inverse = jnp.transpose(token_ref[...])[:, 1:2]
    high, low = halves(grad_ref[...])
    dresid = inverse * (dot_nn(spread, high) + dot_nn(spread, low))
    dnormed = own_ref[...] + r4[...].astype(F32) + r5[...].astype(F32) + r6[...].astype(F32)
    gained = dnormed * gain_ref[...]
    out = dresid + scale * gained - x * (scale * scale * scale) * jnp.mean(gained * x, axis=1, keepdims=True)
    out_ref[...] = out.astype(BF16)


class Chain:
    def __init__(self, numbers, first):
        self.numbers = numbers
        self.last = first

    def __call__(self, kernel, ins, outs, *, steps=1, kept=(), scratch=(), flops=0):
        args, in_specs = zip(*ins)
        args, in_specs = list(args), list(in_specs)
        shapes, out_specs = zip(*outs)
        aliases = {}
        for at, array in kept:
            aliases[1 + len(args)] = at
            args.append(array)
            in_specs.append(pl.BlockSpec(memory_space=pl.ANY))
        args.append(self.last)
        in_specs.append(pl.BlockSpec(memory_space=pl.ANY))
        result = pl.pallas_call(
            kernel,
            out_shape=list(shapes),
            grid_spec=pltpu.PrefetchScalarGridSpec(
                num_scalar_prefetch=1,
                grid=(steps,),
                in_specs=in_specs,
                out_specs=list(out_specs),
                scratch_shapes=scratch,
            ),
            input_output_aliases=aliases,
            compiler_params=pltpu.CompilerParams(vmem_limit_bytes=VMEM_LIMIT),
            cost_estimate=pl.CostEstimate(
                flops=flops, bytes_accessed=sum(x.size * x.dtype.itemsize for x in args), transcendentals=0
            ),
        )(self.numbers, *args)
        self.last = result[0]
        return result


def fixed(shape):
    return pl.BlockSpec(shape, lambda j, n: (0,) * len(shape))


def whole(array):
    return array, fixed(array.shape)


def fast_body(context, o_weight, resid, norm_gain, router, gate_weight, up_weight, down_weight, expert_ids, lengths):
    e = lax.axis_index("expert")
    z = lax.axis_index("tensor")
    rows, width = resid.shape
    heads = context.shape[1]
    experts = router.shape[1]
    top = expert_ids.shape[1]
    seq_count = lengths.shape[1]
    sequences = 4 * seq_count
    hidden_width = gate_weight.shape[2]
    capacity = max(2, rows * top * 5 // (4 * experts))
    slots = 4 * capacity
    leaf = (z == 0) | (z == 3)
    ways = e ^ jnp.arange(4, dtype=jnp.int32)
    numbers = jnp.concatenate(
        [
            jnp.stack([e * 4 + z, leaf.astype(jnp.int32), z]),
            ways,
            ways * 4 + z,
            jnp.asarray(BLOCK_ORDER, jnp.int32)[z],
        ]
    ).astype(jnp.int32)
    gate_w, up_w, down_w = gate_weight[0], up_weight[0], down_weight[0]
    gain = norm_gain.reshape(1, width)
    router_turned = router.T
    router_rows = jnp.pad(router_turned, ((0, ROW_EXTRA - experts), (0, 0)))

    def along_z(value, pairs):
        return lax.ppermute(value, "tensor", pairs)

    def swap_z(value, bits):
        return lax.ppermute(value, "tensor", [(i, i ^ bits) for i in range(4)])

    def swap_e(value, bits):
        return lax.ppermute(value, "expert", [(i, i ^ bits) for i in range(4)])

    mask_own = jnp.sum(
        (expert_ids[None, :, :] == jnp.arange(experts, dtype=jnp.int32)[:, None, None]).astype(F32), axis=2
    )
    mask_wide = jnp.concatenate([jnp.where(z == c, mask_own, 0.0) for c in range(4)], axis=1).astype(BF16)

    seq_lengths = lengths[0]
    seq_ends = jnp.cumsum(seq_lengths)
    places = jnp.arange(4 * rows, dtype=jnp.int32)
    after = places[None, :] >= seq_ends[:, None]
    seq_local = jnp.sum(after.astype(jnp.int32), axis=0)
    token_len = jnp.sum(
        jnp.where(seq_local[None, :] == jnp.arange(seq_count, dtype=jnp.int32)[:, None], seq_lengths[:, None], 0), axis=0
    )
    token_info = jnp.concatenate(
        [
            (seq_local + e * seq_count).astype(F32)[None],
            (1.0 / token_len.astype(F32))[None],
            jnp.zeros((6, 4 * rows), F32),
        ],
        axis=0,
    )

    chain = Chain(numbers, gain)
    shape = jax.ShapeDtypeStruct
    tile = 512
    pieces = []
    for c, cuts in enumerate(PIECES):
        pieces += [(c, i * (rows // cuts), rows // cuts) for i in range(cuts)]
    count = len(pieces)
    parts, half, inner, back, from_leaf, from_inner = ([None] * count for _ in range(6))
    received, pools, shared, kept_rows, kept_acts = [None] * 4, [None] * 4, {}, {}, {}

    def first_hop(i):
        c, offset, size = pieces[i]
        tall = size + (experts if c == 0 else 0)
        at = (c * rows + offset) // size
        ins = [
            (context, pl.BlockSpec((size, heads), lambda j, n: (at, 0))),
            (o_weight, pl.BlockSpec((heads, tile), lambda j, n: (0, j))),
            (resid, pl.BlockSpec((rows, tile), lambda j, n: (0, j))),
        ]
        if c == 0:
            ins.append(whole(mask_wide))
        (parts[i],) = chain(
            functools.partial(project_kernel, c, offset),
            ins,
            [(shape((tall, width), BF16), pl.BlockSpec((tall, tile), lambda j, n: (0, j)))],
            steps=width // tile,
            flops=2 * size * heads * width,
        )
        from_leaf[i] = along_z(parts[i], LEAVES_IN)

    def add(left, right):
        like = shape(right.shape, BF16)
        return chain(add_kernel, [whole(left), whole(right)], [(like, fixed(like.shape))], flops=left.size)[0]

    def second_hop(i):
        half[i] = add(parts[i], from_leaf[i])
        from_inner[i] = along_z(half[i], INNER_SWAP)

    def third_hop(i):
        inner[i] = add(half[i], from_inner[i])
        back[i] = along_z(inner[i], LEAVES_OUT)

    def dispatch(c):
        mine = [i for i in range(count) if pieces[i][0] == c]
        ins = [whole(inner[i]) for i in mine] + [whole(back[i]) for i in mine]
        ins += [
            whole(gain),
            whole(router_turned),
            (token_info, pl.BlockSpec((8, rows), lambda j, n: (0, c))),
        ]
        if c > 0:
            ins.append(whole(shared["mask"]))
        sent_shape = (capacity, width + ROW_EXTRA)
        outs = [(shape(sent_shape, BF16), fixed(sent_shape))] * 4
        for size in ((rows, width), (rows, slots)):
            outs.append((shape((4,) + size, BF16), pl.BlockSpec((1,) + size, lambda j, n: (c, 0, 0))))
        if c == 0:
            outs.append((shape((experts, 4 * rows), BF16), fixed((experts, 4 * rows))))
        result = chain(
            functools.partial(dispatch_kernel, capacity, c, len(mine)),
            ins,
            outs,
            kept=sorted(kept_rows.items()),
            flops=2 * slots * rows * width,
        )
        kept_rows.update({4: result[4], 5: result[5]})
        if c == 0:
            shared["mask"] = result[6]
        received[c] = [result[0]] + [swap_e(result[way], way) for way in (1, 2, 3)]

    def expert(c):
        tile = 256
        block = lambda size: pl.BlockSpec((1, slots, size), lambda j, n: (c, 0, j))
        outs = [(shape((sequences, hidden_width), F32), pl.BlockSpec((sequences, tile), lambda j, n: (0, j)))]
        outs += [(shape((4, slots, hidden_width), kind), block(tile)) for kind in (BF16, F32, F32)]
        outs.append((shape((4, slots, ROW_EXTRA), F32), pl.BlockSpec((1, slots, ROW_EXTRA), lambda j, n: (c, 0, 0))))
        weight_spec = pl.BlockSpec((width, tile), lambda j, n: (0, j))
        result = chain(
            expert_kernel,
            [whole(r) for r in received[c]] + [(gate_w, weight_spec), (up_w, weight_spec)],
            outs,
            steps=hidden_width // tile,
            kept=sorted(kept_acts.items()),
            scratch=[pltpu.VMEM((slots, width), BF16), pltpu.VMEM((2 * sequences, slots), BF16)],
            flops=4 * slots * width * hidden_width,
        )
        pools[c] = result[0]
        kept_acts.update({i: result[i] for i in (1, 2, 3, 4)})

    calls = {"p": first_hop, "s": second_hop, "t": third_hop, "d": dispatch, "x": expert}
    for step in FORWARD_ORDER:
        calls[step[0]](int(step[1:]))

    total_all, place_all = kept_rows[4], kept_rows[5]
    hidden_all, a_all, b_all, info_all = (kept_acts[i] for i in (1, 2, 3, 4))
    own_rows = (total_all, pl.BlockSpec((1, rows, width), lambda j, n: (n[Z], 0, 0)))
    own_tokens = (token_info, pl.BlockSpec((8, rows), lambda j, n: (0, n[Z])))
    seq_shape = shape((seq_count, width), F32)
    quarters = chain(
        embed_kernel,
        [whole(pool) for pool in pools] + [whole(down_w), own_rows, own_tokens],
        [(seq_shape, fixed(seq_shape.shape))] * 4,
        scratch=[pltpu.VMEM((sequences, width), F32)],
        flops=4 * sequences * hidden_width * width,
    )
    mine = (quarters[0] + swap_e(quarters[1], 1)) + (swap_e(quarters[2], 2) + swap_e(quarters[3], 3))
    mine = (mine + swap_z(mine, 1)) + (swap_z(mine, 2) + swap_z(mine, 3))
    gathered = [mine] + [swap_e(mine, way) for way in (1, 2, 3)]
    sizes = ((1, 128), (sequences, width), (sequences, hidden_width))
    loss, dembedded, hidden_grad = chain(
        contrast_kernel,
        [whole(piece) for piece in gathered] + [whole(down_w)],
        [(shape(size, F32), fixed(size)) for size in sizes],
        scratch=[pltpu.VMEM((sequences, width), F32)],
        flops=4 * sequences * hidden_width * width,
    )
    returned, sums = [None] * 4, [None] * 4

    def backward(k):
        block = lambda size: pl.BlockSpec((1, slots, size), lambda j, n: (n[ORDER + k], 0, 0))
        weight_spec = pl.BlockSpec((tile, hidden_width), lambda j, n: (j, 0))
        grads = chain(
            functools.partial(backward_kernel, capacity),
            [
                (a_all, block(hidden_width)),
                (b_all, block(hidden_width)),
                (hidden_all, block(hidden_width)),
                (info_all, block(ROW_EXTRA)),
                whole(hidden_grad),
                (gate_w, weight_spec),
                (up_w, weight_spec),
                (router_rows, pl.BlockSpec((ROW_EXTRA, tile), lambda j, n: (0, j))),
            ],
            [(shape((capacity, width), BF16), pl.BlockSpec((capacity, tile), lambda j, n: (0, j)))] * 4,
            steps=width // tile,
            scratch=[
                pltpu.VMEM((slots, hidden_width), BF16),
                pltpu.VMEM((slots, hidden_width), BF16),
                pltpu.VMEM((slots, ROW_EXTRA), BF16),
            ],
            flops=4 * slots * width * hidden_width,
        )
        returned[k] = [grads[0]] + [swap_e(grads[way], way) for way in (1, 2, 3)]

    def combine(k):
        sums[k] = chain(
            combine_kernel,
            [(place_all, pl.BlockSpec((1, rows, slots), lambda j, n: (n[ORDER + k], 0, 0)))]
            + [whole(r) for r in returned[k]],
            [(shape((rows, width), kind), fixed((rows, width))) for kind in (F32, BF16)],
            flops=2 * slots * rows * width,
        )

    backward(0)
    backward(1)
    backward(2)
    combine(0)
    got1 = along_z(sums[0][1], LEAVES_IN)
    backward(3)
    combine(1)
    got2 = along_z(sums[1][1], LEAVES_IN)
    got3 = along_z(add(sums[0][0], got1), INNER_SWAP)
    combine(2)
    got4 = along_z(sums[2][1], LEAVES_IN)
    combine(3)
    got5 = along_z(add(sums[2][0], got2), INNER_SWAP)
    got6 = along_z(add(sums[1][0], got3), LEAVES_OUT)
    (grad,) = chain(
        finish_kernel,
        [own_rows, whole(gain), whole(dembedded), own_tokens]
        + [whole(value) for value in (sums[3][0], got4, got5, got6)],
        [(shape((rows, width), BF16), fixed((rows, width)))],
        flops=4 * rows * sequences * width,
    )
    return loss[0, :1], grad


def solution(mesh):
    shape = dict(mesh.shape)
    part_body = fast_body if (shape["expert"], shape["tensor"]) == (4, 4) else body
    in_specs = (
        P(("groups", "expert"), "tensor"),
        P("tensor", None),
        P(("groups", "expert", "tensor"), None),
        P(),
        P(),
        P(("expert", "tensor"), None, None),
        P(("expert", "tensor"), None, None),
        P(("expert", "tensor"), None, None),
        P(("groups", "expert", "tensor"), None),
        P(("groups", "expert"), None),
    )
    out_specs = (P("groups"), P(("groups", "expert", "tensor"), None))
    return jax.shard_map(part_body, mesh=mesh, in_specs=in_specs, out_specs=out_specs, check_vma=False)
```

```python
import functools

import jax
import jax.numpy as jnp
from jax import lax
from jax.experimental import pallas as pl
from jax.experimental.pallas import tpu as pltpu
from jax.sharding import PartitionSpec as P

EPSILON = 1e-06
SOFTMAX_WARMTH = 0.05
LOSS_SCALE = 32768.0
EXACT_PRECISION = lax.Precision.HIGHEST


def slot_positions(flat_ids, expert_total):
    onehot = (flat_ids[..., None] == jnp.arange(expert_total, dtype=jnp.int32)).astype(jnp.int32)
    before = jnp.cumsum(onehot, axis=-2) - onehot
    return jnp.sum(before * onehot, axis=-1)


def contract_last(left, right):
    return lax.dot_general(
        left, right, (((1,), (1,)), ((), ())), preferred_element_type=jnp.float32
    )


def contrast(embedded):
    pair_count = embedded.shape[0] // 2
    norms = jnp.sqrt(jnp.sum(embedded * embedded, axis=1, keepdims=True) + EPSILON)
    unit_rows = embedded / norms
    query_rows = unit_rows[0::2]
    passage_rows = unit_rows[1::2]
    similarity_scores = (
        jnp.dot(query_rows, passage_rows.T, precision=EXACT_PRECISION) / SOFTMAX_WARMTH
    )
    exp_scores = jnp.exp(similarity_scores)
    row_total = jnp.sum(exp_scores, axis=1, keepdims=True)
    loss_value = jnp.mean(jnp.log(row_total[:, 0]) - jnp.diagonal(similarity_scores))
    score_gradient = (
        exp_scores / row_total - jnp.eye(pair_count, dtype=similarity_scores.dtype)
    ) * (LOSS_SCALE / pair_count)
    query_gradient = (
        jnp.dot(score_gradient, passage_rows, precision=EXACT_PRECISION) / SOFTMAX_WARMTH
    )
    passage_gradient = (
        jnp.dot(score_gradient.T, query_rows, precision=EXACT_PRECISION) / SOFTMAX_WARMTH
    )
    dunit_rows = jnp.stack([query_gradient, passage_gradient], axis=1).reshape(embedded.shape)
    radial = jnp.sum(unit_rows * dunit_rows, axis=1, keepdims=True)
    return (loss_value, (dunit_rows - unit_rows * radial) / norms)


def body(
    context,
    o_weight,
    resid,
    norm_gain,
    router,
    gate_weight,
    up_weight,
    down_weight,
    expert_ids,
    lengths,
):
    expert_count = lax.axis_size("expert")
    tensor_count = lax.axis_size("tensor")
    device_count = expert_count * tensor_count
    expert_index = lax.axis_index("expert")
    tensor_index = lax.axis_index("tensor")
    local_rows, model_width = resid.shape
    expert_total = router.shape[1]
    top_count = expert_ids.shape[1]
    seq_count = lengths.shape[1]
    seq_total = seq_count * expert_count
    capacity = max(2, local_rows * top_count * 5 // (4 * expert_total))
    attention_out = lax.psum_scatter(
        jnp.dot(context, o_weight, preferred_element_type=jnp.float32).astype(jnp.bfloat16),
        "tensor",
        scatter_dimension=0,
        tiled=True,
    ).astype(jnp.float32)
    resid_mid = resid.astype(jnp.float32) + attention_out
    rms_scale = lax.rsqrt(jnp.mean(resid_mid * resid_mid, axis=1, keepdims=True) + EPSILON)
    normed = (resid_mid * rms_scale * norm_gain).astype(jnp.bfloat16)
    logits = jnp.dot(normed, router, preferred_element_type=jnp.float32)
    expert_onehot = (expert_ids[:, :, None] == jnp.arange(expert_total, dtype=jnp.int32)).astype(
        jnp.float32
    )
    chosen = jnp.sum(logits[:, None, :] * expert_onehot, axis=2)
    exp_chosen = jnp.exp(chosen)
    gate_probs = exp_chosen / jnp.sum(exp_chosen, axis=1, keepdims=True)
    flat_ids = expert_ids.reshape(local_rows * top_count)
    target = flat_ids * capacity + slot_positions(flat_ids, expert_total)

    def move_rows(blocks):
        return lax.all_to_all(blocks, ("expert", "tensor"), split_axis=0, concat_axis=0, tiled=True)

    seq_lengths = lengths[0]
    seq_ends = jnp.cumsum(seq_lengths)
    seq_starts = seq_ends - seq_lengths
    positions = tensor_index * local_rows + jnp.arange(local_rows, dtype=jnp.int32)
    member = (
        (positions[None, :] >= seq_starts[:, None]) & (positions[None, :] < seq_ends[:, None])
    ).astype(jnp.float32)
    tok_len = jnp.sum(member * seq_lengths[:, None].astype(jnp.float32), axis=0)
    repeated = jnp.broadcast_to(normed[:, None, :], (local_rows, top_count, model_width)).reshape(
        local_rows * top_count, model_width
    )
    buffer = (
        jnp.zeros((expert_total * capacity, model_width), jnp.bfloat16).at[target].set(repeated)
    )
    received = move_rows(buffer.reshape(device_count, capacity, model_width)).reshape(
        device_count * capacity, model_width
    )
    pre_gate = jnp.dot(received, gate_weight[0], preferred_element_type=jnp.float32)
    pre_up = jnp.dot(received, up_weight[0], preferred_element_type=jnp.float32)
    hidden = (jax.nn.silu(pre_gate) * pre_up).astype(jnp.bfloat16)
    expert_rows = jnp.dot(hidden, down_weight[0], preferred_element_type=jnp.float32).astype(
        jnp.bfloat16
    )
    seq_local = jnp.dot(jnp.arange(seq_count, dtype=jnp.float32), member, precision=EXACT_PRECISION)
    seq_global = seq_local + (expert_index * seq_count).astype(jnp.float32)
    info_rows = jnp.stack(
        [
            gate_probs,
            jnp.broadcast_to(seq_global[:, None], (local_rows, top_count)),
            jnp.broadcast_to(tok_len[:, None], (local_rows, top_count)),
        ],
        axis=2,
    ).reshape(local_rows * top_count, 3)
    info_init = jnp.zeros((expert_total * capacity, 3), jnp.float32).at[:, 2].set(1.0)
    info_buffer = info_init.at[target].set(info_rows).reshape(device_count, capacity, 3)
    slot_data = lax.all_to_all(
        info_buffer, ("expert", "tensor"), split_axis=0, concat_axis=0, tiled=True
    ).reshape(device_count * capacity, 3)
    slot_gate = slot_data[:, 0:1]
    slot_seq = slot_data[:, 1].astype(jnp.int32)
    slot_len = slot_data[:, 2:3]
    slot_onehot = (slot_seq[:, None] == jnp.arange(seq_total, dtype=jnp.int32)).astype(jnp.float32)
    out_float = expert_rows.astype(jnp.float32)
    expert_part = lax.dot_general(
        slot_onehot,
        slot_gate * out_float / slot_len,
        (((0,), (0,)), ((), ())),
        precision=EXACT_PRECISION,
        preferred_element_type=jnp.float32,
    )
    partial_value = jnp.dot(member, resid_mid / tok_len[:, None], precision=EXACT_PRECISION)
    placed = lax.dynamic_update_slice_in_dim(
        expert_part,
        lax.dynamic_slice_in_dim(expert_part, expert_index * seq_count, seq_count, 0)
        + partial_value,
        expert_index * seq_count,
        0,
    )
    embedded = lax.psum(placed, ("expert", "tensor"))
    loss_value, dembedded = contrast(embedded)
    own_rows = lax.dynamic_slice_in_dim(
        dembedded, expert_index * seq_count, seq_count, 0
    ) / seq_lengths[:, None].astype(jnp.float32)
    dresid_out = lax.dot_general(
        member,
        own_rows,
        (((0,), (0,)), ((), ())),
        precision=EXACT_PRECISION,
        preferred_element_type=jnp.float32,
    )
    slot_dresid = jnp.dot(slot_onehot, dembedded, precision=EXACT_PRECISION) / slot_len
    received_grad = (slot_gate * slot_dresid).astype(jnp.bfloat16)
    slot_dgate = jnp.sum(slot_dresid * out_float, axis=1)
    returned = lax.all_to_all(
        slot_dgate.reshape(device_count, capacity),
        ("expert", "tensor"),
        split_axis=0,
        concat_axis=0,
        tiled=True,
    )
    dgate_prob = returned.reshape(expert_total * capacity)[target].reshape(local_rows, top_count)
    dhidden = contract_last(received_grad, down_weight[0])
    gate_sigmoid = jax.nn.sigmoid(pre_gate)
    dpre_gate = (dhidden * pre_up * gate_sigmoid * (1.0 + pre_gate * (1.0 - gate_sigmoid))).astype(
        jnp.bfloat16
    )
    dpre_up = (dhidden * jax.nn.silu(pre_gate)).astype(jnp.bfloat16)
    dx_rows = (
        contract_last(dpre_gate, gate_weight[0]) + contract_last(dpre_up, up_weight[0])
    ).astype(jnp.bfloat16)
    dx_moe = jnp.sum(
        move_rows(dx_rows.reshape(device_count, capacity, model_width))
        .reshape(expert_total * capacity, model_width)[target]
        .astype(jnp.float32)
        .reshape(local_rows, top_count, model_width),
        axis=1,
    )
    dchosen = gate_probs * (dgate_prob - jnp.sum(gate_probs * dgate_prob, axis=1, keepdims=True))
    dlogits = jnp.sum(dchosen[:, :, None] * expert_onehot, axis=1).astype(jnp.bfloat16)
    dnormed = dx_moe + contract_last(dlogits, router)
    gain_grad = dnormed * norm_gain
    grad_resid = (
        dresid_out
        + rms_scale * gain_grad
        - resid_mid * rms_scale**3 * jnp.mean(gain_grad * resid_mid, axis=1, keepdims=True)
    )
    return (loss_value.reshape(1), grad_resid.astype(jnp.bfloat16))


ROW_EXTRA = 128
LEAVES_IN = ((0, 1), (3, 2))
INNER_SWAP = ((1, 2), (2, 1))
LEAVES_OUT = ((1, 0), (2, 3))
PIECES = (1, 1, 1, 1)
FORWARD_ORDER = (
    "p0", "p1", "p2", "s0", "p3", "s1", "t0", "s2", "t1", "s3", "d0", "t2", "d1", "t3", "x0", "d2", "x1", "d3", "x2", "x3",
)
BACKWARD_ORDER = (
    "b0", "b1", "c0", "b2", "c1", "b3", "c2", "i0", "c3", "i1", "l0",
)
VMEM_LIMIT = 24 * 2**20
BLOCK_ORDER = ((3, 2, 1, 0), (3, 0, 2, 1), (0, 3, 1, 2), (0, 1, 2, 3))
OWN_EXPERT, LEAF, Z, PEER, PEER_EXPERT, ORDER = 0, 1, 2, 3, 7, 11
BF16 = jnp.bfloat16
F32 = jnp.float32


def dot_nn(left, right):
    return lax.dot_general(left, right, (((1,), (0,)), ((), ())), preferred_element_type=F32)


def halves(value):
    high = value.astype(BF16)
    return high, (value - high.astype(F32)).astype(BF16)


def stacked_halves(value):
    high, low = halves(value)
    return jnp.concatenate([high.astype(F32), low.astype(F32)], axis=0).astype(BF16)


def fold(product):
    rows = product.shape[0] // 2
    return product[:rows] + product[rows:]


def iota(shape, axis):
    return lax.broadcasted_iota(jnp.int32, shape, axis)


def project_kernel(block, offset, n, context_ref, weight_ref, resid_ref, *rest):
    out_ref = rest[-1]
    rows = context_ref.shape[0]
    part = dot_nn(context_ref[...], weight_ref[...])
    share = jnp.where(n[Z] == block, resid_ref[offset : offset + rows, :].astype(F32), 0.0)
    out_ref[:rows, :] = (part + share).astype(BF16)
    if block == 0:
        mask = rest[0][...]
        out_ref[rows:, :] = jnp.zeros((mask.shape[0], out_ref.shape[1]), BF16)
        out_ref[rows:, : mask.shape[1]] = mask


def add_kernel(n, left_ref, right_ref, _, out_ref):
    out_ref[...] = (left_ref[...].astype(F32) + right_ref[...].astype(F32)).astype(BF16)


def dispatch_kernel(capacity, block, pieces, n, *refs):
    inner_refs, back_refs, refs = refs[:pieces], refs[pieces : 2 * pieces], refs[2 * pieces :]
    gain_ref, router_ref, token_ref, *refs = refs
    rows = token_ref.shape[1]
    outs = refs[-7:] if block == 0 else refs[-6:]
    row_refs, t_ref, place_ref = outs[:4], outs[4], outs[5]
    experts, width = router_ref.shape
    x = jnp.concatenate(
        [
            jnp.where(n[LEAF] == 1, back[...].astype(F32), inner[...].astype(F32))
            for inner, back in zip(inner_refs, back_refs)
        ],
        axis=0,
    )
    if block == 0:
        wide = x[rows:, : 4 * rows].astype(BF16)
        outs[6][...] = wide
        x = x[:rows]
    else:
        wide = refs[0][...]
    mask = wide[:, block * rows : (block + 1) * rows]
    t_ref[0] = x.astype(BF16)
    scale = lax.rsqrt(jnp.mean(x * x, axis=1, keepdims=True) + EPSILON)
    normed = (x * scale * gain_ref[...]).astype(BF16)
    logits = contract_last(router_ref[...], normed)
    chosen = mask.astype(F32) > 0.5
    exp_chosen = jnp.where(chosen, jnp.exp(jnp.where(chosen, logits, 0.0)), 0.0)
    gates = exp_chosen / jnp.sum(exp_chosen, axis=0, keepdims=True)
    earlier = (iota((rows, rows), 0) < iota((rows, rows), 1)).astype(F32).astype(BF16)
    position = jnp.where(chosen, dot_nn(mask, earlier), -1.0)
    gate_high, gate_low = halves(gates)
    inverse = token_ref[1:2, :]
    inv_high = inverse.astype(BF16).astype(F32)
    inv_mid = (inverse - inv_high).astype(BF16).astype(F32)
    inv_low = inverse - inv_high - inv_mid
    slot_row = iota((8, rows), 0)
    token_part = jnp.where(
        slot_row == 0,
        token_ref[0:1, :],
        jnp.where(slot_row == 1, inv_high, jnp.where(slot_row == 2, inv_mid, jnp.where(slot_row == 3, inv_low, 0.0))),
    )
    extra = jnp.concatenate(
        [
            gate_high.astype(F32),
            gate_low.astype(F32),
            token_part,
            jnp.zeros((ROW_EXTRA - 2 * experts - 8, rows), F32),
        ],
        axis=0,
    ).astype(BF16)
    expert_row = iota((experts, rows), 0)
    slot = iota((capacity, rows), 0).astype(F32)
    picks = []
    for way in range(4):
        own = jnp.sum(jnp.where(expert_row == n[PEER_EXPERT + way], position, 0.0), axis=0, keepdims=True)
        picks.append((slot == own).astype(F32))
    picked = jnp.concatenate(picks, axis=0)
    place_ref[0] = jnp.transpose(picked).astype(BF16)
    picked = picked.astype(BF16)
    sent = dot_nn(picked, normed)
    sent_extra = contract_last(picked, extra)
    for way in range(4):
        at = slice(way * capacity, (way + 1) * capacity)
        row_refs[way][:, :width] = sent[at].astype(BF16)
        row_refs[way][:, width:] = sent_extra[at].astype(BF16)


def expert_kernel(n, r0, r1, r2, r3, gate_ref, up_ref, *refs):
    pooled_ref, hidden_ref, a_ref, b_ref, info_ref, x_ref, weight_ref = refs[-7:]
    width = gate_ref.shape[0]
    experts = 16

    @pl.when(pl.program_id(0) == 0)
    def start():
        x_ref[...] = jnp.concatenate([r[:, :width].astype(F32) for r in (r0, r1, r2, r3)], axis=0).astype(BF16)
        extra = jnp.concatenate([r[:, width:].astype(F32) for r in (r0, r1, r2, r3)], axis=0).astype(BF16)
        own = n[OWN_EXPERT]

        def mixer(source, goal):
            gates = (goal < experts) & ((source == goal) | (source == goal + experts))
            sequence = (goal == experts) & (source == 2 * experts)
            inverse = (goal == experts + 1) & (source > 2 * experts) & (source < 2 * experts + 4)
            gate = (goal == experts + 2) & ((source == own) | (source == own + experts))
            return (gates | sequence | inverse | gate).astype(F32).astype(BF16)

        square = (ROW_EXTRA, ROW_EXTRA)
        info = dot_nn(extra, mixer(iota(square, 0), iota(square, 1)))
        info_ref[0] = info
        turned = contract_last(mixer(iota(square, 1), iota(square, 0)), extra)
        sequence = turned[experts : experts + 1]
        weight = turned[experts + 1 : experts + 2] * turned[experts + 2 : experts + 3]
        pool = jnp.where(iota((pooled_ref.shape[0], extra.shape[0]), 0).astype(F32) == sequence, weight, 0.0)
        weight_ref[...] = stacked_halves(pool)

    x = x_ref[...]
    pre_gate = dot_nn(x, gate_ref[...])
    pre_up = dot_nn(x, up_ref[...])
    sigmoid = 1.0 / (1.0 + jnp.exp(-pre_gate))
    silu = pre_gate * sigmoid
    hidden = (silu * pre_up).astype(BF16)
    hidden_ref[0] = hidden
    a_ref[0] = pre_up * sigmoid * (1.0 + pre_gate * (1.0 - sigmoid))
    b_ref[0] = silu
    pooled_ref[...] = fold(dot_nn(weight_ref[...], hidden))


def sum_kernel(n, p0, p1, p2, p3, _, out_ref):
    near = p0[...].astype(F32) + p1[...].astype(F32)
    out_ref[...] = (near + (p2[...].astype(F32) + p3[...].astype(F32))).astype(BF16)


def embed_kernel(n, p0, p1, p2, p3, down_ref, t_ref, token_ref, _, o0, o1, o2, o3, part_ref):
    pooled = p0[...] + p1[...] + p2[...] + p3[...]
    part = fold(dot_nn(stacked_halves(pooled), down_ref[...]))
    sequences = part.shape[0]
    own = jnp.where(
        iota((sequences, t_ref.shape[1]), 0).astype(F32) == token_ref[0:1, :], token_ref[1:2, :], 0.0
    )
    part_ref[...] = part + fold(dot_nn(stacked_halves(own), t_ref[0]))
    rows = o0.shape[0]
    for way, out in enumerate((o0, o1, o2, o3)):
        out[...] = part_ref[pl.ds(pl.multiple_of(n[PEER + way] * rows, rows), rows), :].astype(out.dtype)


def contrast_kernel(n, q0, q1, q2, q3, down_ref, _, loss_ref, grad_ref, hidden_grad_ref, all_ref):
    rows = q0.shape[0]
    for way, part in enumerate((q0, q1, q2, q3)):
        all_ref[pl.ds(pl.multiple_of(n[PEER + way] * rows, rows), rows), :] = part[...].astype(F32)
    embedded = all_ref[...]
    count = embedded.shape[0]
    pairs = count // 2
    norms = jnp.sqrt(jnp.sum(embedded * embedded, axis=1, keepdims=True) + EPSILON)
    unit = embedded / norms
    scores = (
        lax.dot_general(
            unit, unit, (((1,), (1,)), ((), ())), precision=EXACT_PRECISION, preferred_element_type=F32
        )
        / SOFTMAX_WARMTH
    )
    row, column = iota((count, count), 0), iota((count, count), 1)
    is_pair = (row % 2 == 0) & (column % 2 == 1)
    matched = is_pair & (column == row + 1)
    exp_scores = jnp.where(is_pair, jnp.exp(jnp.where(is_pair, scores, 0.0)), 0.0)
    row_total = jnp.sum(exp_scores, axis=1, keepdims=True)
    is_query = iota((count, 1), 0) % 2 == 0
    row_total = jnp.where(is_query, row_total, 1.0)
    own_score = jnp.sum(jnp.where(matched, scores, 0.0), axis=1, keepdims=True)
    terms = jnp.where(is_query, jnp.log(row_total) - own_score, 0.0)
    loss_ref[...] = jnp.broadcast_to(jnp.sum(terms, axis=0, keepdims=True) / pairs, loss_ref.shape)
    dscore = (exp_scores / row_total - jnp.where(matched, 1.0, 0.0)) * (LOSS_SCALE / pairs)
    both = dscore + jnp.transpose(dscore)
    dunit = (
        lax.dot_general(
            both, unit, (((1,), (0,)), ((), ())), precision=EXACT_PRECISION, preferred_element_type=F32
        )
        / SOFTMAX_WARMTH
    )
    radial = jnp.sum(unit * dunit, axis=1, keepdims=True)
    grad = (dunit - unit * radial) / norms
    grad_ref[...] = grad
    hidden_grad_ref[...] = fold(contract_last(stacked_halves(grad), down_ref[...]))


def backward_kernel(capacity, n, a_ref, b_ref, hidden_ref, info_ref, dh_ref, gate_ref, up_ref, router_ref, _, o0, o1, o2, o3, dgate_ref, dup_ref, dlog_ref):
    experts = 16

    @pl.when(pl.program_id(0) == 0)
    def start():
        info = info_ref[0]
        slots = info.shape[0]
        sequence = info[:, experts : experts + 1]
        weight = info[:, experts + 1 : experts + 2] * info[:, experts + 2 : experts + 3]
        member = (iota((slots, dh_ref.shape[0]), 1).astype(F32) == sequence).astype(F32).astype(BF16)
        high, low = halves(dh_ref[...])
        dhidden = weight * (dot_nn(member, high) + dot_nn(member, low))
        dgate_ref[...] = (dhidden * a_ref[0]).astype(BF16)
        dup_ref[...] = (dhidden * b_ref[0]).astype(BF16)
        moved = jnp.sum(dhidden * hidden_ref[0].astype(F32), axis=1, keepdims=True)
        lane = iota((slots, ROW_EXTRA), 1)
        gates = jnp.where(lane < experts, info, 0.0)
        dlog_ref[...] = (moved * (jnp.where(lane == n[OWN_EXPERT], 1.0, 0.0) - gates)).astype(BF16)

    total = (
        contract_last(dgate_ref[...], gate_ref[...])
        + contract_last(dup_ref[...], up_ref[...])
        + dot_nn(dlog_ref[...], router_ref[...])
    )
    for way, out in enumerate((o0, o1, o2, o3)):
        out[...] = total[way * capacity : (way + 1) * capacity].astype(BF16)


def combine_kernel(n, place_ref, r0, r1, r2, r3, _, out_ref, narrow_ref):
    rows = jnp.concatenate([r[...].astype(F32) for r in (r0, r1, r2, r3)], axis=0).astype(BF16)
    total = dot_nn(place_ref[0], rows)
    out_ref[...] = total
    narrow_ref[...] = total.astype(BF16)


def finish_kernel(n, t_ref, gain_ref, grad_ref, token_ref, own_ref, r4, r5, r6, _, out_ref):
    x = t_ref[0].astype(F32)
    scale = lax.rsqrt(jnp.mean(x * x, axis=1, keepdims=True) + EPSILON)
    sequences = grad_ref.shape[0]
    spread = jnp.where(
        iota((sequences, x.shape[0]), 0).astype(F32) == token_ref[0:1, :], 1.0, 0.0
    )
    spread = jnp.transpose(spread).astype(BF16)
    inverse = jnp.transpose(token_ref[...])[:, 1:2]
    high, low = halves(grad_ref[...])
    dresid = inverse * (dot_nn(spread, high) + dot_nn(spread, low))
    dnormed = own_ref[...] + r4[...].astype(F32) + r5[...].astype(F32) + r6[...].astype(F32)
    gained = dnormed * gain_ref[...]
    out = dresid + scale * gained - x * (scale * scale * scale) * jnp.mean(gained * x, axis=1, keepdims=True)
    out_ref[...] = out.astype(BF16)


class Chain:
    def __init__(self, numbers, first):
        self.numbers = numbers
        self.last = first

    def __call__(self, kernel, ins, outs, *, steps=1, kept=(), scratch=(), flops=0):
        args, in_specs = zip(*ins)
        args, in_specs = list(args), list(in_specs)
        shapes, out_specs = zip(*outs)
        aliases = {}
        for at, array in kept:
            aliases[1 + len(args)] = at
            args.append(array)
            in_specs.append(pl.BlockSpec(memory_space=pl.ANY))
        args.append(self.last)
        in_specs.append(pl.BlockSpec(memory_space=pl.ANY))
        result = pl.pallas_call(
            kernel,
            out_shape=list(shapes),
            grid_spec=pltpu.PrefetchScalarGridSpec(
                num_scalar_prefetch=1,
                grid=(steps,),
                in_specs=in_specs,
                out_specs=list(out_specs),
                scratch_shapes=scratch,
            ),
            input_output_aliases=aliases,
            compiler_params=pltpu.CompilerParams(vmem_limit_bytes=VMEM_LIMIT),
            cost_estimate=pl.CostEstimate(flops=1, bytes_accessed=1, transcendentals=0),
        )(self.numbers, *args)
        self.last = result[0]
        return result


def fixed(shape):
    return pl.BlockSpec(shape, lambda j, n: (0,) * len(shape))


def whole(array):
    return array, pl.BlockSpec(memory_space=pltpu.VMEM)


def fast_body(context, o_weight, resid, norm_gain, router, gate_weight, up_weight, down_weight, expert_ids, lengths):
    e = lax.axis_index("expert")
    z = lax.axis_index("tensor")
    rows, width = resid.shape
    heads = context.shape[1]
    experts = router.shape[1]
    top = expert_ids.shape[1]
    seq_count = lengths.shape[1]
    sequences = 4 * seq_count
    hidden_width = gate_weight.shape[2]
    capacity = max(2, rows * top * 5 // (4 * experts))
    slots = 4 * capacity
    leaf = (z == 0) | (z == 3)
    ways = e ^ jnp.arange(4, dtype=jnp.int32)
    numbers = jnp.concatenate(
        [
            jnp.stack([e * 4 + z, leaf.astype(jnp.int32), z]),
            ways,
            ways * 4 + z,
            jnp.asarray(BLOCK_ORDER, jnp.int32)[z],
        ]
    ).astype(jnp.int32)
    gate_w, up_w, down_w = gate_weight[0], up_weight[0], down_weight[0]
    gain = norm_gain.reshape(1, width)
    router_turned = router.T
    router_rows = jnp.pad(router_turned, ((0, ROW_EXTRA - experts), (0, 0)))

    def along_z(value, pairs):
        return lax.ppermute(value, "tensor", pairs)

    def swap_z(value, bits):
        return lax.ppermute(value, "tensor", [(i, i ^ bits) for i in range(4)])

    def swap_e(value, bits):
        return lax.ppermute(value, "expert", [(i, i ^ bits) for i in range(4)])

    mask_own = jnp.sum(
        (expert_ids[None, :, :] == jnp.arange(experts, dtype=jnp.int32)[:, None, None]).astype(F32), axis=2
    )
    mask_wide = jnp.concatenate([jnp.where(z == c, mask_own, 0.0) for c in range(4)], axis=1).astype(BF16)

    seq_lengths = lengths[0]
    seq_ends = jnp.cumsum(seq_lengths)
    places = jnp.arange(4 * rows, dtype=jnp.int32)
    after = places[None, :] >= seq_ends[:, None]
    seq_local = jnp.sum(after.astype(jnp.int32), axis=0)
    token_len = jnp.sum(
        jnp.where(seq_local[None, :] == jnp.arange(seq_count, dtype=jnp.int32)[:, None], seq_lengths[:, None], 0), axis=0
    )
    token_info = jnp.concatenate(
        [
            (seq_local + e * seq_count).astype(F32)[None],
            (1.0 / token_len.astype(F32))[None],
            jnp.zeros((6, 4 * rows), F32),
        ],
        axis=0,
    )

    chain = Chain(numbers, gain)
    shape = jax.ShapeDtypeStruct
    tile = 512
    pieces = []
    for c, cuts in enumerate(PIECES):
        pieces += [(c, i * (rows // cuts), rows // cuts) for i in range(cuts)]
    count = len(pieces)
    parts, half, inner, back, from_leaf, from_inner = ([None] * count for _ in range(6))
    received, pools, shared, kept_rows, kept_acts = [None] * 4, [None] * 4, {}, {}, {}

    def first_hop(i):
        c, offset, size = pieces[i]
        tall = size + (experts if c == 0 else 0)
        at = (c * rows + offset) // size
        ins = [
            (context, pl.BlockSpec((size, heads), lambda j, n: (at, 0))),
            whole(o_weight),
            whole(resid),
        ]
        if c == 0:
            ins.append(whole(mask_wide))
        (parts[i],) = chain(
            functools.partial(project_kernel, c, offset),
            ins,
            [(shape((tall, width), BF16), fixed((tall, width)))],
            flops=2 * size * heads * width,
        )
        from_leaf[i] = along_z(parts[i], LEAVES_IN)

    def add(left, right):
        like = shape(right.shape, BF16)
        return chain(add_kernel, [whole(left), whole(right)], [(like, fixed(like.shape))], flops=left.size)[0]

    def second_hop(i):
        half[i] = add(parts[i], from_leaf[i])
        from_inner[i] = along_z(half[i], INNER_SWAP)

    def third_hop(i):
        inner[i] = add(half[i], from_inner[i])
        back[i] = along_z(inner[i], LEAVES_OUT)

    def dispatch(c):
        mine = [i for i in range(count) if pieces[i][0] == c]
        ins = [whole(inner[i]) for i in mine] + [whole(back[i]) for i in mine]
        ins += [
            whole(gain),
            whole(router_turned),
            (token_info, pl.BlockSpec((8, rows), lambda j, n: (0, c))),
        ]
        if c > 0:
            ins.append(whole(shared["mask"]))
        sent_shape = (capacity, width + ROW_EXTRA)
        outs = [(shape(sent_shape, BF16), fixed(sent_shape))] * 4
        for size in ((rows, width), (rows, slots)):
            outs.append((shape((4,) + size, BF16), pl.BlockSpec((1,) + size, lambda j, n: (c, 0, 0))))
        if c == 0:
            outs.append((shape((experts, 4 * rows), BF16), fixed((experts, 4 * rows))))
        result = chain(
            functools.partial(dispatch_kernel, capacity, c, len(mine)),
            ins,
            outs,
            kept=sorted(kept_rows.items()),
            flops=2 * slots * rows * width,
        )
        kept_rows.update({4: result[4], 5: result[5]})
        if c == 0:
            shared["mask"] = result[6]
        received[c] = [result[0]] + [swap_e(result[way], way) for way in (1, 2, 3)]

    def expert(c):
        tile = hidden_width
        block = lambda size: pl.BlockSpec((1, slots, size), lambda j, n: (c, 0, j))
        outs = [(shape((sequences, hidden_width), F32), pl.BlockSpec((sequences, tile), lambda j, n: (0, j)))]
        outs += [(shape((4, slots, hidden_width), kind), block(tile)) for kind in (BF16, F32, F32)]
        outs.append((shape((4, slots, ROW_EXTRA), F32), pl.BlockSpec((1, slots, ROW_EXTRA), lambda j, n: (c, 0, 0))))
        weight_spec = pl.BlockSpec(memory_space=pltpu.VMEM)
        result = chain(
            expert_kernel,
            [whole(r) for r in received[c]] + [(gate_w, weight_spec), (up_w, weight_spec)],
            outs,
            steps=hidden_width // tile,
            kept=sorted(kept_acts.items()),
            scratch=[pltpu.VMEM((slots, width), BF16), pltpu.VMEM((2 * sequences, slots), BF16)],
            flops=4 * slots * width * hidden_width,
        )
        pools[c] = result[0]
        kept_acts.update({i: result[i] for i in (1, 2, 3, 4)})

    calls = {"p": first_hop, "s": second_hop, "t": third_hop, "d": dispatch, "x": expert}
    for step in FORWARD_ORDER:
        calls[step[0]](int(step[1:]))

    total_all, place_all = kept_rows[4], kept_rows[5]
    hidden_all, a_all, b_all, info_all = (kept_acts[i] for i in (1, 2, 3, 4))
    own_rows = (total_all, pl.BlockSpec((1, rows, width), lambda j, n: (n[Z], 0, 0)))
    own_tokens = (token_info, pl.BlockSpec((8, rows), lambda j, n: (0, n[Z])))
    seq_size = (seq_count, width)
    quarters = chain(
        embed_kernel,
        [whole(pool) for pool in pools] + [whole(down_w), own_rows, own_tokens],
        [(shape(seq_size, kind), fixed(seq_size)) for kind in (F32, BF16, BF16, BF16)],
        scratch=[pltpu.VMEM((sequences, width), F32)],
        flops=4 * sequences * hidden_width * width,
    )

    def add_four(values):
        return chain(sum_kernel, [whole(v) for v in values], [(shape(seq_size, BF16), fixed(seq_size))])[0]

    mine = add_four([quarters[0]] + [swap_e(quarters[way], way) for way in (1, 2, 3)])
    mine = add_four([mine] + [swap_z(mine, way) for way in (1, 2, 3)])
    gathered = [mine] + [swap_e(mine, way) for way in (1, 2, 3)]
    sizes = ((1, 128), (sequences, width), (sequences, hidden_width))
    loss, dembedded, hidden_grad = chain(
        contrast_kernel,
        [whole(piece) for piece in gathered] + [whole(down_w)],
        [(shape(size, F32), fixed(size)) for size in sizes],
        scratch=[pltpu.VMEM((sequences, width), F32)],
        flops=4 * sequences * hidden_width * width,
    )
    returned, sums = [None] * 4, [None] * 4

    def backward(k):
        tile = width
        block = lambda size: pl.BlockSpec((1, slots, size), lambda j, n: (n[ORDER + k], 0, 0))
        weight_spec = pl.BlockSpec(memory_space=pltpu.VMEM)
        grads = chain(
            functools.partial(backward_kernel, capacity),
            [
                (a_all, block(hidden_width)),
                (b_all, block(hidden_width)),
                (hidden_all, block(hidden_width)),
                (info_all, block(ROW_EXTRA)),
                whole(hidden_grad),
                (gate_w, weight_spec),
                (up_w, weight_spec),
                (router_rows, pl.BlockSpec((ROW_EXTRA, tile), lambda j, n: (0, j))),
            ],
            [(shape((capacity, width), BF16), pl.BlockSpec((capacity, tile), lambda j, n: (0, j)))] * 4,
            steps=width // tile,
            scratch=[
                pltpu.VMEM((slots, hidden_width), BF16),
                pltpu.VMEM((slots, hidden_width), BF16),
                pltpu.VMEM((slots, ROW_EXTRA), BF16),
            ],
            flops=4 * slots * width * hidden_width,
        )
        returned[k] = [grads[0]] + [swap_e(grads[way], way) for way in (1, 2, 3)]

    def combine(k):
        sums[k] = chain(
            combine_kernel,
            [(place_all, pl.BlockSpec((1, rows, slots), lambda j, n: (n[ORDER + k], 0, 0)))]
            + [whole(r) for r in returned[k]],
            [(shape((rows, width), kind), fixed((rows, width))) for kind in (F32, BF16)],
            flops=2 * slots * rows * width,
        )

    hops = {}

    def combined(k):
        combine(k)
        if k < 3:
            hops[k] = along_z(sums[k][1], LEAVES_IN)

    def inner_hop(k):
        total = add(sums[(0, 2)[k]][0], hops[(0, 1)[k]])
        hops[3 + k] = along_z(total, INNER_SWAP)

    def last_hop(_):
        hops[5] = along_z(add(sums[1][0], hops[3]), LEAVES_OUT)

    calls = {"b": backward, "c": combined, "i": inner_hop, "l": last_hop}
    for step in BACKWARD_ORDER:
        calls[step[0]](int(step[1:]))
    (grad,) = chain(
        finish_kernel,
        [own_rows, whole(gain), whole(dembedded), own_tokens]
        + [whole(value) for value in (sums[3][0], hops[2], hops[4], hops[5])],
        [(shape((rows, width), BF16), fixed((rows, width)))],
        flops=4 * rows * sequences * width,
    )
    return loss[0, :1], grad


def solution(mesh):
    shape = dict(mesh.shape)
    part_body = fast_body if (shape["expert"], shape["tensor"]) == (4, 4) else body
    in_specs = (
        P(("groups", "expert"), "tensor"),
        P("tensor", None),
        P(("groups", "expert", "tensor"), None),
        P(),
        P(),
        P(("expert", "tensor"), None, None),
        P(("expert", "tensor"), None, None),
        P(("expert", "tensor"), None, None),
        P(("groups", "expert", "tensor"), None),
        P(("groups", "expert"), None),
    )
    out_specs = (P("groups"), P(("groups", "expert", "tensor"), None))
    return jax.shard_map(part_body, mesh=mesh, in_specs=in_specs, out_specs=out_specs, check_vma=False)
```

```python
import functools

import jax
import jax.numpy as jnp
from jax import lax
from jax.experimental import pallas as pl
from jax.experimental.pallas import tpu as pltpu
from jax.sharding import PartitionSpec as P

EPSILON = 1e-06
SOFTMAX_WARMTH = 0.05
LOSS_SCALE = 32768.0
EXACT_PRECISION = lax.Precision.HIGHEST


def slot_positions(flat_ids, expert_total):
    onehot = (flat_ids[..., None] == jnp.arange(expert_total, dtype=jnp.int32)).astype(jnp.int32)
    before = jnp.cumsum(onehot, axis=-2) - onehot
    return jnp.sum(before * onehot, axis=-1)


def contract_last(left, right):
    return lax.dot_general(
        left, right, (((1,), (1,)), ((), ())), preferred_element_type=jnp.float32
    )


def contrast(embedded):
    pair_count = embedded.shape[0] // 2
    norms = jnp.sqrt(jnp.sum(embedded * embedded, axis=1, keepdims=True) + EPSILON)
    unit_rows = embedded / norms
    query_rows = unit_rows[0::2]
    passage_rows = unit_rows[1::2]
    similarity_scores = (
        jnp.dot(query_rows, passage_rows.T, precision=EXACT_PRECISION) / SOFTMAX_WARMTH
    )
    exp_scores = jnp.exp(similarity_scores)
    row_total = jnp.sum(exp_scores, axis=1, keepdims=True)
    loss_value = jnp.mean(jnp.log(row_total[:, 0]) - jnp.diagonal(similarity_scores))
    score_gradient = (
        exp_scores / row_total - jnp.eye(pair_count, dtype=similarity_scores.dtype)
    ) * (LOSS_SCALE / pair_count)
    query_gradient = (
        jnp.dot(score_gradient, passage_rows, precision=EXACT_PRECISION) / SOFTMAX_WARMTH
    )
    passage_gradient = (
        jnp.dot(score_gradient.T, query_rows, precision=EXACT_PRECISION) / SOFTMAX_WARMTH
    )
    dunit_rows = jnp.stack([query_gradient, passage_gradient], axis=1).reshape(embedded.shape)
    radial = jnp.sum(unit_rows * dunit_rows, axis=1, keepdims=True)
    return (loss_value, (dunit_rows - unit_rows * radial) / norms)


def body(
    context,
    o_weight,
    resid,
    norm_gain,
    router,
    gate_weight,
    up_weight,
    down_weight,
    expert_ids,
    lengths,
):
    expert_count = lax.axis_size("expert")
    tensor_count = lax.axis_size("tensor")
    device_count = expert_count * tensor_count
    expert_index = lax.axis_index("expert")
    tensor_index = lax.axis_index("tensor")
    local_rows, model_width = resid.shape
    expert_total = router.shape[1]
    top_count = expert_ids.shape[1]
    seq_count = lengths.shape[1]
    seq_total = seq_count * expert_count
    capacity = max(2, local_rows * top_count * 5 // (4 * expert_total))
    attention_out = lax.psum_scatter(
        jnp.dot(context, o_weight, preferred_element_type=jnp.float32).astype(jnp.bfloat16),
        "tensor",
        scatter_dimension=0,
        tiled=True,
    ).astype(jnp.float32)
    resid_mid = resid.astype(jnp.float32) + attention_out
    rms_scale = lax.rsqrt(jnp.mean(resid_mid * resid_mid, axis=1, keepdims=True) + EPSILON)
    normed = (resid_mid * rms_scale * norm_gain).astype(jnp.bfloat16)
    logits = jnp.dot(normed, router, preferred_element_type=jnp.float32)
    expert_onehot = (expert_ids[:, :, None] == jnp.arange(expert_total, dtype=jnp.int32)).astype(
        jnp.float32
    )
    chosen = jnp.sum(logits[:, None, :] * expert_onehot, axis=2)
    exp_chosen = jnp.exp(chosen)
    gate_probs = exp_chosen / jnp.sum(exp_chosen, axis=1, keepdims=True)
    flat_ids = expert_ids.reshape(local_rows * top_count)
    target = flat_ids * capacity + slot_positions(flat_ids, expert_total)

    def move_rows(blocks):
        return lax.all_to_all(blocks, ("expert", "tensor"), split_axis=0, concat_axis=0, tiled=True)

    seq_lengths = lengths[0]
    seq_ends = jnp.cumsum(seq_lengths)
    seq_starts = seq_ends - seq_lengths
    positions = tensor_index * local_rows + jnp.arange(local_rows, dtype=jnp.int32)
    member = (
        (positions[None, :] >= seq_starts[:, None]) & (positions[None, :] < seq_ends[:, None])
    ).astype(jnp.float32)
    tok_len = jnp.sum(member * seq_lengths[:, None].astype(jnp.float32), axis=0)
    repeated = jnp.broadcast_to(normed[:, None, :], (local_rows, top_count, model_width)).reshape(
        local_rows * top_count, model_width
    )
    buffer = (
        jnp.zeros((expert_total * capacity, model_width), jnp.bfloat16).at[target].set(repeated)
    )
    received = move_rows(buffer.reshape(device_count, capacity, model_width)).reshape(
        device_count * capacity, model_width
    )
    pre_gate = jnp.dot(received, gate_weight[0], preferred_element_type=jnp.float32)
    pre_up = jnp.dot(received, up_weight[0], preferred_element_type=jnp.float32)
    hidden = (jax.nn.silu(pre_gate) * pre_up).astype(jnp.bfloat16)
    expert_rows = jnp.dot(hidden, down_weight[0], preferred_element_type=jnp.float32).astype(
        jnp.bfloat16
    )
    seq_local = jnp.dot(jnp.arange(seq_count, dtype=jnp.float32), member, precision=EXACT_PRECISION)
    seq_global = seq_local + (expert_index * seq_count).astype(jnp.float32)
    info_rows = jnp.stack(
        [
            gate_probs,
            jnp.broadcast_to(seq_global[:, None], (local_rows, top_count)),
            jnp.broadcast_to(tok_len[:, None], (local_rows, top_count)),
        ],
        axis=2,
    ).reshape(local_rows * top_count, 3)
    info_init = jnp.zeros((expert_total * capacity, 3), jnp.float32).at[:, 2].set(1.0)
    info_buffer = info_init.at[target].set(info_rows).reshape(device_count, capacity, 3)
    slot_data = lax.all_to_all(
        info_buffer, ("expert", "tensor"), split_axis=0, concat_axis=0, tiled=True
    ).reshape(device_count * capacity, 3)
    slot_gate = slot_data[:, 0:1]
    slot_seq = slot_data[:, 1].astype(jnp.int32)
    slot_len = slot_data[:, 2:3]
    slot_onehot = (slot_seq[:, None] == jnp.arange(seq_total, dtype=jnp.int32)).astype(jnp.float32)
    out_float = expert_rows.astype(jnp.float32)
    expert_part = lax.dot_general(
        slot_onehot,
        slot_gate * out_float / slot_len,
        (((0,), (0,)), ((), ())),
        precision=EXACT_PRECISION,
        preferred_element_type=jnp.float32,
    )
    partial_value = jnp.dot(member, resid_mid / tok_len[:, None], precision=EXACT_PRECISION)
    placed = lax.dynamic_update_slice_in_dim(
        expert_part,
        lax.dynamic_slice_in_dim(expert_part, expert_index * seq_count, seq_count, 0)
        + partial_value,
        expert_index * seq_count,
        0,
    )
    embedded = lax.psum(placed, ("expert", "tensor"))
    loss_value, dembedded = contrast(embedded)
    own_rows = lax.dynamic_slice_in_dim(
        dembedded, expert_index * seq_count, seq_count, 0
    ) / seq_lengths[:, None].astype(jnp.float32)
    dresid_out = lax.dot_general(
        member,
        own_rows,
        (((0,), (0,)), ((), ())),
        precision=EXACT_PRECISION,
        preferred_element_type=jnp.float32,
    )
    slot_dresid = jnp.dot(slot_onehot, dembedded, precision=EXACT_PRECISION) / slot_len
    received_grad = (slot_gate * slot_dresid).astype(jnp.bfloat16)
    slot_dgate = jnp.sum(slot_dresid * out_float, axis=1)
    returned = lax.all_to_all(
        slot_dgate.reshape(device_count, capacity),
        ("expert", "tensor"),
        split_axis=0,
        concat_axis=0,
        tiled=True,
    )
    dgate_prob = returned.reshape(expert_total * capacity)[target].reshape(local_rows, top_count)
    dhidden = contract_last(received_grad, down_weight[0])
    gate_sigmoid = jax.nn.sigmoid(pre_gate)
    dpre_gate = (dhidden * pre_up * gate_sigmoid * (1.0 + pre_gate * (1.0 - gate_sigmoid))).astype(
        jnp.bfloat16
    )
    dpre_up = (dhidden * jax.nn.silu(pre_gate)).astype(jnp.bfloat16)
    dx_rows = (
        contract_last(dpre_gate, gate_weight[0]) + contract_last(dpre_up, up_weight[0])
    ).astype(jnp.bfloat16)
    dx_moe = jnp.sum(
        move_rows(dx_rows.reshape(device_count, capacity, model_width))
        .reshape(expert_total * capacity, model_width)[target]
        .astype(jnp.float32)
        .reshape(local_rows, top_count, model_width),
        axis=1,
    )
    dchosen = gate_probs * (dgate_prob - jnp.sum(gate_probs * dgate_prob, axis=1, keepdims=True))
    dlogits = jnp.sum(dchosen[:, :, None] * expert_onehot, axis=1).astype(jnp.bfloat16)
    dnormed = dx_moe + contract_last(dlogits, router)
    gain_grad = dnormed * norm_gain
    grad_resid = (
        dresid_out
        + rms_scale * gain_grad
        - resid_mid * rms_scale**3 * jnp.mean(gain_grad * resid_mid, axis=1, keepdims=True)
    )
    return (loss_value.reshape(1), grad_resid.astype(jnp.bfloat16))


ROW_EXTRA = 128
LEAVES_IN = ((0, 1), (3, 2))
INNER_SWAP = ((1, 2), (2, 1))
LEAVES_OUT = ((1, 0), (2, 3))
PIECES = (1, 1, 1, 1)
FORWARD_ORDER = (
    "p0", "p1", "p2", "p3", "s0", "s1", "t0", "s2", "t1", "s3", "d0", "t2", "d1", "x0", "t3", "d2", "x1", "d3", "x2", "x3",
)
BACKWARD_ORDER = (
    "b0", "b1", "c0", "b2", "c1", "b3", "c2", "i0", "c3", "i1", "l0",
)
VMEM_LIMIT = 24 * 2**20
FIRST_LIMIT = 54 * 2**20
FIRST_CUTS = 8
BLOCK_ORDER = ((3, 2, 1, 0), (3, 0, 2, 1), (0, 3, 1, 2), (0, 1, 2, 3))
OWN_EXPERT, LEAF, Z, PEER, PEER_EXPERT, ORDER = 0, 1, 2, 3, 7, 11
BF16 = jnp.bfloat16
F32 = jnp.float32


def dot_nn(left, right):
    return lax.dot_general(left, right, (((1,), (0,)), ((), ())), preferred_element_type=F32)


def halves(value):
    high = value.astype(BF16)
    return high, (value - high.astype(F32)).astype(BF16)


def stacked_halves(value):
    high, low = halves(value)
    return jnp.concatenate([high.astype(F32), low.astype(F32)], axis=0).astype(BF16)


def fold(product):
    rows = product.shape[0] // 2
    return product[:rows] + product[rows:]


def iota(shape, axis):
    return lax.broadcasted_iota(jnp.int32, shape, axis)


def project_kernel(block, offset, n, context_ref, weight_ref, resid_ref, *rest):
    out_ref = rest[-1]
    rows = context_ref.shape[0]
    part = dot_nn(context_ref[...], weight_ref[...])
    share = jnp.where(n[Z] == block, resid_ref[offset : offset + rows, :].astype(F32), 0.0)
    out_ref[:rows, :] = (part + share).astype(BF16)


def first_kernel(experts, ids_ref, context_hbm, weight_hbm, resid_hbm, out_ref, context_ref, weight_ref, resid_ref, sems):
    rows, heads = context_ref.shape
    cuts = sems.shape[0] - 2
    step = heads // cuts
    copies = []
    for i in range(cuts):
        at = pl.ds(i * step, step)
        copies.append(pltpu.make_async_copy(weight_hbm.at[at], weight_ref.at[at], sems.at[i]))
    context_copy = pltpu.make_async_copy(context_hbm.at[pl.ds(0, rows)], context_ref, sems.at[cuts])
    resid_copy = pltpu.make_async_copy(resid_hbm.at[pl.ds(0, rows)], resid_ref, sems.at[cuts + 1])
    context_copy.start()
    for copy in copies:
        copy.start()
    resid_copy.start()
    z = lax.axis_index("tensor")
    mask = jnp.zeros((experts, rows), F32)
    for k in range(ids_ref.shape[0]):
        mask += (ids_ref[k : k + 1, :] == iota((experts, rows), 0)).astype(F32)
    out_ref[rows:, :] = jnp.zeros((experts, out_ref.shape[1]), BF16)
    for block in range(4):
        out_ref[rows:, block * rows : (block + 1) * rows] = jnp.where(z == block, mask, 0.0).astype(BF16)
    context_copy.wait()
    part = None
    for i, copy in enumerate(copies):
        copy.wait()
        at = slice(i * step, (i + 1) * step)
        term = dot_nn(context_ref[:, at], weight_ref[at, :])
        part = term if part is None else part + term
    resid_copy.wait()
    share = jnp.where(z == 0, resid_ref[...].astype(F32), 0.0)
    out_ref[:rows, :] = (part + share).astype(BF16)


def add_kernel(n, left_ref, right_ref, _, out_ref):
    out_ref[...] = (left_ref[...].astype(F32) + right_ref[...].astype(F32)).astype(BF16)


def dispatch_kernel(capacity, block, pieces, n, *refs):
    inner_refs, back_refs, refs = refs[:pieces], refs[pieces : 2 * pieces], refs[2 * pieces :]
    gain_ref, router_ref, token_ref, *refs = refs
    rows = token_ref.shape[1]
    outs = refs[-7:] if block == 0 else refs[-6:]
    row_refs, t_ref, place_ref = outs[:4], outs[4], outs[5]
    experts, width = router_ref.shape
    x = jnp.concatenate(
        [
            jnp.where(n[LEAF] == 1, back[...].astype(F32), inner[...].astype(F32))
            for inner, back in zip(inner_refs, back_refs)
        ],
        axis=0,
    )
    if block == 0:
        wide = x[rows:, : 4 * rows].astype(BF16)
        outs[6][...] = wide
        x = x[:rows]
    else:
        wide = refs[0][...]
    mask = wide[:, block * rows : (block + 1) * rows]
    t_ref[0] = x.astype(BF16)
    scale = lax.rsqrt(jnp.mean(x * x, axis=1, keepdims=True) + EPSILON)
    normed = (x * scale * gain_ref[...]).astype(BF16)
    logits = contract_last(router_ref[...], normed)
    chosen = mask.astype(F32) > 0.5
    exp_chosen = jnp.where(chosen, jnp.exp(jnp.where(chosen, logits, 0.0)), 0.0)
    gates = exp_chosen / jnp.sum(exp_chosen, axis=0, keepdims=True)
    earlier = (iota((rows, rows), 0) < iota((rows, rows), 1)).astype(F32).astype(BF16)
    position = jnp.where(chosen, dot_nn(mask, earlier), -1.0)
    gate_high, gate_low = halves(gates)
    inverse = token_ref[1:2, :]
    inv_high = inverse.astype(BF16).astype(F32)
    inv_mid = (inverse - inv_high).astype(BF16).astype(F32)
    inv_low = inverse - inv_high - inv_mid
    slot_row = iota((8, rows), 0)
    token_part = jnp.where(
        slot_row == 0,
        token_ref[0:1, :],
        jnp.where(slot_row == 1, inv_high, jnp.where(slot_row == 2, inv_mid, jnp.where(slot_row == 3, inv_low, 0.0))),
    )
    extra = jnp.concatenate(
        [
            gate_high.astype(F32),
            gate_low.astype(F32),
            token_part,
            jnp.zeros((ROW_EXTRA - 2 * experts - 8, rows), F32),
        ],
        axis=0,
    ).astype(BF16)
    expert_row = iota((experts, rows), 0)
    slot = iota((capacity, rows), 0).astype(F32)
    picks = []
    for way in range(4):
        own = jnp.sum(jnp.where(expert_row == n[PEER_EXPERT + way], position, 0.0), axis=0, keepdims=True)
        picks.append((slot == own).astype(F32))
    picked = jnp.concatenate(picks, axis=0)
    place_ref[0] = jnp.transpose(picked).astype(BF16)
    picked = picked.astype(BF16)
    sent = dot_nn(picked, normed)
    sent_extra = contract_last(picked, extra)
    for way in range(4):
        at = slice(way * capacity, (way + 1) * capacity)
        row_refs[way][:, :width] = sent[at].astype(BF16)
        row_refs[way][:, width:] = sent_extra[at].astype(BF16)


def expert_kernel(n, r0, r1, r2, r3, gate_ref, up_ref, *refs):
    pooled_ref, hidden_ref, a_ref, b_ref, info_ref, x_ref, weight_ref = refs[-7:]
    width = gate_ref.shape[0]
    experts = 16

    @pl.when(pl.program_id(0) == 0)
    def start():
        x_ref[...] = jnp.concatenate([r[:, :width].astype(F32) for r in (r0, r1, r2, r3)], axis=0).astype(BF16)
        extra = jnp.concatenate([r[:, width:].astype(F32) for r in (r0, r1, r2, r3)], axis=0).astype(BF16)
        own = n[OWN_EXPERT]

        def mixer(source, goal):
            gates = (goal < experts) & ((source == goal) | (source == goal + experts))
            sequence = (goal == experts) & (source == 2 * experts)
            inverse = (goal == experts + 1) & (source > 2 * experts) & (source < 2 * experts + 4)
            gate = (goal == experts + 2) & ((source == own) | (source == own + experts))
            return (gates | sequence | inverse | gate).astype(F32).astype(BF16)

        square = (ROW_EXTRA, ROW_EXTRA)
        info = dot_nn(extra, mixer(iota(square, 0), iota(square, 1)))
        info_ref[0] = info
        turned = contract_last(mixer(iota(square, 1), iota(square, 0)), extra)
        sequence = turned[experts : experts + 1]
        weight = turned[experts + 1 : experts + 2] * turned[experts + 2 : experts + 3]
        pool = jnp.where(iota((pooled_ref.shape[0], extra.shape[0]), 0).astype(F32) == sequence, weight, 0.0)
        weight_ref[...] = stacked_halves(pool)

    x = x_ref[...]
    pre_gate = dot_nn(x, gate_ref[...])
    pre_up = dot_nn(x, up_ref[...])
    sigmoid = 1.0 / (1.0 + jnp.exp(-pre_gate))
    silu = pre_gate * sigmoid
    hidden = (silu * pre_up).astype(BF16)
    hidden_ref[0] = hidden
    a_ref[0] = pre_up * sigmoid * (1.0 + pre_gate * (1.0 - sigmoid))
    b_ref[0] = silu
    pooled_ref[...] = fold(dot_nn(weight_ref[...], hidden))


def sum_kernel(n, p0, p1, p2, p3, _, out_ref):
    near = p0[...].astype(F32) + p1[...].astype(F32)
    out_ref[...] = (near + (p2[...].astype(F32) + p3[...].astype(F32))).astype(BF16)


def embed_kernel(n, p0, p1, p2, p3, down_ref, t_ref, token_ref, _, o0, o1, o2, o3, part_ref):
    pooled = p0[...] + p1[...] + p2[...] + p3[...]
    part = fold(dot_nn(stacked_halves(pooled), down_ref[...]))
    sequences = part.shape[0]
    own = jnp.where(
        iota((sequences, t_ref.shape[1]), 0).astype(F32) == token_ref[0:1, :], token_ref[1:2, :], 0.0
    )
    part_ref[...] = part + fold(dot_nn(stacked_halves(own), t_ref[0]))
    rows = o0.shape[0]
    for way, out in enumerate((o0, o1, o2, o3)):
        out[...] = part_ref[pl.ds(pl.multiple_of(n[PEER + way] * rows, rows), rows), :].astype(out.dtype)


def contrast_kernel(n, q0, q1, q2, q3, down_ref, _, grad_ref, hidden_grad_ref, loss_ref, all_ref):
    rows = q0.shape[0]
    for way, part in enumerate((q0, q1, q2, q3)):
        all_ref[pl.ds(pl.multiple_of(n[PEER + way] * rows, rows), rows), :] = part[...].astype(F32)
    embedded = all_ref[...]
    count = embedded.shape[0]
    pairs = count // 2
    norms = jnp.sqrt(jnp.sum(embedded * embedded, axis=1, keepdims=True) + EPSILON)
    unit = embedded / norms
    scores = (
        lax.dot_general(
            unit, unit, (((1,), (1,)), ((), ())), precision=EXACT_PRECISION, preferred_element_type=F32
        )
        / SOFTMAX_WARMTH
    )
    row, column = iota((count, count), 0), iota((count, count), 1)
    is_pair = (row % 2 == 0) & (column % 2 == 1)
    matched = is_pair & (column == row + 1)
    exp_scores = jnp.where(is_pair, jnp.exp(jnp.where(is_pair, scores, 0.0)), 0.0)
    row_total = jnp.sum(exp_scores, axis=1, keepdims=True)
    is_query = iota((count, 1), 0) % 2 == 0
    row_total = jnp.where(is_query, row_total, 1.0)
    own_score = jnp.sum(jnp.where(matched, scores, 0.0), axis=1, keepdims=True)
    terms = jnp.where(is_query, jnp.log(row_total) - own_score, 0.0)
    loss_ref[0] = jnp.sum(terms) / pairs
    dscore = (exp_scores / row_total - jnp.where(matched, 1.0, 0.0)) * (LOSS_SCALE / pairs)
    both = dscore + jnp.transpose(dscore)
    dunit = (
        lax.dot_general(
            both, unit, (((1,), (0,)), ((), ())), precision=EXACT_PRECISION, preferred_element_type=F32
        )
        / SOFTMAX_WARMTH
    )
    radial = jnp.sum(unit * dunit, axis=1, keepdims=True)
    grad = (dunit - unit * radial) / norms
    grad_ref[...] = grad
    hidden_grad_ref[...] = fold(contract_last(stacked_halves(grad), down_ref[...]))


def backward_kernel(capacity, n, a_ref, b_ref, hidden_ref, info_ref, dh_ref, gate_ref, up_ref, router_ref, _, o0, o1, o2, o3, dgate_ref, dup_ref, dlog_ref):
    experts = 16

    @pl.when(pl.program_id(0) == 0)
    def start():
        info = info_ref[0]
        slots = info.shape[0]
        sequence = info[:, experts : experts + 1]
        weight = info[:, experts + 1 : experts + 2] * info[:, experts + 2 : experts + 3]
        member = (iota((slots, dh_ref.shape[0]), 1).astype(F32) == sequence).astype(F32).astype(BF16)
        high, low = halves(dh_ref[...])
        dhidden = weight * (dot_nn(member, high) + dot_nn(member, low))
        dgate_ref[...] = (dhidden * a_ref[0]).astype(BF16)
        dup_ref[...] = (dhidden * b_ref[0]).astype(BF16)
        moved = jnp.sum(dhidden * hidden_ref[0].astype(F32), axis=1, keepdims=True)
        lane = iota((slots, ROW_EXTRA), 1)
        gates = jnp.where(lane < experts, info, 0.0)
        dlog_ref[...] = (moved * (jnp.where(lane == n[OWN_EXPERT], 1.0, 0.0) - gates)).astype(BF16)

    total = (
        contract_last(dgate_ref[...], gate_ref[...])
        + contract_last(dup_ref[...], up_ref[...])
        + dot_nn(dlog_ref[...], router_ref[...])
    )
    for way, out in enumerate((o0, o1, o2, o3)):
        out[...] = total[way * capacity : (way + 1) * capacity].astype(BF16)


def combine_kernel(n, place_ref, r0, r1, r2, r3, _, out_ref, narrow_ref):
    rows = jnp.concatenate([r[...].astype(F32) for r in (r0, r1, r2, r3)], axis=0).astype(BF16)
    total = dot_nn(place_ref[0], rows)
    out_ref[...] = total
    narrow_ref[...] = total.astype(BF16)


def spread_kernel(n, t_ref, grad_ref, token_ref, _, out_ref, scale_ref):
    x = t_ref[0].astype(F32)
    scale = lax.rsqrt(jnp.mean(x * x, axis=1, keepdims=True) + EPSILON)
    spread = jnp.where(iota((grad_ref.shape[0], x.shape[0]), 0).astype(F32) == token_ref[0:1, :], 1.0, 0.0)
    spread = jnp.transpose(spread).astype(BF16)
    inverse = jnp.transpose(token_ref[...])[:, 1:2]
    high, low = halves(grad_ref[...])
    out_ref[...] = inverse * (dot_nn(spread, high) + dot_nn(spread, low))
    scale_ref[...] = jnp.broadcast_to(scale, scale_ref.shape)


def finish_kernel(n, t_ref, gain_ref, dresid_ref, scale_ref, own_ref, r4, r5, r6, _, out_ref):
    x = t_ref[0].astype(F32)
    scale = scale_ref[:, :1]
    dnormed = own_ref[...] + r4[...].astype(F32) + r5[...].astype(F32) + r6[...].astype(F32)
    gained = dnormed * gain_ref[...]
    pull = (scale * scale * scale) * jnp.mean(gained * x, axis=1, keepdims=True)
    out_ref[...] = (dresid_ref[...] + scale * gained - x * pull).astype(BF16)


class Chain:
    def __init__(self, numbers, first):
        self.numbers = numbers
        self.last = first

    def __call__(self, kernel, ins, outs, *, steps=1, kept=(), scratch=(), flops=0):
        args, in_specs = zip(*ins)
        args, in_specs = list(args), list(in_specs)
        shapes, out_specs = zip(*outs)
        aliases = {}
        for at, array in kept:
            aliases[1 + len(args)] = at
            args.append(array)
            in_specs.append(pl.BlockSpec(memory_space=pl.ANY))
        args.append(self.last)
        in_specs.append(pl.BlockSpec(memory_space=pl.ANY))
        result = pl.pallas_call(
            kernel,
            out_shape=list(shapes),
            grid_spec=pltpu.PrefetchScalarGridSpec(
                num_scalar_prefetch=1,
                grid=(steps,),
                in_specs=in_specs,
                out_specs=list(out_specs),
                scratch_shapes=scratch,
            ),
            input_output_aliases=aliases,
            compiler_params=pltpu.CompilerParams(vmem_limit_bytes=VMEM_LIMIT),
            cost_estimate=pl.CostEstimate(flops=1, bytes_accessed=1, transcendentals=0),
        )(self.numbers, *args)
        self.last = result[0]
        return result


def fixed(shape):
    return pl.BlockSpec(shape, lambda j, n: (0,) * len(shape))


def whole(array):
    return array, pl.BlockSpec(memory_space=pltpu.VMEM)


def fast_body(context, o_weight, resid, norm_gain, router, gate_weight, up_weight, down_weight, expert_ids, lengths):
    e = lax.axis_index("expert")
    z = lax.axis_index("tensor")
    rows, width = resid.shape
    heads = context.shape[1]
    experts = router.shape[1]
    top = expert_ids.shape[1]
    seq_count = lengths.shape[1]
    sequences = 4 * seq_count
    hidden_width = gate_weight.shape[2]
    capacity = max(2, rows * top * 5 // (4 * experts))
    slots = 4 * capacity
    leaf = (z == 0) | (z == 3)
    ways = e ^ jnp.arange(4, dtype=jnp.int32)
    numbers = jnp.concatenate(
        [
            jnp.stack([e * 4 + z, leaf.astype(jnp.int32), z]),
            ways,
            ways * 4 + z,
            jnp.asarray(BLOCK_ORDER, jnp.int32)[z],
        ]
    ).astype(jnp.int32)
    gate_w, up_w, down_w = gate_weight[0], up_weight[0], down_weight[0]
    gain = norm_gain.reshape(1, width)
    router_turned = router.T
    router_rows = jnp.pad(router_turned, ((0, ROW_EXTRA - experts), (0, 0)))

    def along_z(value, pairs):
        return lax.ppermute(value, "tensor", pairs)

    def swap_z(value, bits):
        return lax.ppermute(value, "tensor", [(i, i ^ bits) for i in range(4)])

    def swap_e(value, bits):
        return lax.ppermute(value, "expert", [(i, i ^ bits) for i in range(4)])

    seq_lengths = lengths[0]
    seq_ends = jnp.cumsum(seq_lengths)
    places = jnp.arange(4 * rows, dtype=jnp.int32)
    after = places[None, :] >= seq_ends[:, None]
    seq_local = jnp.sum(after.astype(jnp.int32), axis=0)
    token_len = jnp.sum(
        jnp.where(seq_local[None, :] == jnp.arange(seq_count, dtype=jnp.int32)[:, None], seq_lengths[:, None], 0), axis=0
    )
    token_info = jnp.concatenate(
        [
            (seq_local + e * seq_count).astype(F32)[None],
            (1.0 / token_len.astype(F32))[None],
            jnp.zeros((6, 4 * rows), F32),
        ],
        axis=0,
    )

    chain = Chain(numbers, gain)
    shape = jax.ShapeDtypeStruct
    tile = 512
    pieces = []
    for c, cuts in enumerate(PIECES):
        pieces += [(c, i * (rows // cuts), rows // cuts) for i in range(cuts)]
    count = len(pieces)
    parts, half, inner, back, from_leaf, from_inner = ([None] * count for _ in range(6))
    received, pools, shared, kept_rows, kept_acts = [None] * 4, [None] * 4, {}, {}, {}

    def first_hop(i):
        c, offset, size = pieces[i]
        if i == 0:
            away = pl.BlockSpec(memory_space=pl.ANY)
            near = pl.BlockSpec(memory_space=pltpu.VMEM)
            chain.last = parts[0] = pl.pallas_call(
                functools.partial(first_kernel, experts),
                out_shape=shape((size + experts, width), BF16),
                in_specs=[near, away, away, away],
                out_specs=near,
                scratch_shapes=[
                    pltpu.VMEM((size, heads), BF16),
                    pltpu.VMEM((heads, width), BF16),
                    pltpu.VMEM((size, width), BF16),
                    pltpu.SemaphoreType.DMA((FIRST_CUTS + 2,)),
                ],
                compiler_params=pltpu.CompilerParams(vmem_limit_bytes=FIRST_LIMIT),
            )(expert_ids.T, context, o_weight, resid)
            from_leaf[0] = along_z(parts[0], LEAVES_IN)
            return
        at = (c * rows + offset) // size
        ins = [
            (context, pl.BlockSpec((size, heads), lambda j, n: (at, 0))),
            whole(o_weight),
            whole(resid),
        ]
        (parts[i],) = chain(
            functools.partial(project_kernel, c, offset),
            ins,
            [(shape((size, width), BF16), fixed((size, width)))],
            flops=2 * size * heads * width,
        )
        from_leaf[i] = along_z(parts[i], LEAVES_IN)

    def add(left, right):
        like = shape(right.shape, BF16)
        return chain(add_kernel, [whole(left), whole(right)], [(like, fixed(like.shape))], flops=left.size)[0]

    def second_hop(i):
        half[i] = add(parts[i], from_leaf[i])
        from_inner[i] = along_z(half[i], INNER_SWAP)

    def third_hop(i):
        inner[i] = add(half[i], from_inner[i])
        back[i] = along_z(inner[i], LEAVES_OUT)

    def dispatch(c):
        mine = [i for i in range(count) if pieces[i][0] == c]
        ins = [whole(inner[i]) for i in mine] + [whole(back[i]) for i in mine]
        ins += [
            whole(gain),
            whole(router_turned),
            (token_info, pl.BlockSpec((8, rows), lambda j, n: (0, c))),
        ]
        if c > 0:
            ins.append(whole(shared["mask"]))
        sent_shape = (capacity, width + ROW_EXTRA)
        outs = [(shape(sent_shape, BF16), fixed(sent_shape))] * 4
        for size in ((rows, width), (rows, slots)):
            outs.append((shape((4,) + size, BF16), pl.BlockSpec((1,) + size, lambda j, n: (c, 0, 0))))
        if c == 0:
            outs.append((shape((experts, 4 * rows), BF16), fixed((experts, 4 * rows))))
        result = chain(
            functools.partial(dispatch_kernel, capacity, c, len(mine)),
            ins,
            outs,
            kept=sorted(kept_rows.items()),
            flops=2 * slots * rows * width,
        )
        kept_rows.update({4: result[4], 5: result[5]})
        if c == 0:
            shared["mask"] = result[6]
        received[c] = [result[0]] + [swap_e(result[way], way) for way in (1, 2, 3)]

    def expert(c):
        tile = hidden_width
        block = lambda size: pl.BlockSpec((1, slots, size), lambda j, n: (c, 0, j))
        outs = [(shape((sequences, hidden_width), F32), pl.BlockSpec((sequences, tile), lambda j, n: (0, j)))]
        outs += [(shape((4, slots, hidden_width), kind), block(tile)) for kind in (BF16, F32, F32)]
        outs.append((shape((4, slots, ROW_EXTRA), F32), pl.BlockSpec((1, slots, ROW_EXTRA), lambda j, n: (c, 0, 0))))
        weight_spec = pl.BlockSpec(memory_space=pltpu.VMEM)
        result = chain(
            expert_kernel,
            [whole(r) for r in received[c]] + [(gate_w, weight_spec), (up_w, weight_spec)],
            outs,
            steps=hidden_width // tile,
            kept=sorted(kept_acts.items()),
            scratch=[pltpu.VMEM((slots, width), BF16), pltpu.VMEM((2 * sequences, slots), BF16)],
            flops=4 * slots * width * hidden_width,
        )
        pools[c] = result[0]
        kept_acts.update({i: result[i] for i in (1, 2, 3, 4)})

    calls = {"p": first_hop, "s": second_hop, "t": third_hop, "d": dispatch, "x": expert}
    for step in FORWARD_ORDER:
        calls[step[0]](int(step[1:]))

    total_all, place_all = kept_rows[4], kept_rows[5]
    hidden_all, a_all, b_all, info_all = (kept_acts[i] for i in (1, 2, 3, 4))
    own_rows = (total_all, pl.BlockSpec((1, rows, width), lambda j, n: (n[Z], 0, 0)))
    own_tokens = (token_info, pl.BlockSpec((8, rows), lambda j, n: (0, n[Z])))
    seq_size = (seq_count, width)
    quarters = chain(
        embed_kernel,
        [whole(pool) for pool in pools] + [whole(down_w), own_rows, own_tokens],
        [(shape(seq_size, kind), fixed(seq_size)) for kind in (F32, BF16, BF16, BF16)],
        scratch=[pltpu.VMEM((sequences, width), F32)],
        flops=4 * sequences * hidden_width * width,
    )

    def add_four(values):
        return chain(sum_kernel, [whole(v) for v in values], [(shape(seq_size, BF16), fixed(seq_size))])[0]

    mine = add_four([quarters[0]] + [swap_e(quarters[way], way) for way in (1, 2, 3)])
    mine = add_four([mine] + [swap_z(mine, way) for way in (1, 2, 3)])
    gathered = [mine] + [swap_e(mine, way) for way in (1, 2, 3)]
    sizes = ((sequences, width), (sequences, hidden_width))
    dembedded, hidden_grad, loss = chain(
        contrast_kernel,
        [whole(piece) for piece in gathered] + [whole(down_w)],
        [(shape(size, F32), fixed(size)) for size in sizes]
        + [(shape((1,), F32), pl.BlockSpec(memory_space=pltpu.SMEM))],
        scratch=[pltpu.VMEM((sequences, width), F32)],
        flops=4 * sequences * hidden_width * width,
    )
    returned, sums = [None] * 4, [None] * 4

    def backward(k):
        tile = width
        block = lambda size: pl.BlockSpec((1, slots, size), lambda j, n: (n[ORDER + k], 0, 0))
        weight_spec = pl.BlockSpec(memory_space=pltpu.VMEM)
        grads = chain(
            functools.partial(backward_kernel, capacity),
            [
                (a_all, block(hidden_width)),
                (b_all, block(hidden_width)),
                (hidden_all, block(hidden_width)),
                (info_all, block(ROW_EXTRA)),
                whole(hidden_grad),
                (gate_w, weight_spec),
                (up_w, weight_spec),
                (router_rows, pl.BlockSpec((ROW_EXTRA, tile), lambda j, n: (0, j))),
            ],
            [(shape((capacity, width), BF16), pl.BlockSpec((capacity, tile), lambda j, n: (0, j)))] * 4,
            steps=width // tile,
            scratch=[
                pltpu.VMEM((slots, hidden_width), BF16),
                pltpu.VMEM((slots, hidden_width), BF16),
                pltpu.VMEM((slots, ROW_EXTRA), BF16),
            ],
            flops=4 * slots * width * hidden_width,
        )
        returned[k] = [grads[0]] + [swap_e(grads[way], way) for way in (1, 2, 3)]

    def combine(k):
        sums[k] = chain(
            combine_kernel,
            [(place_all, pl.BlockSpec((1, rows, slots), lambda j, n: (n[ORDER + k], 0, 0)))]
            + [whole(r) for r in returned[k]],
            [(shape((rows, width), kind), fixed((rows, width))) for kind in (F32, BF16)],
            flops=2 * slots * rows * width,
        )

    hops = {}

    def combined(k):
        combine(k)
        if k < 3:
            hops[k] = along_z(sums[k][1], LEAVES_IN)

    def inner_hop(k):
        total = add(sums[(0, 2)[k]][0], hops[(0, 1)[k]])
        hops[3 + k] = along_z(total, INNER_SWAP)

    def last_hop(_):
        hops[5] = along_z(add(sums[1][0], hops[3]), LEAVES_OUT)

    calls = {"b": backward, "c": combined, "i": inner_hop, "l": last_hop}
    for step in BACKWARD_ORDER:
        calls[step[0]](int(step[1:]))
    dresid, scales = chain(
        spread_kernel,
        [own_rows, whole(dembedded), own_tokens],
        [(shape((rows, width), F32), fixed((rows, width))), (shape((rows, 128), F32), fixed((rows, 128)))],
    )
    (grad,) = chain(
        finish_kernel,
        [own_rows, whole(gain), whole(dresid), whole(scales)]
        + [whole(value) for value in (sums[3][0], hops[2], hops[4], hops[5])],
        [(shape((rows, width), BF16), fixed((rows, width)))],
        flops=4 * rows * sequences * width,
    )
    return loss, grad


def solution(mesh):
    shape = dict(mesh.shape)
    part_body = fast_body if (shape["expert"], shape["tensor"]) == (4, 4) else body
    in_specs = (
        P(("groups", "expert"), "tensor"),
        P("tensor", None),
        P(("groups", "expert", "tensor"), None),
        P(),
        P(),
        P(("expert", "tensor"), None, None),
        P(("expert", "tensor"), None, None),
        P(("expert", "tensor"), None, None),
        P(("groups", "expert", "tensor"), None),
        P(("groups", "expert"), None),
    )
    out_specs = (P("groups"), P(("groups", "expert", "tensor"), None))
    return jax.shard_map(part_body, mesh=mesh, in_specs=in_specs, out_specs=out_specs, check_vma=False)
```

```python
import functools

import jax
import jax.numpy as jnp
from jax import lax
from jax.experimental import pallas as pl
from jax.experimental.pallas import tpu as pltpu
from jax.sharding import PartitionSpec as P

EPSILON = 1e-06
SOFTMAX_WARMTH = 0.05
LOSS_SCALE = 32768.0
EXACT_PRECISION = lax.Precision.HIGHEST


def slot_positions(flat_ids, expert_total):
    onehot = (flat_ids[..., None] == jnp.arange(expert_total, dtype=jnp.int32)).astype(jnp.int32)
    before = jnp.cumsum(onehot, axis=-2) - onehot
    return jnp.sum(before * onehot, axis=-1)


def contract_last(left, right):
    return lax.dot_general(
        left, right, (((1,), (1,)), ((), ())), preferred_element_type=jnp.float32
    )


def contrast(embedded):
    pair_count = embedded.shape[0] // 2
    norms = jnp.sqrt(jnp.sum(embedded * embedded, axis=1, keepdims=True) + EPSILON)
    unit_rows = embedded / norms
    query_rows = unit_rows[0::2]
    passage_rows = unit_rows[1::2]
    similarity_scores = (
        jnp.dot(query_rows, passage_rows.T, precision=EXACT_PRECISION) / SOFTMAX_WARMTH
    )
    exp_scores = jnp.exp(similarity_scores)
    row_total = jnp.sum(exp_scores, axis=1, keepdims=True)
    loss_value = jnp.mean(jnp.log(row_total[:, 0]) - jnp.diagonal(similarity_scores))
    score_gradient = (
        exp_scores / row_total - jnp.eye(pair_count, dtype=similarity_scores.dtype)
    ) * (LOSS_SCALE / pair_count)
    query_gradient = (
        jnp.dot(score_gradient, passage_rows, precision=EXACT_PRECISION) / SOFTMAX_WARMTH
    )
    passage_gradient = (
        jnp.dot(score_gradient.T, query_rows, precision=EXACT_PRECISION) / SOFTMAX_WARMTH
    )
    dunit_rows = jnp.stack([query_gradient, passage_gradient], axis=1).reshape(embedded.shape)
    radial = jnp.sum(unit_rows * dunit_rows, axis=1, keepdims=True)
    return (loss_value, (dunit_rows - unit_rows * radial) / norms)


def body(
    context,
    o_weight,
    resid,
    norm_gain,
    router,
    gate_weight,
    up_weight,
    down_weight,
    expert_ids,
    lengths,
):
    expert_count = lax.axis_size("expert")
    tensor_count = lax.axis_size("tensor")
    device_count = expert_count * tensor_count
    expert_index = lax.axis_index("expert")
    tensor_index = lax.axis_index("tensor")
    local_rows, model_width = resid.shape
    expert_total = router.shape[1]
    top_count = expert_ids.shape[1]
    seq_count = lengths.shape[1]
    seq_total = seq_count * expert_count
    capacity = max(2, local_rows * top_count * 5 // (4 * expert_total))
    attention_out = lax.psum_scatter(
        jnp.dot(context, o_weight, preferred_element_type=jnp.float32).astype(jnp.bfloat16),
        "tensor",
        scatter_dimension=0,
        tiled=True,
    ).astype(jnp.float32)
    resid_mid = resid.astype(jnp.float32) + attention_out
    rms_scale = lax.rsqrt(jnp.mean(resid_mid * resid_mid, axis=1, keepdims=True) + EPSILON)
    normed = (resid_mid * rms_scale * norm_gain).astype(jnp.bfloat16)
    logits = jnp.dot(normed, router, preferred_element_type=jnp.float32)
    expert_onehot = (expert_ids[:, :, None] == jnp.arange(expert_total, dtype=jnp.int32)).astype(
        jnp.float32
    )
    chosen = jnp.sum(logits[:, None, :] * expert_onehot, axis=2)
    exp_chosen = jnp.exp(chosen)
    gate_probs = exp_chosen / jnp.sum(exp_chosen, axis=1, keepdims=True)
    flat_ids = expert_ids.reshape(local_rows * top_count)
    target = flat_ids * capacity + slot_positions(flat_ids, expert_total)

    def move_rows(blocks):
        return lax.all_to_all(blocks, ("expert", "tensor"), split_axis=0, concat_axis=0, tiled=True)

    seq_lengths = lengths[0]
    seq_ends = jnp.cumsum(seq_lengths)
    seq_starts = seq_ends - seq_lengths
    positions = tensor_index * local_rows + jnp.arange(local_rows, dtype=jnp.int32)
    member = (
        (positions[None, :] >= seq_starts[:, None]) & (positions[None, :] < seq_ends[:, None])
    ).astype(jnp.float32)
    tok_len = jnp.sum(member * seq_lengths[:, None].astype(jnp.float32), axis=0)
    repeated = jnp.broadcast_to(normed[:, None, :], (local_rows, top_count, model_width)).reshape(
        local_rows * top_count, model_width
    )
    buffer = (
        jnp.zeros((expert_total * capacity, model_width), jnp.bfloat16).at[target].set(repeated)
    )
    received = move_rows(buffer.reshape(device_count, capacity, model_width)).reshape(
        device_count * capacity, model_width
    )
    pre_gate = jnp.dot(received, gate_weight[0], preferred_element_type=jnp.float32)
    pre_up = jnp.dot(received, up_weight[0], preferred_element_type=jnp.float32)
    hidden = (jax.nn.silu(pre_gate) * pre_up).astype(jnp.bfloat16)
    expert_rows = jnp.dot(hidden, down_weight[0], preferred_element_type=jnp.float32).astype(
        jnp.bfloat16
    )
    seq_local = jnp.dot(jnp.arange(seq_count, dtype=jnp.float32), member, precision=EXACT_PRECISION)
    seq_global = seq_local + (expert_index * seq_count).astype(jnp.float32)
    info_rows = jnp.stack(
        [
            gate_probs,
            jnp.broadcast_to(seq_global[:, None], (local_rows, top_count)),
            jnp.broadcast_to(tok_len[:, None], (local_rows, top_count)),
        ],
        axis=2,
    ).reshape(local_rows * top_count, 3)
    info_init = jnp.zeros((expert_total * capacity, 3), jnp.float32).at[:, 2].set(1.0)
    info_buffer = info_init.at[target].set(info_rows).reshape(device_count, capacity, 3)
    slot_data = lax.all_to_all(
        info_buffer, ("expert", "tensor"), split_axis=0, concat_axis=0, tiled=True
    ).reshape(device_count * capacity, 3)
    slot_gate = slot_data[:, 0:1]
    slot_seq = slot_data[:, 1].astype(jnp.int32)
    slot_len = slot_data[:, 2:3]
    slot_onehot = (slot_seq[:, None] == jnp.arange(seq_total, dtype=jnp.int32)).astype(jnp.float32)
    out_float = expert_rows.astype(jnp.float32)
    expert_part = lax.dot_general(
        slot_onehot,
        slot_gate * out_float / slot_len,
        (((0,), (0,)), ((), ())),
        precision=EXACT_PRECISION,
        preferred_element_type=jnp.float32,
    )
    partial_value = jnp.dot(member, resid_mid / tok_len[:, None], precision=EXACT_PRECISION)
    placed = lax.dynamic_update_slice_in_dim(
        expert_part,
        lax.dynamic_slice_in_dim(expert_part, expert_index * seq_count, seq_count, 0)
        + partial_value,
        expert_index * seq_count,
        0,
    )
    embedded = lax.psum(placed, ("expert", "tensor"))
    loss_value, dembedded = contrast(embedded)
    own_rows = lax.dynamic_slice_in_dim(
        dembedded, expert_index * seq_count, seq_count, 0
    ) / seq_lengths[:, None].astype(jnp.float32)
    dresid_out = lax.dot_general(
        member,
        own_rows,
        (((0,), (0,)), ((), ())),
        precision=EXACT_PRECISION,
        preferred_element_type=jnp.float32,
    )
    slot_dresid = jnp.dot(slot_onehot, dembedded, precision=EXACT_PRECISION) / slot_len
    received_grad = (slot_gate * slot_dresid).astype(jnp.bfloat16)
    slot_dgate = jnp.sum(slot_dresid * out_float, axis=1)
    returned = lax.all_to_all(
        slot_dgate.reshape(device_count, capacity),
        ("expert", "tensor"),
        split_axis=0,
        concat_axis=0,
        tiled=True,
    )
    dgate_prob = returned.reshape(expert_total * capacity)[target].reshape(local_rows, top_count)
    dhidden = contract_last(received_grad, down_weight[0])
    gate_sigmoid = jax.nn.sigmoid(pre_gate)
    dpre_gate = (dhidden * pre_up * gate_sigmoid * (1.0 + pre_gate * (1.0 - gate_sigmoid))).astype(
        jnp.bfloat16
    )
    dpre_up = (dhidden * jax.nn.silu(pre_gate)).astype(jnp.bfloat16)
    dx_rows = (
        contract_last(dpre_gate, gate_weight[0]) + contract_last(dpre_up, up_weight[0])
    ).astype(jnp.bfloat16)
    dx_moe = jnp.sum(
        move_rows(dx_rows.reshape(device_count, capacity, model_width))
        .reshape(expert_total * capacity, model_width)[target]
        .astype(jnp.float32)
        .reshape(local_rows, top_count, model_width),
        axis=1,
    )
    dchosen = gate_probs * (dgate_prob - jnp.sum(gate_probs * dgate_prob, axis=1, keepdims=True))
    dlogits = jnp.sum(dchosen[:, :, None] * expert_onehot, axis=1).astype(jnp.bfloat16)
    dnormed = dx_moe + contract_last(dlogits, router)
    gain_grad = dnormed * norm_gain
    grad_resid = (
        dresid_out
        + rms_scale * gain_grad
        - resid_mid * rms_scale**3 * jnp.mean(gain_grad * resid_mid, axis=1, keepdims=True)
    )
    return (loss_value.reshape(1), grad_resid.astype(jnp.bfloat16))


ROW_EXTRA = 128
LEAVES_IN = ((0, 1), (3, 2))
INNER_SWAP = ((1, 2), (2, 1))
LEAVES_OUT = ((1, 0), (2, 3))
PIECES = (1, 1, 1, 1)
FORWARD_ORDER = (
    "p0", "p1", "p2", "p3", "s0", "s1", "t0", "s2", "t1", "s3", "d0", "t2", "d1", "x0", "t3", "d2", "x1", "d3", "x2", "x3",
)
BACKWARD_ORDER = (
    "b0", "b1", "c0", "b2", "c1", "b3", "c2", "i0", "c3", "i1", "l0",
)
VMEM_LIMIT = 24 * 2**20
FIRST_LIMIT = 54 * 2**20
FIRST_CUTS = 8
BLOCK_ORDER = ((3, 2, 1, 0), (3, 0, 2, 1), (0, 3, 1, 2), (0, 1, 2, 3))
OWN_EXPERT, LEAF, Z, PEER, PEER_EXPERT, ORDER = 0, 1, 2, 3, 7, 11
BF16 = jnp.bfloat16
F32 = jnp.float32


def dot_nn(left, right):
    return lax.dot_general(left, right, (((1,), (0,)), ((), ())), preferred_element_type=F32)


def halves(value):
    high = value.astype(BF16)
    return high, (value - high.astype(F32)).astype(BF16)


def stacked_halves(value):
    high, low = halves(value)
    return jnp.concatenate([high.astype(F32), low.astype(F32)], axis=0).astype(BF16)


def fold(product):
    rows = product.shape[0] // 2
    return product[:rows] + product[rows:]


def iota(shape, axis):
    return lax.broadcasted_iota(jnp.int32, shape, axis)


def project_kernel(block, offset, n, context_ref, weight_ref, resid_ref, *rest):
    out_ref = rest[-1]
    rows = context_ref.shape[0]
    part = dot_nn(context_ref[...], weight_ref[...])
    share = jnp.where(n[Z] == block, resid_ref[offset : offset + rows, :].astype(F32), 0.0)
    out_ref[:rows, :] = (part + share).astype(BF16)


def first_kernel(experts, ids_ref, context_hbm, weight_hbm, resid_hbm, out_ref, context_ref, weight_ref, resid_ref, sems):
    rows, heads = context_ref.shape
    cuts = sems.shape[0] - 2
    step = heads // cuts
    copies = []
    for i in range(cuts):
        at = pl.ds(i * step, step)
        copies.append(pltpu.make_async_copy(weight_hbm.at[at], weight_ref.at[at], sems.at[i]))
    context_copy = pltpu.make_async_copy(context_hbm.at[pl.ds(0, rows)], context_ref, sems.at[cuts])
    resid_copy = pltpu.make_async_copy(resid_hbm.at[pl.ds(0, rows)], resid_ref, sems.at[cuts + 1])
    context_copy.start()
    for copy in copies:
        copy.start()
    resid_copy.start()
    z = lax.axis_index("tensor")
    mask = jnp.zeros((experts, rows), F32)
    for k in range(ids_ref.shape[0]):
        mask += (ids_ref[k : k + 1, :] == iota((experts, rows), 0)).astype(F32)
    out_ref[rows:, :] = jnp.zeros((experts, out_ref.shape[1]), BF16)
    for block in range(4):
        out_ref[rows:, block * rows : (block + 1) * rows] = jnp.where(z == block, mask, 0.0).astype(BF16)
    context_copy.wait()
    part = None
    for i, copy in enumerate(copies):
        copy.wait()
        at = slice(i * step, (i + 1) * step)
        term = dot_nn(context_ref[:, at], weight_ref[at, :])
        part = term if part is None else part + term
    resid_copy.wait()
    share = jnp.where(z == 0, resid_ref[...].astype(F32), 0.0)
    out_ref[:rows, :] = (part + share).astype(BF16)


def add_kernel(n, left_ref, right_ref, _, out_ref):
    out_ref[...] = (left_ref[...].astype(F32) + right_ref[...].astype(F32)).astype(BF16)


def dispatch_kernel(capacity, block, pieces, n, *refs):
    inner_refs, back_refs, refs = refs[:pieces], refs[pieces : 2 * pieces], refs[2 * pieces :]
    gain_ref, router_ref, token_ref, *refs = refs
    rows = token_ref.shape[1]
    outs = refs[-7:] if block == 0 else refs[-6:]
    row_refs, t_ref, place_ref = outs[:4], outs[4], outs[5]
    experts, width = router_ref.shape
    x = jnp.concatenate(
        [
            jnp.where(n[LEAF] == 1, back[...].astype(F32), inner[...].astype(F32))
            for inner, back in zip(inner_refs, back_refs)
        ],
        axis=0,
    )
    if block == 0:
        wide = x[rows:, : 4 * rows].astype(BF16)
        outs[6][...] = wide
        x = x[:rows]
    else:
        wide = refs[0][...]
    mask = wide[:, block * rows : (block + 1) * rows]
    t_ref[0] = x.astype(BF16)
    scale = lax.rsqrt(jnp.mean(x * x, axis=1, keepdims=True) + EPSILON)
    normed = (x * scale * gain_ref[...]).astype(BF16)
    logits = contract_last(router_ref[...], normed)
    chosen = mask.astype(F32) > 0.5
    exp_chosen = jnp.where(chosen, jnp.exp(jnp.where(chosen, logits, 0.0)), 0.0)
    gates = exp_chosen / jnp.sum(exp_chosen, axis=0, keepdims=True)
    earlier = (iota((rows, rows), 0) < iota((rows, rows), 1)).astype(F32).astype(BF16)
    position = jnp.where(chosen, dot_nn(mask, earlier), -1.0)
    gate_high, gate_low = halves(gates)
    inverse = token_ref[1:2, :]
    inv_high = inverse.astype(BF16).astype(F32)
    inv_mid = (inverse - inv_high).astype(BF16).astype(F32)
    inv_low = inverse - inv_high - inv_mid
    slot_row = iota((8, rows), 0)
    token_part = jnp.where(
        slot_row == 0,
        token_ref[0:1, :],
        jnp.where(slot_row == 1, inv_high, jnp.where(slot_row == 2, inv_mid, jnp.where(slot_row == 3, inv_low, 0.0))),
    )
    extra = jnp.concatenate(
        [
            gate_high.astype(F32),
            gate_low.astype(F32),
            token_part,
            jnp.zeros((ROW_EXTRA - 2 * experts - 8, rows), F32),
        ],
        axis=0,
    ).astype(BF16)
    expert_row = iota((experts, rows), 0)
    slot = iota((capacity, rows), 0).astype(F32)
    picks = []
    for way in range(4):
        own = jnp.sum(jnp.where(expert_row == n[PEER_EXPERT + way], position, 0.0), axis=0, keepdims=True)
        picks.append((slot == own).astype(F32))
    picked = jnp.concatenate(picks, axis=0)
    place_ref[0] = jnp.transpose(picked).astype(BF16)
    picked = picked.astype(BF16)
    sent = dot_nn(picked, normed)
    sent_extra = contract_last(picked, extra)
    for way in range(4):
        at = slice(way * capacity, (way + 1) * capacity)
        row_refs[way][:, :width] = sent[at].astype(BF16)
        row_refs[way][:, width:] = sent_extra[at].astype(BF16)


def expert_kernel(n, r0, r1, r2, r3, gate_ref, up_ref, *refs):
    pooled_ref, hidden_ref, a_ref, b_ref, info_ref, x_ref, weight_ref = refs[-7:]
    width = gate_ref.shape[0]
    experts = 16

    @pl.when(pl.program_id(0) == 0)
    def start():
        x_ref[...] = jnp.concatenate([r[:, :width].astype(F32) for r in (r0, r1, r2, r3)], axis=0).astype(BF16)
        extra = jnp.concatenate([r[:, width:].astype(F32) for r in (r0, r1, r2, r3)], axis=0).astype(BF16)
        own = n[OWN_EXPERT]

        def mixer(source, goal):
            gates = (goal < experts) & ((source == goal) | (source == goal + experts))
            sequence = (goal == experts) & (source == 2 * experts)
            inverse = (goal == experts + 1) & (source > 2 * experts) & (source < 2 * experts + 4)
            gate = (goal == experts + 2) & ((source == own) | (source == own + experts))
            return (gates | sequence | inverse | gate).astype(F32).astype(BF16)

        square = (ROW_EXTRA, ROW_EXTRA)
        info = dot_nn(extra, mixer(iota(square, 0), iota(square, 1)))
        info_ref[0] = info
        turned = contract_last(mixer(iota(square, 1), iota(square, 0)), extra)
        sequence = turned[experts : experts + 1]
        weight = turned[experts + 1 : experts + 2] * turned[experts + 2 : experts + 3]
        pool = jnp.where(iota((pooled_ref.shape[0], extra.shape[0]), 0).astype(F32) == sequence, weight, 0.0)
        weight_ref[...] = stacked_halves(pool)

    x = x_ref[...]
    pre_gate = dot_nn(x, gate_ref[...])
    pre_up = dot_nn(x, up_ref[...])
    sigmoid = 1.0 / (1.0 + jnp.exp(-pre_gate))
    silu = pre_gate * sigmoid
    hidden = (silu * pre_up).astype(BF16)
    hidden_ref[0] = hidden
    a_ref[0] = pre_up * sigmoid * (1.0 + pre_gate * (1.0 - sigmoid))
    b_ref[0] = silu
    pooled_ref[...] = fold(dot_nn(weight_ref[...], hidden))


def sum_kernel(n, p0, p1, p2, p3, _, out_ref):
    near = p0[...].astype(F32) + p1[...].astype(F32)
    out_ref[...] = (near + (p2[...].astype(F32) + p3[...].astype(F32))).astype(BF16)


def embed_kernel(n, p0, p1, p2, p3, down_ref, t_ref, token_ref, _, o0, o1, o2, o3, part_ref):
    pooled = p0[...] + p1[...] + p2[...] + p3[...]
    part = fold(dot_nn(stacked_halves(pooled), down_ref[...]))
    sequences = part.shape[0]
    own = jnp.where(
        iota((sequences, t_ref.shape[1]), 0).astype(F32) == token_ref[0:1, :], token_ref[1:2, :], 0.0
    )
    part_ref[...] = part + fold(dot_nn(stacked_halves(own), t_ref[0]))
    rows = o0.shape[0]
    for way, out in enumerate((o0, o1, o2, o3)):
        out[...] = part_ref[pl.ds(pl.multiple_of(n[PEER + way] * rows, rows), rows), :].astype(out.dtype)


def contrast_kernel(n, q0, q1, q2, q3, down_ref, _, grad_ref, hidden_grad_ref, loss_ref, all_ref):
    rows = q0.shape[0]
    for way, part in enumerate((q0, q1, q2, q3)):
        all_ref[pl.ds(pl.multiple_of(n[PEER + way] * rows, rows), rows), :] = part[...].astype(F32)
    embedded = all_ref[...].astype(BF16)
    count = embedded.shape[0]
    pairs = count // 2
    products = contract_last(embedded, embedded)
    row, column = iota((count, count), 0), iota((count, count), 1)
    squares = jnp.where(row == column, products, 0.0)
    inverse = 1.0 / jnp.sqrt(jnp.sum(squares, axis=1, keepdims=True) + EPSILON)
    inverse_row = 1.0 / jnp.sqrt(jnp.sum(squares, axis=0, keepdims=True) + EPSILON)
    cosines = products * inverse * inverse_row
    scores = cosines / SOFTMAX_WARMTH
    is_pair = (row % 2 == 0) & (column % 2 == 1)
    matched = is_pair & (column == row + 1)
    exp_scores = jnp.where(is_pair, jnp.exp(jnp.where(is_pair, scores, 0.0)), 0.0)
    row_total = jnp.sum(exp_scores, axis=1, keepdims=True)
    is_query = iota((count, 1), 0) % 2 == 0
    row_total = jnp.where(is_query, row_total, 1.0)
    own_score = jnp.sum(jnp.where(matched, scores, 0.0), axis=1, keepdims=True)
    terms = jnp.where(is_query, jnp.log(row_total) - own_score, 0.0)
    loss_ref[0] = jnp.sum(terms) / pairs
    dscore = (exp_scores / row_total - jnp.where(matched, 1.0, 0.0)) * (LOSS_SCALE / pairs)
    both = dscore + jnp.transpose(dscore)
    both = both / SOFTMAX_WARMTH
    radial = jnp.sum(both * cosines, axis=1, keepdims=True)
    mixer = (both - jnp.where(row == column, radial, 0.0)) * inverse * inverse_row
    grad = fold(dot_nn(stacked_halves(mixer), embedded))
    grad_ref[...] = grad
    hidden_grad_ref[...] = fold(contract_last(stacked_halves(grad), down_ref[...]))


def backward_kernel(capacity, n, a_ref, b_ref, hidden_ref, info_ref, dh_ref, gate_ref, up_ref, router_ref, _, o0, o1, o2, o3, dgate_ref, dup_ref, dlog_ref):
    experts = 16

    @pl.when(pl.program_id(0) == 0)
    def start():
        info = info_ref[0]
        slots = info.shape[0]
        sequence = info[:, experts : experts + 1]
        weight = info[:, experts + 1 : experts + 2] * info[:, experts + 2 : experts + 3]
        member = (iota((slots, dh_ref.shape[0]), 1).astype(F32) == sequence).astype(F32).astype(BF16)
        high, low = halves(dh_ref[...])
        dhidden = weight * (dot_nn(member, high) + dot_nn(member, low))
        dgate_ref[...] = (dhidden * a_ref[0]).astype(BF16)
        dup_ref[...] = (dhidden * b_ref[0]).astype(BF16)
        moved = jnp.sum(dhidden * hidden_ref[0].astype(F32), axis=1, keepdims=True)
        lane = iota((slots, ROW_EXTRA), 1)
        gates = jnp.where(lane < experts, info, 0.0)
        dlog_ref[...] = (moved * (jnp.where(lane == n[OWN_EXPERT], 1.0, 0.0) - gates)).astype(BF16)

    total = (
        contract_last(dgate_ref[...], gate_ref[...])
        + contract_last(dup_ref[...], up_ref[...])
        + dot_nn(dlog_ref[...], router_ref[...])
    )
    for way, out in enumerate((o0, o1, o2, o3)):
        out[...] = total[way * capacity : (way + 1) * capacity].astype(BF16)


def combine_kernel(n, place_ref, r0, r1, r2, r3, _, out_ref, narrow_ref):
    rows = jnp.concatenate([r[...].astype(F32) for r in (r0, r1, r2, r3)], axis=0).astype(BF16)
    total = dot_nn(place_ref[0], rows)
    out_ref[...] = total
    narrow_ref[...] = total.astype(BF16)


def spread_kernel(n, t_ref, grad_ref, token_ref, _, out_ref, scale_ref):
    x = t_ref[0].astype(F32)
    scale = lax.rsqrt(jnp.mean(x * x, axis=1, keepdims=True) + EPSILON)
    spread = jnp.where(iota((grad_ref.shape[0], x.shape[0]), 0).astype(F32) == token_ref[0:1, :], 1.0, 0.0)
    spread = jnp.transpose(spread).astype(BF16)
    inverse = jnp.transpose(token_ref[...])[:, 1:2]
    high, low = halves(grad_ref[...])
    out_ref[...] = inverse * (dot_nn(spread, high) + dot_nn(spread, low))
    scale_ref[...] = jnp.broadcast_to(scale, scale_ref.shape)


def finish_kernel(n, t_ref, gain_ref, dresid_ref, scale_ref, own_ref, r4, r5, r6, _, out_ref):
    x = t_ref[0].astype(F32)
    scale = scale_ref[:, :1]
    dnormed = own_ref[...] + r4[...].astype(F32) + r5[...].astype(F32) + r6[...].astype(F32)
    gained = dnormed * gain_ref[...]
    pull = (scale * scale * scale) * jnp.mean(gained * x, axis=1, keepdims=True)
    out_ref[...] = (dresid_ref[...] + scale * gained - x * pull).astype(BF16)


class Chain:
    def __init__(self, numbers, first):
        self.numbers = numbers
        self.last = first

    def __call__(self, kernel, ins, outs, *, steps=1, kept=(), scratch=(), flops=0):
        args, in_specs = zip(*ins)
        args, in_specs = list(args), list(in_specs)
        shapes, out_specs = zip(*outs)
        aliases = {}
        for at, array in kept:
            aliases[1 + len(args)] = at
            args.append(array)
            in_specs.append(pl.BlockSpec(memory_space=pl.ANY))
        args.append(self.last)
        in_specs.append(pl.BlockSpec(memory_space=pl.ANY))
        result = pl.pallas_call(
            kernel,
            out_shape=list(shapes),
            grid_spec=pltpu.PrefetchScalarGridSpec(
                num_scalar_prefetch=1,
                grid=(steps,),
                in_specs=in_specs,
                out_specs=list(out_specs),
                scratch_shapes=scratch,
            ),
            input_output_aliases=aliases,
            compiler_params=pltpu.CompilerParams(vmem_limit_bytes=VMEM_LIMIT),
            cost_estimate=pl.CostEstimate(flops=1, bytes_accessed=1, transcendentals=0),
        )(self.numbers, *args)
        self.last = result[0]
        return result


def fixed(shape):
    return pl.BlockSpec(shape, lambda j, n: (0,) * len(shape))


def whole(array):
    return array, pl.BlockSpec(memory_space=pltpu.VMEM)


def fast_body(context, o_weight, resid, norm_gain, router, gate_weight, up_weight, down_weight, expert_ids, lengths):
    e = lax.axis_index("expert")
    z = lax.axis_index("tensor")
    rows, width = resid.shape
    heads = context.shape[1]
    experts = router.shape[1]
    top = expert_ids.shape[1]
    seq_count = lengths.shape[1]
    sequences = 4 * seq_count
    hidden_width = gate_weight.shape[2]
    capacity = max(2, rows * top * 5 // (4 * experts))
    slots = 4 * capacity
    leaf = (z == 0) | (z == 3)
    ways = e ^ jnp.arange(4, dtype=jnp.int32)
    numbers = jnp.concatenate(
        [
            jnp.stack([e * 4 + z, leaf.astype(jnp.int32), z]),
            ways,
            ways * 4 + z,
            jnp.asarray(BLOCK_ORDER, jnp.int32)[z],
        ]
    ).astype(jnp.int32)
    gate_w, up_w, down_w = gate_weight[0], up_weight[0], down_weight[0]
    gain = norm_gain.reshape(1, width)
    router_turned = router.T
    router_rows = jnp.pad(router_turned, ((0, ROW_EXTRA - experts), (0, 0)))

    def along_z(value, pairs):
        return lax.ppermute(value, "tensor", pairs)

    def swap_z(value, bits):
        return lax.ppermute(value, "tensor", [(i, i ^ bits) for i in range(4)])

    def swap_e(value, bits):
        return lax.ppermute(value, "expert", [(i, i ^ bits) for i in range(4)])

    seq_lengths = lengths[0]
    seq_ends = jnp.cumsum(seq_lengths)
    places = jnp.arange(4 * rows, dtype=jnp.int32)
    after = places[None, :] >= seq_ends[:, None]
    seq_local = jnp.sum(after.astype(jnp.int32), axis=0)
    token_len = jnp.sum(
        jnp.where(seq_local[None, :] == jnp.arange(seq_count, dtype=jnp.int32)[:, None], seq_lengths[:, None], 0), axis=0
    )
    token_info = jnp.concatenate(
        [
            (seq_local + e * seq_count).astype(F32)[None],
            (1.0 / token_len.astype(F32))[None],
            jnp.zeros((6, 4 * rows), F32),
        ],
        axis=0,
    )

    chain = Chain(numbers, gain)
    shape = jax.ShapeDtypeStruct
    tile = 512
    pieces = []
    for c, cuts in enumerate(PIECES):
        pieces += [(c, i * (rows // cuts), rows // cuts) for i in range(cuts)]
    count = len(pieces)
    parts, half, inner, back, from_leaf, from_inner = ([None] * count for _ in range(6))
    received, pools, shared, kept_rows, kept_acts = [None] * 4, [None] * 4, {}, {}, {}

    def first_hop(i):
        c, offset, size = pieces[i]
        if i == 0:
            away = pl.BlockSpec(memory_space=pl.ANY)
            near = pl.BlockSpec(memory_space=pltpu.VMEM)
            chain.last = parts[0] = pl.pallas_call(
                functools.partial(first_kernel, experts),
                out_shape=shape((size + experts, width), BF16),
                in_specs=[near, away, away, away],
                out_specs=near,
                scratch_shapes=[
                    pltpu.VMEM((size, heads), BF16),
                    pltpu.VMEM((heads, width), BF16),
                    pltpu.VMEM((size, width), BF16),
                    pltpu.SemaphoreType.DMA((FIRST_CUTS + 2,)),
                ],
                compiler_params=pltpu.CompilerParams(vmem_limit_bytes=FIRST_LIMIT),
            )(expert_ids.T, context, o_weight, resid)
            from_leaf[0] = along_z(parts[0], LEAVES_IN)
            return
        at = (c * rows + offset) // size
        ins = [
            (context, pl.BlockSpec((size, heads), lambda j, n: (at, 0))),
            whole(o_weight),
            whole(resid),
        ]
        (parts[i],) = chain(
            functools.partial(project_kernel, c, offset),
            ins,
            [(shape((size, width), BF16), fixed((size, width)))],
            flops=2 * size * heads * width,
        )
        from_leaf[i] = along_z(parts[i], LEAVES_IN)

    def add(left, right):
        like = shape(right.shape, BF16)
        return chain(add_kernel, [whole(left), whole(right)], [(like, fixed(like.shape))], flops=left.size)[0]

    def second_hop(i):
        half[i] = add(parts[i], from_leaf[i])
        from_inner[i] = along_z(half[i], INNER_SWAP)

    def third_hop(i):
        inner[i] = add(half[i], from_inner[i])
        back[i] = along_z(inner[i], LEAVES_OUT)

    def dispatch(c):
        mine = [i for i in range(count) if pieces[i][0] == c]
        ins = [whole(inner[i]) for i in mine] + [whole(back[i]) for i in mine]
        ins += [
            whole(gain),
            whole(router_turned),
            (token_info, pl.BlockSpec((8, rows), lambda j, n: (0, c))),
        ]
        if c > 0:
            ins.append(whole(shared["mask"]))
        sent_shape = (capacity, width + ROW_EXTRA)
        outs = [(shape(sent_shape, BF16), fixed(sent_shape))] * 4
        for size in ((rows, width), (rows, slots)):
            outs.append((shape((4,) + size, BF16), pl.BlockSpec((1,) + size, lambda j, n: (c, 0, 0))))
        if c == 0:
            outs.append((shape((experts, 4 * rows), BF16), fixed((experts, 4 * rows))))
        result = chain(
            functools.partial(dispatch_kernel, capacity, c, len(mine)),
            ins,
            outs,
            kept=sorted(kept_rows.items()),
            flops=2 * slots * rows * width,
        )
        kept_rows.update({4: result[4], 5: result[5]})
        if c == 0:
            shared["mask"] = result[6]
        received[c] = [result[0]] + [swap_e(result[way], way) for way in (1, 2, 3)]

    def expert(c):
        tile = hidden_width
        block = lambda size: pl.BlockSpec((1, slots, size), lambda j, n: (c, 0, j))
        outs = [(shape((sequences, hidden_width), F32), pl.BlockSpec((sequences, tile), lambda j, n: (0, j)))]
        outs += [(shape((4, slots, hidden_width), kind), block(tile)) for kind in (BF16, F32, F32)]
        outs.append((shape((4, slots, ROW_EXTRA), F32), pl.BlockSpec((1, slots, ROW_EXTRA), lambda j, n: (c, 0, 0))))
        weight_spec = pl.BlockSpec(memory_space=pltpu.VMEM)
        result = chain(
            expert_kernel,
            [whole(r) for r in received[c]] + [(gate_w, weight_spec), (up_w, weight_spec)],
            outs,
            steps=hidden_width // tile,
            kept=sorted(kept_acts.items()),
            scratch=[pltpu.VMEM((slots, width), BF16), pltpu.VMEM((2 * sequences, slots), BF16)],
            flops=4 * slots * width * hidden_width,
        )
        pools[c] = result[0]
        kept_acts.update({i: result[i] for i in (1, 2, 3, 4)})

    calls = {"p": first_hop, "s": second_hop, "t": third_hop, "d": dispatch, "x": expert}
    for step in FORWARD_ORDER:
        calls[step[0]](int(step[1:]))

    total_all, place_all = kept_rows[4], kept_rows[5]
    hidden_all, a_all, b_all, info_all = (kept_acts[i] for i in (1, 2, 3, 4))
    own_rows = (total_all, pl.BlockSpec((1, rows, width), lambda j, n: (n[Z], 0, 0)))
    own_tokens = (token_info, pl.BlockSpec((8, rows), lambda j, n: (0, n[Z])))
    seq_size = (seq_count, width)
    quarters = chain(
        embed_kernel,
        [whole(pool) for pool in pools] + [whole(down_w), own_rows, own_tokens],
        [(shape(seq_size, kind), fixed(seq_size)) for kind in (F32, BF16, BF16, BF16)],
        scratch=[pltpu.VMEM((sequences, width), F32)],
        flops=4 * sequences * hidden_width * width,
    )

    def add_four(values):
        return chain(sum_kernel, [whole(v) for v in values], [(shape(seq_size, BF16), fixed(seq_size))])[0]

    mine = add_four([quarters[0]] + [swap_e(quarters[way], way) for way in (1, 2, 3)])
    mine = add_four([mine] + [swap_z(mine, way) for way in (1, 2, 3)])
    gathered = [mine] + [swap_e(mine, way) for way in (1, 2, 3)]
    sizes = ((sequences, width), (sequences, hidden_width))
    dembedded, hidden_grad, loss = chain(
        contrast_kernel,
        [whole(piece) for piece in gathered] + [whole(down_w)],
        [(shape(size, F32), fixed(size)) for size in sizes]
        + [(shape((1,), F32), pl.BlockSpec(memory_space=pltpu.SMEM))],
        scratch=[pltpu.VMEM((sequences, width), F32)],
        flops=4 * sequences * hidden_width * width,
    )
    returned, sums = [None] * 4, [None] * 4

    def backward(k):
        tile = width
        block = lambda size: pl.BlockSpec((1, slots, size), lambda j, n: (n[ORDER + k], 0, 0))
        weight_spec = pl.BlockSpec(memory_space=pltpu.VMEM)
        grads = chain(
            functools.partial(backward_kernel, capacity),
            [
                (a_all, block(hidden_width)),
                (b_all, block(hidden_width)),
                (hidden_all, block(hidden_width)),
                (info_all, block(ROW_EXTRA)),
                whole(hidden_grad),
                (gate_w, weight_spec),
                (up_w, weight_spec),
                (router_rows, pl.BlockSpec((ROW_EXTRA, tile), lambda j, n: (0, j))),
            ],
            [(shape((capacity, width), BF16), pl.BlockSpec((capacity, tile), lambda j, n: (0, j)))] * 4,
            steps=width // tile,
            scratch=[
                pltpu.VMEM((slots, hidden_width), BF16),
                pltpu.VMEM((slots, hidden_width), BF16),
                pltpu.VMEM((slots, ROW_EXTRA), BF16),
            ],
            flops=4 * slots * width * hidden_width,
        )
        returned[k] = [grads[0]] + [swap_e(grads[way], way) for way in (1, 2, 3)]

    def combine(k):
        sums[k] = chain(
            combine_kernel,
            [(place_all, pl.BlockSpec((1, rows, slots), lambda j, n: (n[ORDER + k], 0, 0)))]
            + [whole(r) for r in returned[k]],
            [(shape((rows, width), kind), fixed((rows, width))) for kind in (F32, BF16)],
            flops=2 * slots * rows * width,
        )

    hops = {}

    def combined(k):
        combine(k)
        if k < 3:
            hops[k] = along_z(sums[k][1], LEAVES_IN)

    def inner_hop(k):
        total = add(sums[(0, 2)[k]][0], hops[(0, 1)[k]])
        hops[3 + k] = along_z(total, INNER_SWAP)

    def last_hop(_):
        hops[5] = along_z(add(sums[1][0], hops[3]), LEAVES_OUT)

    calls = {"b": backward, "c": combined, "i": inner_hop, "l": last_hop}
    for step in BACKWARD_ORDER:
        calls[step[0]](int(step[1:]))
    dresid, scales = chain(
        spread_kernel,
        [own_rows, whole(dembedded), own_tokens],
        [(shape((rows, width), F32), fixed((rows, width))), (shape((rows, 128), F32), fixed((rows, 128)))],
    )
    (grad,) = chain(
        finish_kernel,
        [own_rows, whole(gain), whole(dresid), whole(scales)]
        + [whole(value) for value in (sums[3][0], hops[2], hops[4], hops[5])],
        [(shape((rows, width), BF16), fixed((rows, width)))],
        flops=4 * rows * sequences * width,
    )
    return loss, grad


def solution(mesh):
    shape = dict(mesh.shape)
    part_body = fast_body if (shape["expert"], shape["tensor"]) == (4, 4) else body
    in_specs = (
        P(("groups", "expert"), "tensor"),
        P("tensor", None),
        P(("groups", "expert", "tensor"), None),
        P(),
        P(),
        P(("expert", "tensor"), None, None),
        P(("expert", "tensor"), None, None),
        P(("expert", "tensor"), None, None),
        P(("groups", "expert", "tensor"), None),
        P(("groups", "expert"), None),
    )
    out_specs = (P("groups"), P(("groups", "expert", "tensor"), None))
    return jax.shard_map(part_body, mesh=mesh, in_specs=in_specs, out_specs=out_specs, check_vma=False)
```

```python
import functools

import jax
import jax.numpy as jnp
from jax import lax
from jax.experimental import pallas as pl
from jax.experimental.pallas import tpu as pltpu
from jax.sharding import PartitionSpec as P

EPSILON = 1e-06
SOFTMAX_WARMTH = 0.05
LOSS_SCALE = 32768.0
EXACT_PRECISION = lax.Precision.HIGHEST


def slot_positions(flat_ids, expert_total):
    onehot = (flat_ids[..., None] == jnp.arange(expert_total, dtype=jnp.int32)).astype(jnp.int32)
    before = jnp.cumsum(onehot, axis=-2) - onehot
    return jnp.sum(before * onehot, axis=-1)


def contract_last(left, right):
    return lax.dot_general(
        left, right, (((1,), (1,)), ((), ())), preferred_element_type=jnp.float32
    )


def contrast(embedded):
    pair_count = embedded.shape[0] // 2
    norms = jnp.sqrt(jnp.sum(embedded * embedded, axis=1, keepdims=True) + EPSILON)
    unit_rows = embedded / norms
    query_rows = unit_rows[0::2]
    passage_rows = unit_rows[1::2]
    similarity_scores = (
        jnp.dot(query_rows, passage_rows.T, precision=EXACT_PRECISION) / SOFTMAX_WARMTH
    )
    exp_scores = jnp.exp(similarity_scores)
    row_total = jnp.sum(exp_scores, axis=1, keepdims=True)
    loss_value = jnp.mean(jnp.log(row_total[:, 0]) - jnp.diagonal(similarity_scores))
    score_gradient = (
        exp_scores / row_total - jnp.eye(pair_count, dtype=similarity_scores.dtype)
    ) * (LOSS_SCALE / pair_count)
    query_gradient = (
        jnp.dot(score_gradient, passage_rows, precision=EXACT_PRECISION) / SOFTMAX_WARMTH
    )
    passage_gradient = (
        jnp.dot(score_gradient.T, query_rows, precision=EXACT_PRECISION) / SOFTMAX_WARMTH
    )
    dunit_rows = jnp.stack([query_gradient, passage_gradient], axis=1).reshape(embedded.shape)
    radial = jnp.sum(unit_rows * dunit_rows, axis=1, keepdims=True)
    return (loss_value, (dunit_rows - unit_rows * radial) / norms)


def body(
    context,
    o_weight,
    resid,
    norm_gain,
    router,
    gate_weight,
    up_weight,
    down_weight,
    expert_ids,
    lengths,
):
    expert_count = lax.axis_size("expert")
    tensor_count = lax.axis_size("tensor")
    device_count = expert_count * tensor_count
    expert_index = lax.axis_index("expert")
    tensor_index = lax.axis_index("tensor")
    local_rows, model_width = resid.shape
    expert_total = router.shape[1]
    top_count = expert_ids.shape[1]
    seq_count = lengths.shape[1]
    seq_total = seq_count * expert_count
    capacity = max(2, local_rows * top_count * 5 // (4 * expert_total))
    attention_out = lax.psum_scatter(
        jnp.dot(context, o_weight, preferred_element_type=jnp.float32).astype(jnp.bfloat16),
        "tensor",
        scatter_dimension=0,
        tiled=True,
    ).astype(jnp.float32)
    resid_mid = resid.astype(jnp.float32) + attention_out
    rms_scale = lax.rsqrt(jnp.mean(resid_mid * resid_mid, axis=1, keepdims=True) + EPSILON)
    normed = (resid_mid * rms_scale * norm_gain).astype(jnp.bfloat16)
    logits = jnp.dot(normed, router, preferred_element_type=jnp.float32)
    expert_onehot = (expert_ids[:, :, None] == jnp.arange(expert_total, dtype=jnp.int32)).astype(
        jnp.float32
    )
    chosen = jnp.sum(logits[:, None, :] * expert_onehot, axis=2)
    exp_chosen = jnp.exp(chosen)
    gate_probs = exp_chosen / jnp.sum(exp_chosen, axis=1, keepdims=True)
    flat_ids = expert_ids.reshape(local_rows * top_count)
    target = flat_ids * capacity + slot_positions(flat_ids, expert_total)

    def move_rows(blocks):
        return lax.all_to_all(blocks, ("expert", "tensor"), split_axis=0, concat_axis=0, tiled=True)

    seq_lengths = lengths[0]
    seq_ends = jnp.cumsum(seq_lengths)
    seq_starts = seq_ends - seq_lengths
    positions = tensor_index * local_rows + jnp.arange(local_rows, dtype=jnp.int32)
    member = (
        (positions[None, :] >= seq_starts[:, None]) & (positions[None, :] < seq_ends[:, None])
    ).astype(jnp.float32)
    tok_len = jnp.sum(member * seq_lengths[:, None].astype(jnp.float32), axis=0)
    repeated = jnp.broadcast_to(normed[:, None, :], (local_rows, top_count, model_width)).reshape(
        local_rows * top_count, model_width
    )
    buffer = (
        jnp.zeros((expert_total * capacity, model_width), jnp.bfloat16).at[target].set(repeated)
    )
    received = move_rows(buffer.reshape(device_count, capacity, model_width)).reshape(
        device_count * capacity, model_width
    )
    pre_gate = jnp.dot(received, gate_weight[0], preferred_element_type=jnp.float32)
    pre_up = jnp.dot(received, up_weight[0], preferred_element_type=jnp.float32)
    hidden = (jax.nn.silu(pre_gate) * pre_up).astype(jnp.bfloat16)
    expert_rows = jnp.dot(hidden, down_weight[0], preferred_element_type=jnp.float32).astype(
        jnp.bfloat16
    )
    seq_local = jnp.dot(jnp.arange(seq_count, dtype=jnp.float32), member, precision=EXACT_PRECISION)
    seq_global = seq_local + (expert_index * seq_count).astype(jnp.float32)
    info_rows = jnp.stack(
        [
            gate_probs,
            jnp.broadcast_to(seq_global[:, None], (local_rows, top_count)),
            jnp.broadcast_to(tok_len[:, None], (local_rows, top_count)),
        ],
        axis=2,
    ).reshape(local_rows * top_count, 3)
    info_init = jnp.zeros((expert_total * capacity, 3), jnp.float32).at[:, 2].set(1.0)
    info_buffer = info_init.at[target].set(info_rows).reshape(device_count, capacity, 3)
    slot_data = lax.all_to_all(
        info_buffer, ("expert", "tensor"), split_axis=0, concat_axis=0, tiled=True
    ).reshape(device_count * capacity, 3)
    slot_gate = slot_data[:, 0:1]
    slot_seq = slot_data[:, 1].astype(jnp.int32)
    slot_len = slot_data[:, 2:3]
    slot_onehot = (slot_seq[:, None] == jnp.arange(seq_total, dtype=jnp.int32)).astype(jnp.float32)
    out_float = expert_rows.astype(jnp.float32)
    expert_part = lax.dot_general(
        slot_onehot,
        slot_gate * out_float / slot_len,
        (((0,), (0,)), ((), ())),
        precision=EXACT_PRECISION,
        preferred_element_type=jnp.float32,
    )
    partial_value = jnp.dot(member, resid_mid / tok_len[:, None], precision=EXACT_PRECISION)
    placed = lax.dynamic_update_slice_in_dim(
        expert_part,
        lax.dynamic_slice_in_dim(expert_part, expert_index * seq_count, seq_count, 0)
        + partial_value,
        expert_index * seq_count,
        0,
    )
    embedded = lax.psum(placed, ("expert", "tensor"))
    loss_value, dembedded = contrast(embedded)
    own_rows = lax.dynamic_slice_in_dim(
        dembedded, expert_index * seq_count, seq_count, 0
    ) / seq_lengths[:, None].astype(jnp.float32)
    dresid_out = lax.dot_general(
        member,
        own_rows,
        (((0,), (0,)), ((), ())),
        precision=EXACT_PRECISION,
        preferred_element_type=jnp.float32,
    )
    slot_dresid = jnp.dot(slot_onehot, dembedded, precision=EXACT_PRECISION) / slot_len
    received_grad = (slot_gate * slot_dresid).astype(jnp.bfloat16)
    slot_dgate = jnp.sum(slot_dresid * out_float, axis=1)
    returned = lax.all_to_all(
        slot_dgate.reshape(device_count, capacity),
        ("expert", "tensor"),
        split_axis=0,
        concat_axis=0,
        tiled=True,
    )
    dgate_prob = returned.reshape(expert_total * capacity)[target].reshape(local_rows, top_count)
    dhidden = contract_last(received_grad, down_weight[0])
    gate_sigmoid = jax.nn.sigmoid(pre_gate)
    dpre_gate = (dhidden * pre_up * gate_sigmoid * (1.0 + pre_gate * (1.0 - gate_sigmoid))).astype(
        jnp.bfloat16
    )
    dpre_up = (dhidden * jax.nn.silu(pre_gate)).astype(jnp.bfloat16)
    dx_rows = (
        contract_last(dpre_gate, gate_weight[0]) + contract_last(dpre_up, up_weight[0])
    ).astype(jnp.bfloat16)
    dx_moe = jnp.sum(
        move_rows(dx_rows.reshape(device_count, capacity, model_width))
        .reshape(expert_total * capacity, model_width)[target]
        .astype(jnp.float32)
        .reshape(local_rows, top_count, model_width),
        axis=1,
    )
    dchosen = gate_probs * (dgate_prob - jnp.sum(gate_probs * dgate_prob, axis=1, keepdims=True))
    dlogits = jnp.sum(dchosen[:, :, None] * expert_onehot, axis=1).astype(jnp.bfloat16)
    dnormed = dx_moe + contract_last(dlogits, router)
    gain_grad = dnormed * norm_gain
    grad_resid = (
        dresid_out
        + rms_scale * gain_grad
        - resid_mid * rms_scale**3 * jnp.mean(gain_grad * resid_mid, axis=1, keepdims=True)
    )
    return (loss_value.reshape(1), grad_resid.astype(jnp.bfloat16))


ROW_EXTRA = 128
LEAVES_IN = ((0, 1), (3, 2))
INNER_SWAP = ((1, 2), (2, 1))
LEAVES_OUT = ((1, 0), (2, 3))
PIECES = (1, 1, 1, 1)
FORWARD_ORDER = (
    "p0", "p1", "p2", "p3", "s0", "s1", "t0", "s2", "t1", "s3", "t2", "d0", "d1", "x0", "t3", "d2", "x1", "d3", "x2", "x3",
)
BACKWARD_ORDER = (
    "b0", "b1", "b2", "c0", "b3", "c1", "c2", "i0", "c3", "i1", "l0",
)
VMEM_LIMIT = 24 * 2**20
FIRST_LIMIT = 54 * 2**20
FIRST_CUTS = 8
BLOCK_ORDER = ((3, 2, 1, 0), (3, 0, 2, 1), (0, 3, 1, 2), (0, 1, 2, 3))
OWN_EXPERT, LEAF, Z, PEER, PEER_EXPERT, ORDER = 0, 1, 2, 3, 7, 11
BF16 = jnp.bfloat16
F32 = jnp.float32


def dot_nn(left, right):
    return lax.dot_general(left, right, (((1,), (0,)), ((), ())), preferred_element_type=F32)


def halves(value):
    high = value.astype(BF16)
    return high, (value - high.astype(F32)).astype(BF16)


def stacked_halves(value):
    high, low = halves(value)
    return jnp.concatenate([high.astype(F32), low.astype(F32)], axis=0).astype(BF16)


def fold(product):
    rows = product.shape[0] // 2
    return product[:rows] + product[rows:]


def iota(shape, axis):
    return lax.broadcasted_iota(jnp.int32, shape, axis)


def project_kernel(block, offset, n, context_ref, weight_ref, resid_ref, *rest):
    out_ref = rest[-1]
    rows = context_ref.shape[0]
    part = dot_nn(context_ref[...], weight_ref[...])
    share = jnp.where(n[Z] == block, resid_ref[offset : offset + rows, :].astype(F32), 0.0)
    out_ref[:rows, :] = (part + share).astype(BF16)


def first_kernel(experts, ids_ref, context_hbm, weight_hbm, resid_hbm, out_ref, context_ref, weight_ref, resid_ref, sems):
    rows, heads = context_ref.shape
    cuts = sems.shape[0] - 2
    step = heads // cuts
    copies = []
    for i in range(cuts):
        at = pl.ds(i * step, step)
        copies.append(pltpu.make_async_copy(weight_hbm.at[at], weight_ref.at[at], sems.at[i]))
    context_copy = pltpu.make_async_copy(context_hbm.at[pl.ds(0, rows)], context_ref, sems.at[cuts])
    resid_copy = pltpu.make_async_copy(resid_hbm.at[pl.ds(0, rows)], resid_ref, sems.at[cuts + 1])
    context_copy.start()
    for copy in copies:
        copy.start()
    resid_copy.start()
    z = lax.axis_index("tensor")
    mask = jnp.zeros((experts, rows), F32)
    for k in range(ids_ref.shape[0]):
        mask += (ids_ref[k : k + 1, :] == iota((experts, rows), 0)).astype(F32)
    out_ref[rows:, :] = jnp.zeros((experts, out_ref.shape[1]), BF16)
    for block in range(4):
        out_ref[rows:, block * rows : (block + 1) * rows] = jnp.where(z == block, mask, 0.0).astype(BF16)
    context_copy.wait()
    part = None
    for i, copy in enumerate(copies):
        copy.wait()
        at = slice(i * step, (i + 1) * step)
        term = dot_nn(context_ref[:, at], weight_ref[at, :])
        part = term if part is None else part + term
    resid_copy.wait()
    share = jnp.where(z == 0, resid_ref[...].astype(F32), 0.0)
    out_ref[:rows, :] = (part + share).astype(BF16)


def add_kernel(n, left_ref, right_ref, _, out_ref):
    out_ref[...] = (left_ref[...].astype(F32) + right_ref[...].astype(F32)).astype(BF16)


def dispatch_kernel(capacity, block, pieces, n, *refs):
    inner_refs, back_refs, refs = refs[:pieces], refs[pieces : 2 * pieces], refs[2 * pieces :]
    gain_ref, router_ref, token_ref, *refs = refs
    rows = token_ref.shape[1]
    outs = refs[-7:] if block == 0 else refs[-6:]
    row_refs, t_ref, place_ref = outs[:4], outs[4], outs[5]
    experts, width = router_ref.shape
    x = jnp.concatenate(
        [
            jnp.where(n[LEAF] == 1, back[...].astype(F32), inner[...].astype(F32))
            for inner, back in zip(inner_refs, back_refs)
        ],
        axis=0,
    )
    if block == 0:
        wide = x[rows:, : 4 * rows].astype(BF16)
        outs[6][...] = wide
        x = x[:rows]
    else:
        wide = refs[0][...]
    mask = wide[:, block * rows : (block + 1) * rows]
    t_ref[0] = x.astype(BF16)
    scale = lax.rsqrt(jnp.mean(x * x, axis=1, keepdims=True) + EPSILON)
    normed = (x * scale * gain_ref[...]).astype(BF16)
    logits = contract_last(router_ref[...], normed)
    chosen = mask.astype(F32) > 0.5
    exp_chosen = jnp.where(chosen, jnp.exp(jnp.where(chosen, logits, 0.0)), 0.0)
    gates = exp_chosen / jnp.sum(exp_chosen, axis=0, keepdims=True)
    earlier = (iota((rows, rows), 0) < iota((rows, rows), 1)).astype(F32).astype(BF16)
    position = jnp.where(chosen, dot_nn(mask, earlier), -1.0)
    gate_high, gate_low = halves(gates)
    inverse = token_ref[1:2, :]
    inv_high = inverse.astype(BF16).astype(F32)
    inv_mid = (inverse - inv_high).astype(BF16).astype(F32)
    inv_low = inverse - inv_high - inv_mid
    slot_row = iota((8, rows), 0)
    token_part = jnp.where(
        slot_row == 0,
        token_ref[0:1, :],
        jnp.where(slot_row == 1, inv_high, jnp.where(slot_row == 2, inv_mid, jnp.where(slot_row == 3, inv_low, 0.0))),
    )
    extra = jnp.concatenate(
        [
            gate_high.astype(F32),
            gate_low.astype(F32),
            token_part,
            jnp.zeros((ROW_EXTRA - 2 * experts - 8, rows), F32),
        ],
        axis=0,
    ).astype(BF16)
    expert_row = iota((experts, rows), 0)
    slot = iota((capacity, rows), 0).astype(F32)
    picks = []
    for way in range(4):
        own = jnp.sum(jnp.where(expert_row == n[PEER_EXPERT + way], position, 0.0), axis=0, keepdims=True)
        picks.append((slot == own).astype(F32))
    picked = jnp.concatenate(picks, axis=0)
    place_ref[0] = jnp.transpose(picked).astype(BF16)
    picked = picked.astype(BF16)
    sent = dot_nn(picked, normed)
    sent_extra = contract_last(picked, extra)
    for way in range(4):
        at = slice(way * capacity, (way + 1) * capacity)
        row_refs[way][:, :width] = sent[at].astype(BF16)
        row_refs[way][:, width:] = sent_extra[at].astype(BF16)


def expert_kernel(n, r0, r1, r2, r3, gate_ref, up_ref, *refs):
    pooled_ref, hidden_ref, a_ref, b_ref, info_ref, x_ref, weight_ref = refs[-7:]
    width = gate_ref.shape[0]
    experts = 16

    @pl.when(pl.program_id(0) == 0)
    def start():
        x_ref[...] = jnp.concatenate([r[:, :width].astype(F32) for r in (r0, r1, r2, r3)], axis=0).astype(BF16)
        extra = jnp.concatenate([r[:, width:].astype(F32) for r in (r0, r1, r2, r3)], axis=0).astype(BF16)
        own = n[OWN_EXPERT]

        def mixer(source, goal):
            gates = (goal < experts) & ((source == goal) | (source == goal + experts))
            sequence = (goal == experts) & (source == 2 * experts)
            inverse = (goal == experts + 1) & (source > 2 * experts) & (source < 2 * experts + 4)
            gate = (goal == experts + 2) & ((source == own) | (source == own + experts))
            return (gates | sequence | inverse | gate).astype(F32).astype(BF16)

        square = (ROW_EXTRA, ROW_EXTRA)
        info = dot_nn(extra, mixer(iota(square, 0), iota(square, 1)))
        info_ref[0] = info
        turned = contract_last(mixer(iota(square, 1), iota(square, 0)), extra)
        sequence = turned[experts : experts + 1]
        weight = turned[experts + 1 : experts + 2] * turned[experts + 2 : experts + 3]
        pool = jnp.where(iota((pooled_ref.shape[0], extra.shape[0]), 0).astype(F32) == sequence, weight, 0.0)
        weight_ref[...] = stacked_halves(pool)

    x = x_ref[...]
    pre_gate = dot_nn(x, gate_ref[...])
    pre_up = dot_nn(x, up_ref[...])
    sigmoid = 1.0 / (1.0 + jnp.exp(-pre_gate))
    silu = pre_gate * sigmoid
    hidden = (silu * pre_up).astype(BF16)
    hidden_ref[0] = hidden
    a_ref[0] = pre_up * sigmoid * (1.0 + pre_gate * (1.0 - sigmoid))
    b_ref[0] = silu
    pooled_ref[...] = fold(dot_nn(weight_ref[...], hidden))


def sum_kernel(n, p0, p1, p2, p3, _, out_ref):
    near = p0[...].astype(F32) + p1[...].astype(F32)
    out_ref[...] = (near + (p2[...].astype(F32) + p3[...].astype(F32))).astype(BF16)


def embed_kernel(n, p0, p1, p2, p3, down_ref, t_ref, token_ref, _, o0, o1, o2, o3, part_ref):
    pooled = p0[...] + p1[...] + p2[...] + p3[...]
    part = fold(dot_nn(stacked_halves(pooled), down_ref[...]))
    sequences = part.shape[0]
    own = jnp.where(
        iota((sequences, t_ref.shape[1]), 0).astype(F32) == token_ref[0:1, :], token_ref[1:2, :], 0.0
    )
    part_ref[...] = part + fold(dot_nn(stacked_halves(own), t_ref[0]))
    rows = o0.shape[0]
    for way, out in enumerate((o0, o1, o2, o3)):
        out[...] = part_ref[pl.ds(pl.multiple_of(n[PEER + way] * rows, rows), rows), :].astype(out.dtype)


def contrast_kernel(n, q0, q1, q2, q3, down_ref, _, grad_ref, hidden_grad_ref, loss_ref, all_ref):
    rows = q0.shape[0]
    for way, part in enumerate((q0, q1, q2, q3)):
        all_ref[pl.ds(pl.multiple_of(n[PEER + way] * rows, rows), rows), :] = part[...].astype(F32)
    embedded = all_ref[...].astype(BF16)
    count = embedded.shape[0]
    pairs = count // 2
    products = contract_last(embedded, embedded)
    row, column = iota((count, count), 0), iota((count, count), 1)
    squares = jnp.where(row == column, products, 0.0)
    inverse = 1.0 / jnp.sqrt(jnp.sum(squares, axis=1, keepdims=True) + EPSILON)
    inverse_row = 1.0 / jnp.sqrt(jnp.sum(squares, axis=0, keepdims=True) + EPSILON)
    cosines = products * inverse * inverse_row
    scores = cosines / SOFTMAX_WARMTH
    is_pair = (row % 2 == 0) & (column % 2 == 1)
    matched = is_pair & (column == row + 1)
    exp_scores = jnp.where(is_pair, jnp.exp(jnp.where(is_pair, scores, 0.0)), 0.0)
    row_total = jnp.sum(exp_scores, axis=1, keepdims=True)
    is_query = iota((count, 1), 0) % 2 == 0
    row_total = jnp.where(is_query, row_total, 1.0)
    own_score = jnp.sum(jnp.where(matched, scores, 0.0), axis=1, keepdims=True)
    terms = jnp.where(is_query, jnp.log(row_total) - own_score, 0.0)
    loss_ref[0] = jnp.sum(terms) / pairs
    dscore = (exp_scores / row_total - jnp.where(matched, 1.0, 0.0)) * (LOSS_SCALE / pairs)
    both = dscore + jnp.transpose(dscore)
    both = both / SOFTMAX_WARMTH
    radial = jnp.sum(both * cosines, axis=1, keepdims=True)
    mixer = (both - jnp.where(row == column, radial, 0.0)) * inverse * inverse_row
    grad = fold(dot_nn(stacked_halves(mixer), embedded))
    grad_ref[...] = grad
    hidden_grad_ref[...] = fold(contract_last(stacked_halves(grad), down_ref[...]))


def backward_kernel(capacity, n, a_ref, b_ref, hidden_ref, info_ref, dh_ref, gate_ref, up_ref, router_ref, _, o0, o1, o2, o3, dgate_ref, dup_ref, dlog_ref):
    experts = 16

    @pl.when(pl.program_id(0) == 0)
    def start():
        info = info_ref[0]
        slots = info.shape[0]
        sequence = info[:, experts : experts + 1]
        weight = info[:, experts + 1 : experts + 2] * info[:, experts + 2 : experts + 3]
        member = (iota((slots, dh_ref.shape[0]), 1).astype(F32) == sequence).astype(F32).astype(BF16)
        high, low = halves(dh_ref[...])
        dhidden = weight * (dot_nn(member, high) + dot_nn(member, low))
        dgate_ref[...] = (dhidden * a_ref[0]).astype(BF16)
        dup_ref[...] = (dhidden * b_ref[0]).astype(BF16)
        moved = jnp.sum(dhidden * hidden_ref[0].astype(F32), axis=1, keepdims=True)
        lane = iota((slots, ROW_EXTRA), 1)
        gates = jnp.where(lane < experts, info, 0.0)
        dlog_ref[...] = (moved * (jnp.where(lane == n[OWN_EXPERT], 1.0, 0.0) - gates)).astype(BF16)

    total = (
        dot_nn(dgate_ref[...], gate_ref[...])
        + dot_nn(dup_ref[...], up_ref[...])
        + dot_nn(dlog_ref[...], router_ref[...])
    )
    for way, out in enumerate((o0, o1, o2, o3)):
        out[...] = total[way * capacity : (way + 1) * capacity].astype(BF16)


def turn_kernel(n, weight_ref, _, out_ref):
    out_ref[...] = jnp.transpose(weight_ref[...])


def combine_kernel(n, place_ref, r0, r1, r2, r3, _, out_ref, narrow_ref):
    rows = jnp.concatenate([r[...].astype(F32) for r in (r0, r1, r2, r3)], axis=0).astype(BF16)
    total = dot_nn(place_ref[0], rows)
    out_ref[...] = total
    narrow_ref[...] = total.astype(BF16)


def spread_kernel(n, t_ref, grad_ref, token_ref, _, out_ref, scale_ref):
    x = t_ref[0].astype(F32)
    scale = lax.rsqrt(jnp.mean(x * x, axis=1, keepdims=True) + EPSILON)
    spread = jnp.where(iota((grad_ref.shape[0], x.shape[0]), 0).astype(F32) == token_ref[0:1, :], 1.0, 0.0)
    spread = jnp.transpose(spread).astype(BF16)
    inverse = jnp.transpose(token_ref[...])[:, 1:2]
    high, low = halves(grad_ref[...])
    out_ref[...] = inverse * (dot_nn(spread, high) + dot_nn(spread, low))
    scale_ref[...] = jnp.broadcast_to(scale, scale_ref.shape)


def finish_kernel(n, t_ref, gain_ref, dresid_ref, scale_ref, own_ref, r4, r5, r6, _, out_ref):
    x = t_ref[0].astype(F32)
    scale = scale_ref[:, :1]
    dnormed = own_ref[...] + r4[...].astype(F32) + r5[...].astype(F32) + r6[...].astype(F32)
    gained = dnormed * gain_ref[...]
    pull = (scale * scale * scale) * jnp.mean(gained * x, axis=1, keepdims=True)
    out_ref[...] = (dresid_ref[...] + scale * gained - x * pull).astype(BF16)


class Chain:
    def __init__(self, numbers, first):
        self.numbers = numbers
        self.last = first

    def __call__(self, kernel, ins, outs, *, steps=1, kept=(), scratch=(), flops=0):
        args, in_specs = zip(*ins)
        args, in_specs = list(args), list(in_specs)
        shapes, out_specs = zip(*outs)
        aliases = {}
        for at, array in kept:
            aliases[1 + len(args)] = at
            args.append(array)
            in_specs.append(pl.BlockSpec(memory_space=pl.ANY))
        args.append(self.last)
        in_specs.append(pl.BlockSpec(memory_space=pl.ANY))
        result = pl.pallas_call(
            kernel,
            out_shape=list(shapes),
            grid_spec=pltpu.PrefetchScalarGridSpec(
                num_scalar_prefetch=1,
                grid=(steps,),
                in_specs=in_specs,
                out_specs=list(out_specs),
                scratch_shapes=scratch,
            ),
            input_output_aliases=aliases,
            compiler_params=pltpu.CompilerParams(vmem_limit_bytes=VMEM_LIMIT),
            cost_estimate=pl.CostEstimate(flops=1, bytes_accessed=1, transcendentals=0),
        )(self.numbers, *args)
        self.last = result[0]
        return result


def fixed(shape):
    return pl.BlockSpec(shape, lambda j, n: (0,) * len(shape))


def whole(array):
    return array, pl.BlockSpec(memory_space=pltpu.VMEM)


def fast_body(context, o_weight, resid, norm_gain, router, gate_weight, up_weight, down_weight, expert_ids, lengths):
    e = lax.axis_index("expert")
    z = lax.axis_index("tensor")
    rows, width = resid.shape
    heads = context.shape[1]
    experts = router.shape[1]
    top = expert_ids.shape[1]
    seq_count = lengths.shape[1]
    sequences = 4 * seq_count
    hidden_width = gate_weight.shape[2]
    capacity = max(2, rows * top * 5 // (4 * experts))
    slots = 4 * capacity
    leaf = (z == 0) | (z == 3)
    ways = e ^ jnp.arange(4, dtype=jnp.int32)
    numbers = jnp.concatenate(
        [
            jnp.stack([e * 4 + z, leaf.astype(jnp.int32), z]),
            ways,
            ways * 4 + z,
            jnp.asarray(BLOCK_ORDER, jnp.int32)[z],
        ]
    ).astype(jnp.int32)
    gate_w, up_w, down_w = gate_weight[0], up_weight[0], down_weight[0]
    gain = norm_gain.reshape(1, width)
    router_turned = router.T
    router_rows = jnp.pad(router_turned, ((0, ROW_EXTRA - experts), (0, 0)))

    def along_z(value, pairs):
        return lax.ppermute(value, "tensor", pairs)

    def swap_z(value, bits):
        return lax.ppermute(value, "tensor", [(i, i ^ bits) for i in range(4)])

    def swap_e(value, bits):
        return lax.ppermute(value, "expert", [(i, i ^ bits) for i in range(4)])

    seq_lengths = lengths[0]
    seq_ends = jnp.cumsum(seq_lengths)
    places = jnp.arange(4 * rows, dtype=jnp.int32)
    after = places[None, :] >= seq_ends[:, None]
    seq_local = jnp.sum(after.astype(jnp.int32), axis=0)
    token_len = jnp.sum(
        jnp.where(seq_local[None, :] == jnp.arange(seq_count, dtype=jnp.int32)[:, None], seq_lengths[:, None], 0), axis=0
    )
    token_info = jnp.concatenate(
        [
            (seq_local + e * seq_count).astype(F32)[None],
            (1.0 / token_len.astype(F32))[None],
            jnp.zeros((6, 4 * rows), F32),
        ],
        axis=0,
    )

    chain = Chain(numbers, gain)
    shape = jax.ShapeDtypeStruct
    tile = 512
    pieces = []
    for c, cuts in enumerate(PIECES):
        pieces += [(c, i * (rows // cuts), rows // cuts) for i in range(cuts)]
    count = len(pieces)
    parts, half, inner, back, from_leaf, from_inner = ([None] * count for _ in range(6))
    received, pools, shared, kept_rows, kept_acts = [None] * 4, [None] * 4, {}, {}, {}

    def first_hop(i):
        c, offset, size = pieces[i]
        if i == 0:
            away = pl.BlockSpec(memory_space=pl.ANY)
            near = pl.BlockSpec(memory_space=pltpu.VMEM)
            chain.last = parts[0] = pl.pallas_call(
                functools.partial(first_kernel, experts),
                out_shape=shape((size + experts, width), BF16),
                in_specs=[near, away, away, away],
                out_specs=near,
                scratch_shapes=[
                    pltpu.VMEM((size, heads), BF16),
                    pltpu.VMEM((heads, width), BF16),
                    pltpu.VMEM((size, width), BF16),
                    pltpu.SemaphoreType.DMA((FIRST_CUTS + 2,)),
                ],
                compiler_params=pltpu.CompilerParams(vmem_limit_bytes=FIRST_LIMIT),
            )(expert_ids.T, context, o_weight, resid)
            from_leaf[0] = along_z(parts[0], LEAVES_IN)
            return
        at = (c * rows + offset) // size
        ins = [
            (context, pl.BlockSpec((size, heads), lambda j, n: (at, 0))),
            whole(o_weight),
            whole(resid),
        ]
        (parts[i],) = chain(
            functools.partial(project_kernel, c, offset),
            ins,
            [(shape((size, width), BF16), fixed((size, width)))],
            flops=2 * size * heads * width,
        )
        from_leaf[i] = along_z(parts[i], LEAVES_IN)

    def add(left, right):
        like = shape(right.shape, BF16)
        return chain(add_kernel, [whole(left), whole(right)], [(like, fixed(like.shape))], flops=left.size)[0]

    def second_hop(i):
        half[i] = add(parts[i], from_leaf[i])
        from_inner[i] = along_z(half[i], INNER_SWAP)

    def third_hop(i):
        inner[i] = add(half[i], from_inner[i])
        back[i] = along_z(inner[i], LEAVES_OUT)

    def dispatch(c):
        mine = [i for i in range(count) if pieces[i][0] == c]
        ins = [whole(inner[i]) for i in mine] + [whole(back[i]) for i in mine]
        ins += [
            whole(gain),
            whole(router_turned),
            (token_info, pl.BlockSpec((8, rows), lambda j, n: (0, c))),
        ]
        if c > 0:
            ins.append(whole(shared["mask"]))
        sent_shape = (capacity, width + ROW_EXTRA)
        outs = [(shape(sent_shape, BF16), fixed(sent_shape))] * 4
        for size in ((rows, width), (rows, slots)):
            outs.append((shape((4,) + size, BF16), pl.BlockSpec((1,) + size, lambda j, n: (c, 0, 0))))
        if c == 0:
            outs.append((shape((experts, 4 * rows), BF16), fixed((experts, 4 * rows))))
        result = chain(
            functools.partial(dispatch_kernel, capacity, c, len(mine)),
            ins,
            outs,
            kept=sorted(kept_rows.items()),
            flops=2 * slots * rows * width,
        )
        kept_rows.update({4: result[4], 5: result[5]})
        if c == 0:
            shared["mask"] = result[6]
        received[c] = [result[0]] + [swap_e(result[way], way) for way in (1, 2, 3)]

    def expert(c):
        tile = hidden_width
        block = lambda size: pl.BlockSpec((1, slots, size), lambda j, n: (c, 0, j))
        outs = [(shape((sequences, hidden_width), F32), pl.BlockSpec((sequences, tile), lambda j, n: (0, j)))]
        outs += [(shape((4, slots, hidden_width), kind), block(tile)) for kind in (BF16, F32, F32)]
        outs.append((shape((4, slots, ROW_EXTRA), F32), pl.BlockSpec((1, slots, ROW_EXTRA), lambda j, n: (c, 0, 0))))
        weight_spec = pl.BlockSpec(memory_space=pltpu.VMEM)
        result = chain(
            expert_kernel,
            [whole(r) for r in received[c]] + [(gate_w, weight_spec), (up_w, weight_spec)],
            outs,
            steps=hidden_width // tile,
            kept=sorted(kept_acts.items()),
            scratch=[pltpu.VMEM((slots, width), BF16), pltpu.VMEM((2 * sequences, slots), BF16)],
            flops=4 * slots * width * hidden_width,
        )
        pools[c] = result[0]
        kept_acts.update({i: result[i] for i in (1, 2, 3, 4)})

    turned = [None, None]

    def turn(k):
        size = (hidden_width, width)
        (turned[k],) = chain(turn_kernel, [whole((gate_w, up_w)[k])], [(shape(size, BF16), fixed(size))])

    calls = {"p": first_hop, "s": second_hop, "t": third_hop, "d": dispatch, "x": expert}
    for step in FORWARD_ORDER:
        calls[step[0]](int(step[1:]))

    total_all, place_all = kept_rows[4], kept_rows[5]
    hidden_all, a_all, b_all, info_all = (kept_acts[i] for i in (1, 2, 3, 4))
    own_rows = (total_all, pl.BlockSpec((1, rows, width), lambda j, n: (n[Z], 0, 0)))
    own_tokens = (token_info, pl.BlockSpec((8, rows), lambda j, n: (0, n[Z])))
    seq_size = (seq_count, width)
    quarters = chain(
        embed_kernel,
        [whole(pool) for pool in pools] + [whole(down_w), own_rows, own_tokens],
        [(shape(seq_size, kind), fixed(seq_size)) for kind in (F32, BF16, BF16, BF16)],
        scratch=[pltpu.VMEM((sequences, width), F32)],
        flops=4 * sequences * hidden_width * width,
    )

    def add_four(values):
        return chain(sum_kernel, [whole(v) for v in values], [(shape(seq_size, BF16), fixed(seq_size))])[0]

    parts_e = [quarters[0]] + [swap_e(quarters[way], way) for way in (1, 2, 3)]
    turn(0)
    mine = add_four(parts_e)
    parts_z = [mine] + [swap_z(mine, way) for way in (1, 2, 3)]
    turn(1)
    mine = add_four(parts_z)
    gathered = [mine] + [swap_e(mine, way) for way in (1, 2, 3)]
    sizes = ((sequences, width), (sequences, hidden_width))
    dembedded, hidden_grad, loss = chain(
        contrast_kernel,
        [whole(piece) for piece in gathered] + [whole(down_w)],
        [(shape(size, F32), fixed(size)) for size in sizes]
        + [(shape((1,), F32), pl.BlockSpec(memory_space=pltpu.SMEM))],
        scratch=[pltpu.VMEM((sequences, width), F32)],
        flops=4 * sequences * hidden_width * width,
    )
    returned, sums = [None] * 4, [None] * 4

    def backward(k):
        tile = width
        block = lambda size: pl.BlockSpec((1, slots, size), lambda j, n: (n[ORDER + k], 0, 0))
        grads = chain(
            functools.partial(backward_kernel, capacity),
            [
                (a_all, block(hidden_width)),
                (b_all, block(hidden_width)),
                (hidden_all, block(hidden_width)),
                (info_all, block(ROW_EXTRA)),
                whole(hidden_grad),
                whole(turned[0]),
                whole(turned[1]),
                (router_rows, pl.BlockSpec((ROW_EXTRA, tile), lambda j, n: (0, j))),
            ],
            [(shape((capacity, width), BF16), pl.BlockSpec((capacity, tile), lambda j, n: (0, j)))] * 4,
            steps=width // tile,
            scratch=[
                pltpu.VMEM((slots, hidden_width), BF16),
                pltpu.VMEM((slots, hidden_width), BF16),
                pltpu.VMEM((slots, ROW_EXTRA), BF16),
            ],
            flops=4 * slots * width * hidden_width,
        )
        returned[k] = [grads[0]] + [swap_e(grads[way], way) for way in (1, 2, 3)]

    def combine(k):
        sums[k] = chain(
            combine_kernel,
            [(place_all, pl.BlockSpec((1, rows, slots), lambda j, n: (n[ORDER + k], 0, 0)))]
            + [whole(r) for r in returned[k]],
            [(shape((rows, width), kind), fixed((rows, width))) for kind in (F32, BF16)],
            flops=2 * slots * rows * width,
        )

    hops = {}

    def combined(k):
        combine(k)
        if k < 3:
            hops[k] = along_z(sums[k][1], LEAVES_IN)

    def inner_hop(k):
        total = add(sums[(0, 2)[k]][0], hops[(0, 1)[k]])
        hops[3 + k] = along_z(total, INNER_SWAP)

    def last_hop(_):
        hops[5] = along_z(add(sums[1][0], hops[3]), LEAVES_OUT)

    calls = {"b": backward, "c": combined, "i": inner_hop, "l": last_hop}
    for step in BACKWARD_ORDER:
        calls[step[0]](int(step[1:]))
    dresid, scales = chain(
        spread_kernel,
        [own_rows, whole(dembedded), own_tokens],
        [(shape((rows, width), F32), fixed((rows, width))), (shape((rows, 128), F32), fixed((rows, 128)))],
    )
    (grad,) = chain(
        finish_kernel,
        [own_rows, whole(gain), whole(dresid), whole(scales)]
        + [whole(value) for value in (sums[3][0], hops[2], hops[4], hops[5])],
        [(shape((rows, width), BF16), fixed((rows, width)))],
        flops=4 * rows * sequences * width,
    )
    return loss, grad


def solution(mesh):
    shape = dict(mesh.shape)
    part_body = fast_body if (shape["expert"], shape["tensor"]) == (4, 4) else body
    in_specs = (
        P(("groups", "expert"), "tensor"),
        P("tensor", None),
        P(("groups", "expert", "tensor"), None),
        P(),
        P(),
        P(("expert", "tensor"), None, None),
        P(("expert", "tensor"), None, None),
        P(("expert", "tensor"), None, None),
        P(("groups", "expert", "tensor"), None),
        P(("groups", "expert"), None),
    )
    out_specs = (P("groups"), P(("groups", "expert", "tensor"), None))
    return jax.shard_map(part_body, mesh=mesh, in_specs=in_specs, out_specs=out_specs, check_vma=False)
```

```python
import functools

import jax
import jax.numpy as jnp
from jax import lax
from jax.experimental import pallas as pl
from jax.experimental.pallas import tpu as pltpu
from jax.sharding import PartitionSpec as P

EPSILON = 1e-06
SOFTMAX_WARMTH = 0.05
LOSS_SCALE = 32768.0
EXACT_PRECISION = lax.Precision.HIGHEST


def slot_positions(flat_ids, expert_total):
    onehot = (flat_ids[..., None] == jnp.arange(expert_total, dtype=jnp.int32)).astype(jnp.int32)
    before = jnp.cumsum(onehot, axis=-2) - onehot
    return jnp.sum(before * onehot, axis=-1)


def contract_last(left, right):
    return lax.dot_general(
        left, right, (((1,), (1,)), ((), ())), preferred_element_type=jnp.float32
    )


def contrast(embedded):
    pair_count = embedded.shape[0] // 2
    norms = jnp.sqrt(jnp.sum(embedded * embedded, axis=1, keepdims=True) + EPSILON)
    unit_rows = embedded / norms
    query_rows = unit_rows[0::2]
    passage_rows = unit_rows[1::2]
    similarity_scores = (
        jnp.dot(query_rows, passage_rows.T, precision=EXACT_PRECISION) / SOFTMAX_WARMTH
    )
    exp_scores = jnp.exp(similarity_scores)
    row_total = jnp.sum(exp_scores, axis=1, keepdims=True)
    loss_value = jnp.mean(jnp.log(row_total[:, 0]) - jnp.diagonal(similarity_scores))
    score_gradient = (
        exp_scores / row_total - jnp.eye(pair_count, dtype=similarity_scores.dtype)
    ) * (LOSS_SCALE / pair_count)
    query_gradient = (
        jnp.dot(score_gradient, passage_rows, precision=EXACT_PRECISION) / SOFTMAX_WARMTH
    )
    passage_gradient = (
        jnp.dot(score_gradient.T, query_rows, precision=EXACT_PRECISION) / SOFTMAX_WARMTH
    )
    dunit_rows = jnp.stack([query_gradient, passage_gradient], axis=1).reshape(embedded.shape)
    radial = jnp.sum(unit_rows * dunit_rows, axis=1, keepdims=True)
    return (loss_value, (dunit_rows - unit_rows * radial) / norms)


def body(
    context,
    o_weight,
    resid,
    norm_gain,
    router,
    gate_weight,
    up_weight,
    down_weight,
    expert_ids,
    lengths,
):
    expert_count = lax.axis_size("expert")
    tensor_count = lax.axis_size("tensor")
    device_count = expert_count * tensor_count
    expert_index = lax.axis_index("expert")
    tensor_index = lax.axis_index("tensor")
    local_rows, model_width = resid.shape
    expert_total = router.shape[1]
    top_count = expert_ids.shape[1]
    seq_count = lengths.shape[1]
    seq_total = seq_count * expert_count
    capacity = max(2, local_rows * top_count * 5 // (4 * expert_total))
    attention_out = lax.psum_scatter(
        jnp.dot(context, o_weight, preferred_element_type=jnp.float32).astype(jnp.bfloat16),
        "tensor",
        scatter_dimension=0,
        tiled=True,
    ).astype(jnp.float32)
    resid_mid = resid.astype(jnp.float32) + attention_out
    rms_scale = lax.rsqrt(jnp.mean(resid_mid * resid_mid, axis=1, keepdims=True) + EPSILON)
    normed = (resid_mid * rms_scale * norm_gain).astype(jnp.bfloat16)
    logits = jnp.dot(normed, router, preferred_element_type=jnp.float32)
    expert_onehot = (expert_ids[:, :, None] == jnp.arange(expert_total, dtype=jnp.int32)).astype(
        jnp.float32
    )
    chosen = jnp.sum(logits[:, None, :] * expert_onehot, axis=2)
    exp_chosen = jnp.exp(chosen)
    gate_probs = exp_chosen / jnp.sum(exp_chosen, axis=1, keepdims=True)
    flat_ids = expert_ids.reshape(local_rows * top_count)
    target = flat_ids * capacity + slot_positions(flat_ids, expert_total)

    def move_rows(blocks):
        return lax.all_to_all(blocks, ("expert", "tensor"), split_axis=0, concat_axis=0, tiled=True)

    seq_lengths = lengths[0]
    seq_ends = jnp.cumsum(seq_lengths)
    seq_starts = seq_ends - seq_lengths
    positions = tensor_index * local_rows + jnp.arange(local_rows, dtype=jnp.int32)
    member = (
        (positions[None, :] >= seq_starts[:, None]) & (positions[None, :] < seq_ends[:, None])
    ).astype(jnp.float32)
    tok_len = jnp.sum(member * seq_lengths[:, None].astype(jnp.float32), axis=0)
    repeated = jnp.broadcast_to(normed[:, None, :], (local_rows, top_count, model_width)).reshape(
        local_rows * top_count, model_width
    )
    buffer = (
        jnp.zeros((expert_total * capacity, model_width), jnp.bfloat16).at[target].set(repeated)
    )
    received = move_rows(buffer.reshape(device_count, capacity, model_width)).reshape(
        device_count * capacity, model_width
    )
    pre_gate = jnp.dot(received, gate_weight[0], preferred_element_type=jnp.float32)
    pre_up = jnp.dot(received, up_weight[0], preferred_element_type=jnp.float32)
    hidden = (jax.nn.silu(pre_gate) * pre_up).astype(jnp.bfloat16)
    expert_rows = jnp.dot(hidden, down_weight[0], preferred_element_type=jnp.float32).astype(
        jnp.bfloat16
    )
    seq_local = jnp.dot(jnp.arange(seq_count, dtype=jnp.float32), member, precision=EXACT_PRECISION)
    seq_global = seq_local + (expert_index * seq_count).astype(jnp.float32)
    info_rows = jnp.stack(
        [
            gate_probs,
            jnp.broadcast_to(seq_global[:, None], (local_rows, top_count)),
            jnp.broadcast_to(tok_len[:, None], (local_rows, top_count)),
        ],
        axis=2,
    ).reshape(local_rows * top_count, 3)
    info_init = jnp.zeros((expert_total * capacity, 3), jnp.float32).at[:, 2].set(1.0)
    info_buffer = info_init.at[target].set(info_rows).reshape(device_count, capacity, 3)
    slot_data = lax.all_to_all(
        info_buffer, ("expert", "tensor"), split_axis=0, concat_axis=0, tiled=True
    ).reshape(device_count * capacity, 3)
    slot_gate = slot_data[:, 0:1]
    slot_seq = slot_data[:, 1].astype(jnp.int32)
    slot_len = slot_data[:, 2:3]
    slot_onehot = (slot_seq[:, None] == jnp.arange(seq_total, dtype=jnp.int32)).astype(jnp.float32)
    out_float = expert_rows.astype(jnp.float32)
    expert_part = lax.dot_general(
        slot_onehot,
        slot_gate * out_float / slot_len,
        (((0,), (0,)), ((), ())),
        precision=EXACT_PRECISION,
        preferred_element_type=jnp.float32,
    )
    partial_value = jnp.dot(member, resid_mid / tok_len[:, None], precision=EXACT_PRECISION)
    placed = lax.dynamic_update_slice_in_dim(
        expert_part,
        lax.dynamic_slice_in_dim(expert_part, expert_index * seq_count, seq_count, 0)
        + partial_value,
        expert_index * seq_count,
        0,
    )
    embedded = lax.psum(placed, ("expert", "tensor"))
    loss_value, dembedded = contrast(embedded)
    own_rows = lax.dynamic_slice_in_dim(
        dembedded, expert_index * seq_count, seq_count, 0
    ) / seq_lengths[:, None].astype(jnp.float32)
    dresid_out = lax.dot_general(
        member,
        own_rows,
        (((0,), (0,)), ((), ())),
        precision=EXACT_PRECISION,
        preferred_element_type=jnp.float32,
    )
    slot_dresid = jnp.dot(slot_onehot, dembedded, precision=EXACT_PRECISION) / slot_len
    received_grad = (slot_gate * slot_dresid).astype(jnp.bfloat16)
    slot_dgate = jnp.sum(slot_dresid * out_float, axis=1)
    returned = lax.all_to_all(
        slot_dgate.reshape(device_count, capacity),
        ("expert", "tensor"),
        split_axis=0,
        concat_axis=0,
        tiled=True,
    )
    dgate_prob = returned.reshape(expert_total * capacity)[target].reshape(local_rows, top_count)
    dhidden = contract_last(received_grad, down_weight[0])
    gate_sigmoid = jax.nn.sigmoid(pre_gate)
    dpre_gate = (dhidden * pre_up * gate_sigmoid * (1.0 + pre_gate * (1.0 - gate_sigmoid))).astype(
        jnp.bfloat16
    )
    dpre_up = (dhidden * jax.nn.silu(pre_gate)).astype(jnp.bfloat16)
    dx_rows = (
        contract_last(dpre_gate, gate_weight[0]) + contract_last(dpre_up, up_weight[0])
    ).astype(jnp.bfloat16)
    dx_moe = jnp.sum(
        move_rows(dx_rows.reshape(device_count, capacity, model_width))
        .reshape(expert_total * capacity, model_width)[target]
        .astype(jnp.float32)
        .reshape(local_rows, top_count, model_width),
        axis=1,
    )
    dchosen = gate_probs * (dgate_prob - jnp.sum(gate_probs * dgate_prob, axis=1, keepdims=True))
    dlogits = jnp.sum(dchosen[:, :, None] * expert_onehot, axis=1).astype(jnp.bfloat16)
    dnormed = dx_moe + contract_last(dlogits, router)
    gain_grad = dnormed * norm_gain
    grad_resid = (
        dresid_out
        + rms_scale * gain_grad
        - resid_mid * rms_scale**3 * jnp.mean(gain_grad * resid_mid, axis=1, keepdims=True)
    )
    return (loss_value.reshape(1), grad_resid.astype(jnp.bfloat16))


ROW_EXTRA = 128
LEAVES_IN = ((0, 1), (3, 2))
INNER_SWAP = ((1, 2), (2, 1))
LEAVES_OUT = ((1, 0), (2, 3))
PIECES = (1, 1, 1, 1)
FORWARD_ORDER = (
    "p0", "p1", "p2", "p3", "s0", "s1", "t0", "s2", "t1", "s3", "t2", "d0", "d1", "x0", "t3", "d2", "x1", "d3", "x2", "x3",
)
BACKWARD_ORDER = (
    "b0", "b1", "b2", "c0", "b3", "c1", "c2", "i0", "c3", "i1", "l0",
)
VMEM_LIMIT = 24 * 2**20
FIRST_LIMIT = 54 * 2**20
FIRST_CUTS = 4
BLOCK_ORDER = ((3, 2, 1, 0), (3, 0, 2, 1), (0, 3, 1, 2), (0, 1, 2, 3))
OWN_EXPERT, LEAF, Z, PEER, PEER_EXPERT, ORDER = 0, 1, 2, 3, 7, 11
BF16 = jnp.bfloat16
F32 = jnp.float32


def dot_nn(left, right):
    return lax.dot_general(left, right, (((1,), (0,)), ((), ())), preferred_element_type=F32)


def halves(value):
    high = value.astype(BF16)
    return high, (value - high.astype(F32)).astype(BF16)


def stacked_halves(value):
    high, low = halves(value)
    return jnp.concatenate([high.astype(F32), low.astype(F32)], axis=0).astype(BF16)


def fold(product):
    rows = product.shape[0] // 2
    return product[:rows] + product[rows:]


def iota(shape, axis):
    return lax.broadcasted_iota(jnp.int32, shape, axis)


def project_kernel(block, offset, n, context_ref, weight_ref, resid_ref, *rest):
    out_ref = rest[-1]
    rows = context_ref.shape[0]
    part = dot_nn(context_ref[...], weight_ref[...])
    share = jnp.where(n[Z] == block, resid_ref[offset : offset + rows, :].astype(F32), 0.0)
    out_ref[:rows, :] = (part + share).astype(BF16)


def first_kernel(experts, ids_ref, context_hbm, weight_hbm, resid_hbm, out_ref, context_ref, weight_ref, resid_ref, sems):
    rows, heads = context_ref.shape
    cuts = sems.shape[0] - 2
    step = heads // cuts
    copies = []
    for i in range(cuts):
        at = pl.ds(i * step, step)
        copies.append(pltpu.make_async_copy(weight_hbm.at[at], weight_ref.at[at], sems.at[i]))
    context_copy = pltpu.make_async_copy(context_hbm.at[pl.ds(0, rows)], context_ref, sems.at[cuts])
    resid_copy = pltpu.make_async_copy(resid_hbm.at[pl.ds(0, rows)], resid_ref, sems.at[cuts + 1])
    context_copy.start()
    for copy in copies:
        copy.start()
    resid_copy.start()
    z = lax.axis_index("tensor")
    mask = jnp.zeros((experts, rows), F32)
    for k in range(ids_ref.shape[0]):
        mask += (ids_ref[k : k + 1, :] == iota((experts, rows), 0)).astype(F32)
    out_ref[rows:, :] = jnp.zeros((experts, out_ref.shape[1]), BF16)
    for block in range(4):
        out_ref[rows:, block * rows : (block + 1) * rows] = jnp.where(z == block, mask, 0.0).astype(BF16)
    context_copy.wait()
    part = None
    for i, copy in enumerate(copies):
        copy.wait()
        at = slice(i * step, (i + 1) * step)
        term = dot_nn(context_ref[:, at], weight_ref[at, :])
        part = term if part is None else part + term
    resid_copy.wait()
    share = jnp.where(z == 0, resid_ref[...].astype(F32), 0.0)
    out_ref[:rows, :] = (part + share).astype(BF16)


def add_kernel(n, left_ref, right_ref, _, out_ref):
    out_ref[...] = (left_ref[...].astype(F32) + right_ref[...].astype(F32)).astype(BF16)


def dispatch_kernel(capacity, block, pieces, n, *refs):
    inner_refs, back_refs, refs = refs[:pieces], refs[pieces : 2 * pieces], refs[2 * pieces :]
    gain_ref, router_ref, token_ref, *refs = refs
    rows = token_ref.shape[1]
    outs = refs[-7:] if block == 0 else refs[-6:]
    row_refs, t_ref, place_ref = outs[:4], outs[4], outs[5]
    experts, width = router_ref.shape
    x = jnp.concatenate(
        [
            jnp.where(n[LEAF] == 1, back[...].astype(F32), inner[...].astype(F32))
            for inner, back in zip(inner_refs, back_refs)
        ],
        axis=0,
    )
    if block == 0:
        wide = x[rows:, : 4 * rows].astype(BF16)
        outs[6][...] = wide
        x = x[:rows]
    else:
        wide = refs[0][...]
    mask = wide[:, block * rows : (block + 1) * rows]
    t_ref[0] = x.astype(BF16)
    scale = lax.rsqrt(jnp.mean(x * x, axis=1, keepdims=True) + EPSILON)
    normed = (x * scale * gain_ref[...]).astype(BF16)
    logits = contract_last(router_ref[...], normed)
    chosen = mask.astype(F32) > 0.5
    exp_chosen = jnp.where(chosen, jnp.exp(jnp.where(chosen, logits, 0.0)), 0.0)
    gates = exp_chosen / jnp.sum(exp_chosen, axis=0, keepdims=True)
    earlier = (iota((rows, rows), 0) < iota((rows, rows), 1)).astype(F32).astype(BF16)
    position = jnp.where(chosen, dot_nn(mask, earlier), -1.0)
    gate_high, gate_low = halves(gates)
    inverse = token_ref[1:2, :]
    inv_high = inverse.astype(BF16).astype(F32)
    inv_mid = (inverse - inv_high).astype(BF16).astype(F32)
    inv_low = inverse - inv_high - inv_mid
    slot_row = iota((8, rows), 0)
    token_part = jnp.where(
        slot_row == 0,
        token_ref[0:1, :],
        jnp.where(slot_row == 1, inv_high, jnp.where(slot_row == 2, inv_mid, jnp.where(slot_row == 3, inv_low, 0.0))),
    )
    extra = jnp.concatenate(
        [
            gate_high.astype(F32),
            gate_low.astype(F32),
            token_part,
            jnp.zeros((ROW_EXTRA - 2 * experts - 8, rows), F32),
        ],
        axis=0,
    ).astype(BF16)
    expert_row = iota((experts, rows), 0)
    slot = iota((capacity, rows), 0).astype(F32)
    picks = []
    for way in range(4):
        own = jnp.sum(jnp.where(expert_row == n[PEER_EXPERT + way], position, 0.0), axis=0, keepdims=True)
        picks.append((slot == own).astype(F32))
    picked = jnp.concatenate(picks, axis=0)
    place_ref[0] = jnp.transpose(picked).astype(BF16)
    picked = picked.astype(BF16)
    sent = dot_nn(picked, normed)
    sent_extra = contract_last(picked, extra)
    for way in range(4):
        at = slice(way * capacity, (way + 1) * capacity)
        row_refs[way][:, :width] = sent[at].astype(BF16)
        row_refs[way][:, width:] = sent_extra[at].astype(BF16)


def expert_kernel(n, r0, r1, r2, r3, gate_ref, up_ref, *refs):
    pooled_ref, hidden_ref, a_ref, b_ref, info_ref, x_ref, weight_ref = refs[-7:]
    width = gate_ref.shape[0]
    experts = 16

    @pl.when(pl.program_id(0) == 0)
    def start():
        x_ref[...] = jnp.concatenate([r[:, :width].astype(F32) for r in (r0, r1, r2, r3)], axis=0).astype(BF16)
        extra = jnp.concatenate([r[:, width:].astype(F32) for r in (r0, r1, r2, r3)], axis=0).astype(BF16)
        own = n[OWN_EXPERT]

        def mixer(source, goal):
            gates = (goal < experts) & ((source == goal) | (source == goal + experts))
            sequence = (goal == experts) & (source == 2 * experts)
            inverse = (goal == experts + 1) & (source > 2 * experts) & (source < 2 * experts + 4)
            gate = (goal == experts + 2) & ((source == own) | (source == own + experts))
            return (gates | sequence | inverse | gate).astype(F32).astype(BF16)

        square = (ROW_EXTRA, ROW_EXTRA)
        info = dot_nn(extra, mixer(iota(square, 0), iota(square, 1)))
        info_ref[0] = info
        turned = contract_last(mixer(iota(square, 1), iota(square, 0)), extra)
        sequence = turned[experts : experts + 1]
        weight = turned[experts + 1 : experts + 2] * turned[experts + 2 : experts + 3]
        pool = jnp.where(iota((pooled_ref.shape[0], extra.shape[0]), 0).astype(F32) == sequence, weight, 0.0)
        weight_ref[...] = stacked_halves(pool)

    x = x_ref[...]
    pre_gate = dot_nn(x, gate_ref[...])
    pre_up = dot_nn(x, up_ref[...])
    sigmoid = 1.0 / (1.0 + jnp.exp(-pre_gate))
    silu = pre_gate * sigmoid
    hidden = (silu * pre_up).astype(BF16)
    hidden_ref[0] = hidden
    a_ref[0] = pre_up * sigmoid * (1.0 + pre_gate * (1.0 - sigmoid))
    b_ref[0] = silu
    pooled_ref[...] = fold(dot_nn(weight_ref[...], hidden))


def sum_kernel(n, p0, p1, p2, p3, _, out_ref):
    near = p0[...].astype(F32) + p1[...].astype(F32)
    out_ref[...] = (near + (p2[...].astype(F32) + p3[...].astype(F32))).astype(BF16)


def embed_kernel(n, p0, p1, p2, p3, down_ref, t_ref, token_ref, _, o0, o1, o2, o3, part_ref):
    pooled = p0[...] + p1[...] + p2[...] + p3[...]
    part = fold(dot_nn(stacked_halves(pooled), down_ref[...]))
    sequences = part.shape[0]
    own = jnp.where(
        iota((sequences, t_ref.shape[1]), 0).astype(F32) == token_ref[0:1, :], token_ref[1:2, :], 0.0
    )
    part_ref[...] = part + fold(dot_nn(stacked_halves(own), t_ref[0]))
    rows = o0.shape[0]
    for way, out in enumerate((o0, o1, o2, o3)):
        out[...] = part_ref[pl.ds(pl.multiple_of(n[PEER + way] * rows, rows), rows), :].astype(out.dtype)


def contrast_kernel(n, q0, q1, q2, q3, down_ref, _, grad_ref, hidden_grad_ref, loss_ref, all_ref):
    rows = q0.shape[0]
    for way, part in enumerate((q0, q1, q2, q3)):
        all_ref[pl.ds(pl.multiple_of(n[PEER + way] * rows, rows), rows), :] = part[...].astype(F32)
    embedded = all_ref[...].astype(BF16)
    count = embedded.shape[0]
    pairs = count // 2
    products = contract_last(embedded, embedded)
    row, column = iota((count, count), 0), iota((count, count), 1)
    squares = jnp.where(row == column, products, 0.0)
    inverse = 1.0 / jnp.sqrt(jnp.sum(squares, axis=1, keepdims=True) + EPSILON)
    inverse_row = 1.0 / jnp.sqrt(jnp.sum(squares, axis=0, keepdims=True) + EPSILON)
    cosines = products * inverse * inverse_row
    scores = cosines / SOFTMAX_WARMTH
    is_pair = (row % 2 == 0) & (column % 2 == 1)
    matched = is_pair & (column == row + 1)
    exp_scores = jnp.where(is_pair, jnp.exp(jnp.where(is_pair, scores, 0.0)), 0.0)
    row_total = jnp.sum(exp_scores, axis=1, keepdims=True)
    is_query = iota((count, 1), 0) % 2 == 0
    row_total = jnp.where(is_query, row_total, 1.0)
    own_score = jnp.sum(jnp.where(matched, scores, 0.0), axis=1, keepdims=True)
    terms = jnp.where(is_query, jnp.log(row_total) - own_score, 0.0)
    loss_ref[0] = jnp.sum(terms) / pairs
    dscore = (exp_scores / row_total - jnp.where(matched, 1.0, 0.0)) * (LOSS_SCALE / pairs)
    both = dscore + jnp.transpose(dscore)
    both = both / SOFTMAX_WARMTH
    radial = jnp.sum(both * cosines, axis=1, keepdims=True)
    mixer = (both - jnp.where(row == column, radial, 0.0)) * inverse * inverse_row
    grad = fold(dot_nn(stacked_halves(mixer), embedded))
    grad_ref[...] = grad
    hidden_grad_ref[...] = fold(contract_last(stacked_halves(grad), down_ref[...]))


def backward_kernel(capacity, n, a_ref, b_ref, hidden_ref, info_ref, dh_ref, gate_ref, up_ref, router_ref, _, o0, o1, o2, o3, dgate_ref, dup_ref, dlog_ref):
    experts = 16

    @pl.when(pl.program_id(0) == 0)
    def start():
        info = info_ref[0]
        slots = info.shape[0]
        sequence = info[:, experts : experts + 1]
        weight = info[:, experts + 1 : experts + 2] * info[:, experts + 2 : experts + 3]
        member = (iota((slots, dh_ref.shape[0]), 1).astype(F32) == sequence).astype(F32).astype(BF16)
        high, low = halves(dh_ref[...])
        dhidden = weight * (dot_nn(member, high) + dot_nn(member, low))
        dgate_ref[...] = (dhidden * a_ref[0]).astype(BF16)
        dup_ref[...] = (dhidden * b_ref[0]).astype(BF16)
        moved = jnp.sum(dhidden * hidden_ref[0].astype(F32), axis=1, keepdims=True)
        lane = iota((slots, ROW_EXTRA), 1)
        gates = jnp.where(lane < experts, info, 0.0)
        dlog_ref[...] = (moved * (jnp.where(lane == n[OWN_EXPERT], 1.0, 0.0) - gates)).astype(BF16)

    total = (
        dot_nn(dgate_ref[...], gate_ref[...])
        + dot_nn(dup_ref[...], up_ref[...])
        + dot_nn(dlog_ref[...], router_ref[...])
    )
    for way, out in enumerate((o0, o1, o2, o3)):
        out[...] = total[way * capacity : (way + 1) * capacity].astype(BF16)


def turn_kernel(n, weight_ref, _, out_ref):
    out_ref[...] = jnp.transpose(weight_ref[...])


def combine_kernel(n, place_ref, r0, r1, r2, r3, _, out_ref, narrow_ref):
    rows = jnp.concatenate([r[...].astype(F32) for r in (r0, r1, r2, r3)], axis=0).astype(BF16)
    total = dot_nn(place_ref[0], rows)
    out_ref[...] = total
    narrow_ref[...] = total.astype(BF16)


def spread_kernel(n, t_ref, grad_ref, token_ref, _, out_ref, scale_ref):
    x = t_ref[0].astype(F32)
    scale = lax.rsqrt(jnp.mean(x * x, axis=1, keepdims=True) + EPSILON)
    spread = jnp.where(iota((grad_ref.shape[0], x.shape[0]), 0).astype(F32) == token_ref[0:1, :], 1.0, 0.0)
    spread = jnp.transpose(spread).astype(BF16)
    inverse = jnp.transpose(token_ref[...])[:, 1:2]
    high, low = halves(grad_ref[...])
    out_ref[...] = inverse * (dot_nn(spread, high) + dot_nn(spread, low))
    scale_ref[...] = jnp.broadcast_to(scale, scale_ref.shape)


def finish_kernel(n, t_ref, gain_ref, dresid_ref, scale_ref, own_ref, r4, r5, r6, _, out_ref):
    x = t_ref[0].astype(F32)
    scale = scale_ref[:, :1]
    dnormed = own_ref[...] + r4[...].astype(F32) + r5[...].astype(F32) + r6[...].astype(F32)
    gained = dnormed * gain_ref[...]
    pull = (scale * scale * scale) * jnp.mean(gained * x, axis=1, keepdims=True)
    out_ref[...] = (dresid_ref[...] + scale * gained - x * pull).astype(BF16)


class Chain:
    def __init__(self, numbers, first):
        self.numbers = numbers
        self.last = first

    def __call__(self, kernel, ins, outs, *, steps=1, kept=(), scratch=(), flops=0):
        args, in_specs = zip(*ins)
        args, in_specs = list(args), list(in_specs)
        shapes, out_specs = zip(*outs)
        aliases = {}
        for at, array in kept:
            aliases[1 + len(args)] = at
            args.append(array)
            in_specs.append(pl.BlockSpec(memory_space=pl.ANY))
        args.append(self.last)
        in_specs.append(pl.BlockSpec(memory_space=pl.ANY))
        result = pl.pallas_call(
            kernel,
            out_shape=list(shapes),
            grid_spec=pltpu.PrefetchScalarGridSpec(
                num_scalar_prefetch=1,
                grid=(steps,),
                in_specs=in_specs,
                out_specs=list(out_specs),
                scratch_shapes=scratch,
            ),
            input_output_aliases=aliases,
            compiler_params=pltpu.CompilerParams(vmem_limit_bytes=VMEM_LIMIT),
            cost_estimate=pl.CostEstimate(flops=1, bytes_accessed=1, transcendentals=0),
        )(self.numbers, *args)
        self.last = result[0]
        return result


def fixed(shape):
    return pl.BlockSpec(shape, lambda j, n: (0,) * len(shape))


def whole(array):
    return array, pl.BlockSpec(memory_space=pltpu.VMEM)


def fast_body(context, o_weight, resid, norm_gain, router, gate_weight, up_weight, down_weight, expert_ids, lengths):
    e = lax.axis_index("expert")
    z = lax.axis_index("tensor")
    rows, width = resid.shape
    heads = context.shape[1]
    experts = router.shape[1]
    top = expert_ids.shape[1]
    seq_count = lengths.shape[1]
    sequences = 4 * seq_count
    hidden_width = gate_weight.shape[2]
    capacity = max(2, rows * top * 5 // (4 * experts))
    slots = 4 * capacity
    leaf = (z == 0) | (z == 3)
    ways = e ^ jnp.arange(4, dtype=jnp.int32)
    numbers = jnp.concatenate(
        [
            jnp.stack([e * 4 + z, leaf.astype(jnp.int32), z]),
            ways,
            ways * 4 + z,
            jnp.asarray(BLOCK_ORDER, jnp.int32)[z],
        ]
    ).astype(jnp.int32)
    gate_w, up_w, down_w = gate_weight[0], up_weight[0], down_weight[0]
    gain = norm_gain.reshape(1, width)
    router_turned = router.T
    router_rows = jnp.pad(router_turned, ((0, ROW_EXTRA - experts), (0, 0)))

    def along_z(value, pairs):
        return lax.ppermute(value, "tensor", pairs)

    def swap_z(value, bits):
        return lax.ppermute(value, "tensor", [(i, i ^ bits) for i in range(4)])

    def swap_e(value, bits):
        return lax.ppermute(value, "expert", [(i, i ^ bits) for i in range(4)])

    seq_lengths = lengths[0]
    seq_ends = jnp.cumsum(seq_lengths)
    places = jnp.arange(4 * rows, dtype=jnp.int32)
    after = places[None, :] >= seq_ends[:, None]
    seq_local = jnp.sum(after.astype(jnp.int32), axis=0)
    token_len = jnp.sum(
        jnp.where(seq_local[None, :] == jnp.arange(seq_count, dtype=jnp.int32)[:, None], seq_lengths[:, None], 0), axis=0
    )
    token_info = jnp.concatenate(
        [
            (seq_local + e * seq_count).astype(F32)[None],
            (1.0 / token_len.astype(F32))[None],
            jnp.zeros((6, 4 * rows), F32),
        ],
        axis=0,
    )

    chain = Chain(numbers, gain)
    shape = jax.ShapeDtypeStruct
    tile = 512
    pieces = []
    for c, cuts in enumerate(PIECES):
        pieces += [(c, i * (rows // cuts), rows // cuts) for i in range(cuts)]
    count = len(pieces)
    parts, half, inner, back, from_leaf, from_inner = ([None] * count for _ in range(6))
    received, pools, shared, kept_rows, kept_acts = [None] * 4, [None] * 4, {}, {}, {}

    def first_hop(i):
        c, offset, size = pieces[i]
        if i == 0:
            away = pl.BlockSpec(memory_space=pl.ANY)
            near = pl.BlockSpec(memory_space=pltpu.VMEM)
            chain.last = parts[0] = pl.pallas_call(
                functools.partial(first_kernel, experts),
                out_shape=shape((size + experts, width), BF16),
                in_specs=[near, away, away, away],
                out_specs=near,
                scratch_shapes=[
                    pltpu.VMEM((size, heads), BF16),
                    pltpu.VMEM((heads, width), BF16),
                    pltpu.VMEM((size, width), BF16),
                    pltpu.SemaphoreType.DMA((FIRST_CUTS + 2,)),
                ],
                compiler_params=pltpu.CompilerParams(vmem_limit_bytes=FIRST_LIMIT),
            )(expert_ids.T, context, o_weight, resid)
            from_leaf[0] = along_z(parts[0], LEAVES_IN)
            return
        at = (c * rows + offset) // size
        ins = [
            (context, pl.BlockSpec((size, heads), lambda j, n: (at, 0))),
            whole(o_weight),
            whole(resid),
        ]
        (parts[i],) = chain(
            functools.partial(project_kernel, c, offset),
            ins,
            [(shape((size, width), BF16), fixed((size, width)))],
            flops=2 * size * heads * width,
        )
        from_leaf[i] = along_z(parts[i], LEAVES_IN)

    def add(left, right):
        like = shape(right.shape, BF16)
        return chain(add_kernel, [whole(left), whole(right)], [(like, fixed(like.shape))], flops=left.size)[0]

    def second_hop(i):
        half[i] = add(parts[i], from_leaf[i])
        from_inner[i] = along_z(half[i], INNER_SWAP)

    def third_hop(i):
        inner[i] = add(half[i], from_inner[i])
        back[i] = along_z(inner[i], LEAVES_OUT)

    def dispatch(c):
        mine = [i for i in range(count) if pieces[i][0] == c]
        ins = [whole(inner[i]) for i in mine] + [whole(back[i]) for i in mine]
        ins += [
            whole(gain),
            whole(router_turned),
            (token_info, pl.BlockSpec((8, rows), lambda j, n: (0, c))),
        ]
        if c > 0:
            ins.append(whole(shared["mask"]))
        sent_shape = (capacity, width + ROW_EXTRA)
        outs = [(shape(sent_shape, BF16), fixed(sent_shape))] * 4
        for size in ((rows, width), (rows, slots)):
            outs.append((shape((4,) + size, BF16), pl.BlockSpec((1,) + size, lambda j, n: (c, 0, 0))))
        if c == 0:
            outs.append((shape((experts, 4 * rows), BF16), fixed((experts, 4 * rows))))
        result = chain(
            functools.partial(dispatch_kernel, capacity, c, len(mine)),
            ins,
            outs,
            kept=sorted(kept_rows.items()),
            flops=2 * slots * rows * width,
        )
        kept_rows.update({4: result[4], 5: result[5]})
        if c == 0:
            shared["mask"] = result[6]
        received[c] = [result[0]] + [swap_e(result[way], way) for way in (1, 2, 3)]

    def expert(c):
        tile = hidden_width
        block = lambda size: pl.BlockSpec((1, slots, size), lambda j, n: (c, 0, j))
        outs = [(shape((sequences, hidden_width), F32), pl.BlockSpec((sequences, tile), lambda j, n: (0, j)))]
        outs += [(shape((4, slots, hidden_width), kind), block(tile)) for kind in (BF16, F32, F32)]
        outs.append((shape((4, slots, ROW_EXTRA), F32), pl.BlockSpec((1, slots, ROW_EXTRA), lambda j, n: (c, 0, 0))))
        weight_spec = pl.BlockSpec(memory_space=pltpu.VMEM)
        result = chain(
            expert_kernel,
            [whole(r) for r in received[c]] + [(gate_w, weight_spec), (up_w, weight_spec)],
            outs,
            steps=hidden_width // tile,
            kept=sorted(kept_acts.items()),
            scratch=[pltpu.VMEM((slots, width), BF16), pltpu.VMEM((2 * sequences, slots), BF16)],
            flops=4 * slots * width * hidden_width,
        )
        pools[c] = result[0]
        kept_acts.update({i: result[i] for i in (1, 2, 3, 4)})

    turned = [None, None]

    def turn(k):
        size = (hidden_width, width)
        (turned[k],) = chain(turn_kernel, [whole((gate_w, up_w)[k])], [(shape(size, BF16), fixed(size))])

    calls = {"p": first_hop, "s": second_hop, "t": third_hop, "d": dispatch, "x": expert}
    for step in FORWARD_ORDER:
        calls[step[0]](int(step[1:]))

    total_all, place_all = kept_rows[4], kept_rows[5]
    hidden_all, a_all, b_all, info_all = (kept_acts[i] for i in (1, 2, 3, 4))
    own_rows = (total_all, pl.BlockSpec((1, rows, width), lambda j, n: (n[Z], 0, 0)))
    own_tokens = (token_info, pl.BlockSpec((8, rows), lambda j, n: (0, n[Z])))
    seq_size = (seq_count, width)
    quarters = chain(
        embed_kernel,
        [whole(pool) for pool in pools] + [whole(down_w), own_rows, own_tokens],
        [(shape(seq_size, kind), fixed(seq_size)) for kind in (F32, BF16, BF16, BF16)],
        scratch=[pltpu.VMEM((sequences, width), F32)],
        flops=4 * sequences * hidden_width * width,
    )

    def add_four(values):
        return chain(sum_kernel, [whole(v) for v in values], [(shape(seq_size, BF16), fixed(seq_size))])[0]

    parts_e = [quarters[0]] + [swap_e(quarters[way], way) for way in (1, 2, 3)]
    turn(0)
    mine = add_four(parts_e)
    parts_z = [mine] + [swap_z(mine, way) for way in (1, 2, 3)]
    turn(1)
    mine = add_four(parts_z)
    gathered = [mine] + [swap_e(mine, way) for way in (1, 2, 3)]
    sizes = ((sequences, width), (sequences, hidden_width))
    dembedded, hidden_grad, loss = chain(
        contrast_kernel,
        [whole(piece) for piece in gathered] + [whole(down_w)],
        [(shape(size, F32), fixed(size)) for size in sizes]
        + [(shape((1,), F32), pl.BlockSpec(memory_space=pltpu.SMEM))],
        scratch=[pltpu.VMEM((sequences, width), F32)],
        flops=4 * sequences * hidden_width * width,
    )
    returned, sums = [None] * 4, [None] * 4

    def backward(k):
        tile = width
        block = lambda size: pl.BlockSpec((1, slots, size), lambda j, n: (n[ORDER + k], 0, 0))
        grads = chain(
            functools.partial(backward_kernel, capacity),
            [
                (a_all, block(hidden_width)),
                (b_all, block(hidden_width)),
                (hidden_all, block(hidden_width)),
                (info_all, block(ROW_EXTRA)),
                whole(hidden_grad),
                whole(turned[0]),
                whole(turned[1]),
                (router_rows, pl.BlockSpec((ROW_EXTRA, tile), lambda j, n: (0, j))),
            ],
            [(shape((capacity, width), BF16), pl.BlockSpec((capacity, tile), lambda j, n: (0, j)))] * 4,
            steps=width // tile,
            scratch=[
                pltpu.VMEM((slots, hidden_width), BF16),
                pltpu.VMEM((slots, hidden_width), BF16),
                pltpu.VMEM((slots, ROW_EXTRA), BF16),
            ],
            flops=4 * slots * width * hidden_width,
        )
        returned[k] = [grads[0]] + [swap_e(grads[way], way) for way in (1, 2, 3)]

    def combine(k):
        sums[k] = chain(
            combine_kernel,
            [(place_all, pl.BlockSpec((1, rows, slots), lambda j, n: (n[ORDER + k], 0, 0)))]
            + [whole(r) for r in returned[k]],
            [(shape((rows, width), kind), fixed((rows, width))) for kind in (F32, BF16)],
            flops=2 * slots * rows * width,
        )

    hops = {}

    def combined(k):
        combine(k)
        if k < 3:
            hops[k] = along_z(sums[k][1], LEAVES_IN)

    def inner_hop(k):
        total = add(sums[(0, 2)[k]][0], hops[(0, 1)[k]])
        hops[3 + k] = along_z(total, INNER_SWAP)

    def last_hop(_):
        hops[5] = along_z(add(sums[1][0], hops[3]), LEAVES_OUT)

    calls = {"b": backward, "c": combined, "i": inner_hop, "l": last_hop}
    for step in BACKWARD_ORDER:
        calls[step[0]](int(step[1:]))
    dresid, scales = chain(
        spread_kernel,
        [own_rows, whole(dembedded), own_tokens],
        [(shape((rows, width), F32), fixed((rows, width))), (shape((rows, 128), F32), fixed((rows, 128)))],
    )
    (grad,) = chain(
        finish_kernel,
        [own_rows, whole(gain), whole(dresid), whole(scales)]
        + [whole(value) for value in (sums[3][0], hops[2], hops[4], hops[5])],
        [(shape((rows, width), BF16), fixed((rows, width)))],
        flops=4 * rows * sequences * width,
    )
    return loss, grad


def solution(mesh):
    shape = dict(mesh.shape)
    part_body = fast_body if (shape["expert"], shape["tensor"]) == (4, 4) else body
    in_specs = (
        P(("groups", "expert"), "tensor"),
        P("tensor", None),
        P(("groups", "expert", "tensor"), None),
        P(),
        P(),
        P(("expert", "tensor"), None, None),
        P(("expert", "tensor"), None, None),
        P(("expert", "tensor"), None, None),
        P(("groups", "expert", "tensor"), None),
        P(("groups", "expert"), None),
    )
    out_specs = (P("groups"), P(("groups", "expert", "tensor"), None))
    return jax.shard_map(part_body, mesh=mesh, in_specs=in_specs, out_specs=out_specs, check_vma=False)
```
